256 devices in a mesh: gossip: 4 (over x_lo, core), fsdp: 64 (over z, x_hi, y).
Axes of the slice: x: 4 (x_hi: 2, x_lo: 2; x = x_hi * 2 + x_lo), y: 4, z: 8, core: 2. Of those that a mesh axis runs over, the one named last changes fastest.
Arguments:
- tokens: bfloat16 [4, 1280, 5120], P('gossip', 'fsdp'), may hold values from -6 to 6
- cotangent: bfloat16 [4, 1280, 5120], P('gossip', 'fsdp'), may hold values from -6 to 6
- gate_num: float32 [4, 7168, 5120], P('gossip', 'fsdp'), may hold values from -6 to 6
- push_weight: float32 [4], P('gossip'), may hold values from 0.5 to 2
- stale_num: float32 [4, 7168, 5120], P('gossip', 'fsdp'), may hold values from -3 to 3
- stale_weight: float32 [4], P('gossip'), may hold values from 0.25 to 1
- up_weight: bfloat16 [7168, 5120], P('fsdp'), may hold values from -0.078125 to 0.078125
- down_weight: bfloat16 [7168, 5120], P('fsdp')
- step: int32 [1], replicated, may hold values from 0 to 999999
Outputs:
- new_num: float32 [4, 7168, 5120], P('gossip', 'fsdp')
- new_weight: float32 [4], P('gossip')
- next_num: float32 [4, 7168, 5120], P('gossip', 'fsdp')
- next_weight: float32 [4], P('gossip')
The draws below stay inside these ranges and needn't reach their ends.
All inputs are finite; a program needn't handle non-finite values.
Results may differ from the reference program's by a relative error of at most 0.0003.
Values may be sent and summed in bfloat16 or wider, within the bound.
No kernel may reach another device: no remote copies, remote signals or barrier semaphores. Data moves between devices by JAX's collectives and lax.ppermute only.
A program may use at most 192 MiB of HBM per device.

```python
import math
import jax
import jax.numpy as jnp

D = 5120
FFW = 7168
TOKENS = 1280
GROUPS = 4


def draw_down_weight(key, part):
    key = jax.random.fold_in(key, 7)
    base_key, spread_key = jax.random.split(key)
    position = jnp.arange(FFW, dtype=jnp.float32) / FFW
    spread = jnp.exp(jax.random.uniform(spread_key, (FFW, 1), jnp.float32) * math.log(10.0))
    row_scale = jnp.exp(position * math.log(3.0))[:, None] * spread
    base = jax.random.normal(base_key, (FFW, D), jnp.float32)
    return (base * row_scale / (7.0 * math.sqrt(FFW))).astype(jnp.bfloat16)


def level_of(own_key, shape, cuts, smallest, high):
    factor_of = 1.0
    for axis_at, shards_of in cuts:
        heights = jax.random.uniform(jax.random.fold_in(jax.random.fold_in(own_key, 6), axis_at), (shards_of,), jnp.float32, smallest / len(cuts), high / len(cuts))
        factor_of = factor_of * jnp.repeat(jnp.exp(heights), shape[axis_at] // shards_of).reshape((-1,) + (1,) * (len(shape) - 1 - axis_at))
    return factor_of


def centred(rng, dims, scale, limit, cuts=(), kind=jnp.bfloat16):
    entries = scale * jax.random.normal(rng, dims, jnp.float32)
    if cuts:
        entries = entries * level_of(rng, dims, cuts, -0.22, 0.18)
    return jnp.clip(entries, -limit, limit).astype(kind)


def setup_inputs(seed: int = 0) -> dict:
    splits = jax.random.split(jax.random.key(seed), 10)
    return {
        "tokens": centred(splits[0], (GROUPS, TOKENS, D), 1.0, 6.0, ((0, 4), (1, 64))),
        "cotangent": centred(splits[1], (GROUPS, TOKENS, D), 1.0, 6.0, ((0, 4), (1, 64))),
        "gate_num": centred(splits[2], (GROUPS, FFW, D), 1.0, 6.0, ((0, 4), (1, 64)), jnp.float32),
        "push_weight": jnp.clip(jnp.exp(math.log(2.0) - 1.3862944 * jax.random.uniform(splits[3], (GROUPS,), jnp.float32) ** level_of(splits[3], (GROUPS,), ((0, 4),), -0.2, 0.2)), 0.5, 2.0),
        "stale_num": centred(splits[4], (GROUPS, FFW, D), 0.5, 3.0, ((0, 4), (1, 64)), jnp.float32),
        "stale_weight": jnp.clip(jnp.exp(math.log(1.0) - 1.3862944 * jax.random.uniform(splits[5], (GROUPS,), jnp.float32) ** level_of(splits[5], (GROUPS,), ((0, 4),), -0.2, 0.2)), 0.25, 1.0),
        "up_weight": centred(splits[6], (FFW, D), D ** -0.5, 0.078125, ((0, 64),)),
        "down_weight": draw_down_weight(jax.random.fold_in(splits[9], 71), 0),
        "step": jax.random.randint(splits[8], (1,), 0, 1000000).astype(jnp.int32),
    }


eps = 1e-06

def silu_slope(preact):
    sigmoid_val = jax.nn.sigmoid(preact)
    return sigmoid_val * (1.0 + preact * (1.0 - sigmoid_val))

def plan_rate(step):
    phase = (step[0] % 1000).astype(jnp.float32) / 1000.0
    return 0.4 + 1.8 * (1.0 + jnp.cos(math.pi * phase))

def group_half(rows_in, rows_grad, numerator, weight, up_weight, down_weight, rate):
    width_scale = D ** (-0.5)
    max_norm = 0.05 * math.sqrt(D * FFW)
    params = (numerator / weight).astype(jnp.bfloat16)
    preact = jnp.dot(rows_in, params.T, preferred_element_type=jnp.float32) * width_scale
    up_proj = jnp.dot(rows_in, up_weight.T, preferred_element_type=jnp.float32)
    hidden_grad = jnp.dot(rows_grad, down_weight.T, preferred_element_type=jnp.float32)
    pre_grad = (hidden_grad * up_proj * silu_slope(preact)).astype(jnp.bfloat16)
    gate_grad = jnp.dot(pre_grad.T, rows_in, preferred_element_type=jnp.float32) * width_scale
    norm_sq = jnp.sum(gate_grad * gate_grad)
    clip_factor = jnp.minimum(1.0, max_norm / jnp.sqrt(norm_sq + eps))
    return 0.5 * (numerator - rate * clip_factor * gate_grad)

def reference(tokens, cotangent, gate_num, push_weight, stale_num, stale_weight, up_weight, down_weight, step):
    rate = plan_rate(step)
    halves = []
    for group in range(GROUPS):
        halves.append(group_half(tokens[group], cotangent[group], gate_num[group], push_weight[group], up_weight, down_weight, rate))
    next_num = jnp.stack(halves, axis=0)
    next_weight = 0.5 * push_weight
    distances = GROUPS.bit_length() - 1
    distance = jnp.left_shift(jnp.int32(1), (step[0] % distances).astype(jnp.int32))
    new_num = next_num + jnp.roll(stale_num, distance, axis=0)
    new_weight = next_weight + jnp.roll(stale_weight, distance, axis=0)
    return (new_num, new_weight, next_num, next_weight)
```

```python
import math

import jax
import jax.numpy as jnp
import numpy as np
from jax import lax
from jax.sharding import Mesh, PartitionSpec as P

D = 5120
FFW = 7168

eps = 1e-06

SIZES = {"x_lo": 2, "core": 2, "z": 8, "x_hi": 2, "y": 4}
GOSSIP = ("x_lo", "core")
FSDP = ("z", "x_hi", "y")


def shifted(value, axis, steps):
    count = SIZES[axis]
    pairs = [((place + steps) % count, place) for place in range(count)]
    return lax.ppermute(value, axis, pairs)


def transposed(value):
    pairs = [(2 * x_hi + core, 2 * core + x_hi) for x_hi in range(2) for core in range(2)]
    return lax.ppermute(value, ("core", "x_hi"), pairs)


def silu_slope(preact):
    sigmoid_val = jax.nn.sigmoid(preact)
    return sigmoid_val * (1.0 + preact * (1.0 - sigmoid_val))


def plan_rate(step):
    phase = (step[0] % 1000).astype(jnp.float32) / 1000.0
    return 0.4 + 1.8 * (1.0 + jnp.cos(math.pi * phase))


def deliver(stale, step):
    two_before = shifted(stale, "x_lo", 1)
    payload = jnp.where(lax.axis_index("core") == 1, two_before, stale)
    one_before = shifted(payload, "core", 1)
    return jnp.where(step[0] % 2 == 0, one_before, two_before)


def dot_t(rows, weights):
    return lax.dot_general(
        rows, weights, (((1,), (1,)), ((), ())), preferred_element_type=jnp.float32
    )


def gather_tokens(block):
    near = [block] + [shifted(block, "y", d) for d in (1, 3, 2)]
    return lax.all_gather(jnp.concatenate(near, axis=0), "z", axis=0, tiled=True)


def hidden_of(block, down):
    up_way, down_way = [block], [block]
    for _ in range(4):
        up_way.append(shifted(up_way[-1], "z", 1))
    for _ in range(3):
        down_way.append(shifted(down_way[-1], "z", 7))
    column = jnp.concatenate(up_way + down_way[:0:-1], axis=0)
    after = shifted(column, "y", 1)
    before = shifted(column, "y", 3)
    half = column.shape[0] // 2
    far = [shifted(after[:half], "y", 1), shifted(before[half:], "y", 3)]
    hidden = jnp.concatenate([dot_t(part, down) for part in (column, after, before, *far)], axis=0)
    width = hidden.shape[1]
    hidden = hidden.reshape(4, 8, -1, width).transpose(1, 0, 2, 3).reshape(-1, width)
    start = (8 - lax.axis_index("z")) % 8 * (hidden.shape[0] // 8)
    return lax.dynamic_slice_in_dim(
        jnp.concatenate([hidden, hidden], axis=0), start, hidden.shape[0], axis=0
    )


def shards(
    tokens, cotangent, gate_num, push_weight, stale_num, stale_weight, up_weight, down_weight, step
):
    width_scale = D ** (-0.5)
    max_norm = 0.05 * math.sqrt(D * FFW)
    rate = plan_rate(step)
    numerator = gate_num[0]

    rows_in, rows_grad = transposed(tokens[0]), transposed(cotangent[0])
    params = transposed((numerator / push_weight[0]).astype(jnp.bfloat16))
    up, down = transposed(up_weight), transposed(down_weight)
    params, up, down = (
        jnp.concatenate([value, shifted(value, "core", 1)], axis=0) for value in (params, up, down)
    )
    hidden_grad = hidden_of(rows_grad, down)
    rows_in = gather_tokens(rows_in)
    preact = dot_t(rows_in, params) * width_scale
    up_proj = dot_t(rows_in, up)
    pre_grad = (hidden_grad * up_proj * silu_slope(preact)).astype(jnp.bfloat16)
    partial = (
        lax.dot_general(
            pre_grad, rows_in, (((0,), (0,)), ((), ())), preferred_element_type=jnp.float32
        )
        * width_scale
    )
    half = partial.shape[0] // 2
    gate_grad = partial[:half] + shifted(partial[half:], "core", 1)
    norm_sq = jnp.sum(gate_grad * gate_grad)
    for axes in ("z", "y", "core"):
        norm_sq = lax.psum(norm_sq, axes)
    gate_grad, norm_sq = transposed(gate_grad), transposed(norm_sq)

    clip_factor = jnp.minimum(1.0, max_norm / jnp.sqrt(norm_sq + eps))
    kept_half = (0.5 * (numerator - rate * clip_factor * gate_grad))[None]
    kept_weight = 0.5 * push_weight
    new_num = kept_half + deliver(stale_num, step)
    new_weight = kept_weight + deliver(stale_weight, step)
    return (new_num, new_weight, kept_half, kept_weight)


def solution(mesh):
    named = Mesh(np.asarray(mesh.devices).reshape(tuple(SIZES.values())), tuple(SIZES))
    groups = P(GOSSIP, FSDP, None)
    in_specs = (
        groups,
        groups,
        groups,
        P(GOSSIP),
        groups,
        P(GOSSIP),
        P(FSDP, None),
        P(FSDP, None),
        P(),
    )
    out_specs = (groups, P(GOSSIP), groups, P(GOSSIP))
    return jax.shard_map(shards, mesh=named, in_specs=in_specs, out_specs=out_specs, check_vma=False)
```

```python
import math

import jax
import jax.numpy as jnp
import numpy as np
from jax import lax
from jax.experimental import pallas as pl
from jax.experimental.pallas import tpu as pltpu
from jax.sharding import Mesh, PartitionSpec as P

D = 5120
FFW = 7168

eps = 1e-06

WIDTH_SCALE = D ** (-0.5)
MAX_NORM = 0.05 * math.sqrt(D * FFW)

SIZES = {"x_lo": 2, "core": 2, "z": 8, "x_hi": 2, "y": 4}
GOSSIP = ("x_lo", "core")
FSDP = ("z", "x_hi", "y")

ROWS = 112
HALF = 128
BLOCK = 512


def shifted(value, axis, steps):
    count = SIZES[axis]
    pairs = [((place + steps) % count, place) for place in range(count)]
    return lax.ppermute(value, axis, pairs)


def transposed(value, axis=None, steps=0):
    names = [name for name in SIZES if name in ("core", "x_hi", axis)]
    sizes = [SIZES[name] for name in names]
    pairs = []
    for place in np.ndindex(*sizes):
        here = dict(zip(names, place))
        there = dict(here, core=here["x_hi"], x_hi=here["core"])
        if axis is not None:
            there[axis] = (there[axis] + steps) % SIZES[axis]
        source = np.ravel_multi_index([there[name] for name in names], sizes)
        pairs.append((int(source), int(np.ravel_multi_index(place, sizes))))
    return lax.ppermute(value, tuple(names), pairs)


def after(ready, *values):
    zero = jnp.minimum(jnp.abs(ready[0, 0]), 0)
    return [value + zero.astype(value.dtype) for value in values]


def silu_slope(preact):
    sigmoid_val = jax.nn.sigmoid(preact)
    return sigmoid_val * (1.0 + preact * (1.0 - sigmoid_val))


def plan_rate(step):
    phase = (step[0] % 1000).astype(jnp.float32) / 1000.0
    return 0.4 + 1.8 * (1.0 + jnp.cos(math.pi * phase))


def deliver(stale, step):
    two_before = shifted(stale, "x_lo", 1)
    payload = jnp.where(lax.axis_index("core") == 1, two_before, stale)
    one_before = shifted(payload, "core", 1)
    return jnp.where(step[0] % 2 == 0, one_before, two_before)


def dot_t(rows, weights):
    return lax.dot_general(
        rows, weights, (((1,), (1,)), ((), ())), preferred_element_type=jnp.float32
    )


def both_cores(own):
    pad = jnp.zeros((HALF - ROWS, D), own.dtype)
    return jnp.concatenate([own, pad, shifted(own, "core", 1), pad], axis=0)


def stack_kernel(*refs):
    *blocks, out_ref = refs
    for at, block in enumerate(blocks):
        count = block.shape[0]
        out_ref[at * count : (at + 1) * count, :] = block[...]


def stacked(blocks):
    count = blocks[0].shape[0]
    wide = D // 4
    return pl.pallas_call(
        stack_kernel,
        grid=(4,),
        in_specs=[pl.BlockSpec((count, wide), lambda at: (0, at))] * len(blocks),
        out_specs=pl.BlockSpec((count * len(blocks), wide), lambda at: (0, at)),
        out_shape=jax.ShapeDtypeStruct((count * len(blocks), D), blocks[0].dtype),
        compiler_params=pltpu.CompilerParams(vmem_limit_bytes=32 * 2**20),
        name="stacked",
    )(*blocks)


def column_of(block):
    own, *ways = [transposed(block, "z", steps) for steps in (0, 1, 7)]
    up_way, down_way = [ways[0]], [ways[1]]
    for _ in range(3):
        up_way.append(shifted(up_way[-1], "z", 1))
    for _ in range(2):
        down_way.append(shifted(down_way[-1], "z", 7))
    return own, stacked([own] + up_way + down_way[::-1])


def hidden_of(column, down):
    following = shifted(column, "y", 1)
    before = shifted(column, "y", 3)
    half = column.shape[0] // 2
    far = [shifted(following[:half], "y", 1), shifted(before[half:], "y", 3)]
    hidden = jnp.concatenate(
        [dot_t(part, down) for part in (column, following, before, *far)], axis=0
    )
    width = hidden.shape[1]
    hidden = hidden.reshape(4, 8, -1, width).transpose(1, 0, 2, 3).reshape(-1, width)
    start = (8 - lax.axis_index("z")) % 8 * (hidden.shape[0] // 8)
    return lax.dynamic_slice_in_dim(
        jnp.concatenate([hidden, hidden], axis=0), start, hidden.shape[0], axis=0
    )


def other_kernel(x_ref, params_ref, up_ref, hidden_ref, own_ref, grad_ref, preact, up_proj, other):
    at = pl.program_id(0)
    blocks = D // BLOCK

    @pl.when(at == 0)
    def _():
        preact[...] = jnp.zeros_like(preact)
        up_proj[...] = jnp.zeros_like(up_proj)

    @pl.when(at < blocks)
    def _():
        rows = x_ref[...]
        preact[...] += dot_t(rows, params_ref[...])
        up_proj[...] += dot_t(rows, up_ref[...])

    @pl.when(at == blocks - 1)
    def _():
        slope = silu_slope(preact[...] * WIDTH_SCALE)
        turned = (hidden_ref[...] * up_proj[...] * slope).T.astype(jnp.bfloat16)
        own_ref[...] = turned[:HALF]
        other[...] = turned[HALF:]

    @pl.when(at >= blocks)
    def _():
        grad = jnp.dot(other[...], x_ref[...], preferred_element_type=jnp.float32)
        grad_ref[...] = grad[:ROWS] * WIDTH_SCALE


def other_half(rows_in, params, up, hidden):
    count = rows_in.shape[0]
    blocks = D // BLOCK
    weights = pl.BlockSpec((2 * HALF, BLOCK), lambda at: (0, jnp.minimum(at, blocks - 1)))
    return pl.pallas_call(
        other_kernel,
        grid=(2 * blocks,),
        in_specs=[
            pl.BlockSpec((count, BLOCK), lambda at: (0, lax.rem(at, blocks))),
            weights,
            weights,
            pl.BlockSpec((count, 2 * HALF), lambda at: (0, 0)),
        ],
        out_specs=[
            pl.BlockSpec((HALF, count), lambda at: (0, 0)),
            pl.BlockSpec((ROWS, BLOCK), lambda at: (0, jnp.maximum(at - blocks, 0))),
        ],
        out_shape=[
            jax.ShapeDtypeStruct((HALF, count), jnp.bfloat16),
            jax.ShapeDtypeStruct((ROWS, D), jnp.float32),
        ],
        scratch_shapes=[
            pltpu.VMEM((count, 2 * HALF), jnp.float32),
            pltpu.VMEM((count, 2 * HALF), jnp.float32),
            pltpu.VMEM((HALF, count), jnp.bfloat16),
        ],
        compiler_params=pltpu.CompilerParams(vmem_limit_bytes=32 * 2**20),
        cost_estimate=pl.CostEstimate(
            flops=2 * count * D * 640, bytes_accessed=4 * count * D + 2**23, transcendentals=0
        ),
        name="other_half",
    )(rows_in, params, up, hidden)


def own_kernel(x_ref, own_ref, grad_ref):
    grad = jnp.dot(own_ref[...], x_ref[...], preferred_element_type=jnp.float32)
    grad_ref[...] = grad[:ROWS] * WIDTH_SCALE


def own_half(rows_in, own):
    count = rows_in.shape[0]
    return pl.pallas_call(
        own_kernel,
        grid=(D // BLOCK,),
        in_specs=[
            pl.BlockSpec((count, BLOCK), lambda at: (0, at)),
            pl.BlockSpec((HALF, count), lambda at: (0, 0)),
        ],
        out_specs=pl.BlockSpec((ROWS, BLOCK), lambda at: (0, at)),
        out_shape=jax.ShapeDtypeStruct((ROWS, D), jnp.float32),
        compiler_params=pltpu.CompilerParams(vmem_limit_bytes=32 * 2**20),
        cost_estimate=pl.CostEstimate(
            flops=2 * count * D * HALF, bytes_accessed=2 * count * D + 2**21, transcendentals=0
        ),
        name="own_half",
    )(rows_in, own)


def shards(
    tokens, cotangent, gate_num, push_weight, stale_num, stale_weight, up_weight, down_weight, step
):
    rate = plan_rate(step)
    numerator = gate_num[0]

    near = [transposed(tokens[0], "y", steps) for steps in (0, 1, 3, 2)]
    own, column = column_of(cotangent[0])
    rows_in = lax.all_gather(stacked(near), "z", axis=0, tiled=True)

    params, up, down, stale = after(
        own,
        (numerator / push_weight[0]).astype(jnp.bfloat16),
        up_weight,
        down_weight,
        jnp.concatenate([stale_num[0], jnp.broadcast_to(stale_weight, (8, D))], axis=0),
    )
    params, up, down = (both_cores(transposed(value)) for value in (params, up, down))
    hidden = hidden_of(column, down)
    received = deliver(stale, step)
    rows_in, received = lax.optimization_barrier((rows_in, received))

    own, other_grad = other_half(rows_in, params, up, hidden)
    gate_grad = own_half(rows_in, own) + shifted(other_grad, "core", 1)
    norm_sq = jnp.sum(gate_grad * gate_grad)
    gate_grad = transposed(gate_grad)
    for axes in ("z", "y", "core"):
        norm_sq = lax.psum(norm_sq, axes)
    norm_sq = transposed(norm_sq)

    clip_factor = jnp.minimum(1.0, MAX_NORM / jnp.sqrt(norm_sq + eps))
    kept_half = 0.5 * (numerator - rate * clip_factor * gate_grad)
    kept_weight = 0.5 * push_weight
    new_num = kept_half + received[:ROWS]
    new_weight = kept_weight + received[ROWS, :1]
    return (new_num[None], new_weight, kept_half[None], kept_weight)


def solution(mesh):
    named = Mesh(np.asarray(mesh.devices).reshape(tuple(SIZES.values())), tuple(SIZES))
    groups = P(GOSSIP, FSDP, None)
    in_specs = (
        groups,
        groups,
        groups,
        P(GOSSIP),
        groups,
        P(GOSSIP),
        P(FSDP, None),
        P(FSDP, None),
        P(),
    )
    out_specs = (groups, P(GOSSIP), groups, P(GOSSIP))
    return jax.shard_map(shards, mesh=named, in_specs=in_specs, out_specs=out_specs, check_vma=False)
```

```python
import math

import jax
import jax.numpy as jnp
import numpy as np
from jax import lax
from jax.experimental import pallas as pl
from jax.experimental.pallas import tpu as pltpu
from jax.sharding import Mesh, PartitionSpec as P

D = 5120
FFW = 7168

eps = 1e-06

WIDTH_SCALE = D ** (-0.5)
MAX_NORM = 0.05 * math.sqrt(D * FFW)

SIZES = {"x_lo": 2, "core": 2, "z": 8, "x_hi": 2, "y": 4}
GOSSIP = ("x_lo", "core")
FSDP = ("z", "x_hi", "y")

ROWS = 112
HALF = 128
BLOCK = 1024


def shifted(value, axis, steps):
    count = SIZES[axis]
    pairs = [((place + steps) % count, place) for place in range(count)]
    return lax.ppermute(value, axis, pairs)


def transposed(value):
    pairs = [(2 * x_hi + core, 2 * core + x_hi) for core in range(2) for x_hi in range(2)]
    return lax.ppermute(value, ("core", "x_hi"), pairs)


def held(value, *ready):
    return pl.pallas_call(
        lambda *refs: None,
        in_specs=[pl.BlockSpec(memory_space=pl.ANY)] * (1 + len(ready)),
        out_specs=pl.BlockSpec(memory_space=pl.ANY),
        out_shape=jax.ShapeDtypeStruct(value.shape, value.dtype),
        input_output_aliases={0: 0},
        compiler_params=params_of(1),
        name="held",
    )(value, *ready)


def silu_slope(preact):
    sigmoid_val = jax.nn.sigmoid(preact)
    return sigmoid_val * (1.0 + preact * (1.0 - sigmoid_val))


def plan_rate(step):
    phase = (step[0] % 1000).astype(jnp.float32) / 1000.0
    return 0.4 + 1.8 * (1.0 + jnp.cos(math.pi * phase))


def deliver(stale, step, *ready):
    two_before = held(shifted(stale, "x_lo", 1), *ready)
    payload = jnp.where(lax.axis_index("core") == 1, two_before, stale)
    one_before = shifted(payload, "core", 1)
    return jnp.where(step[0] % 2 == 0, one_before, two_before)


def dot_t(rows, weights):
    return lax.dot_general(
        rows, weights, (((1,), (1,)), ((), ())), preferred_element_type=jnp.float32
    )


def params_of(vmem, **more):
    return pltpu.CompilerParams(vmem_limit_bytes=vmem * 2**20, **more)


def stack_kernel(*refs):
    *blocks, out_ref = refs
    for at, block in enumerate(blocks):
        count = block.shape[0]
        out_ref[at * count : (at + 1) * count, :] = block[...]


def stacked(blocks):
    count = blocks[0].shape[0]
    wide = D // 4
    return pl.pallas_call(
        stack_kernel,
        grid=(4,),
        in_specs=[pl.BlockSpec((count, wide), lambda at: (0, at))] * len(blocks),
        out_specs=pl.BlockSpec((count * len(blocks), wide), lambda at: (0, at)),
        out_shape=jax.ShapeDtypeStruct((count * len(blocks), D), blocks[0].dtype),
        compiler_params=params_of(32),
        name="stacked",
    )(*blocks)


def gathered_z(block):
    by = {0: block}
    for steps in (1, 7, 2, 6):
        by[steps] = shifted(block, "z", steps)
    by[3] = shifted(by[2], "z", 1)
    by[5] = shifted(by[6], "z", 7)
    by[4] = shifted(by[2], "z", 2)
    return stacked([by[steps] for steps in range(8)])


def gathered_y(column):
    following = shifted(column, "y", 1)
    before = shifted(column, "y", 3)
    half = column.shape[0] // 2
    far = [shifted(following[:half], "y", 1), shifted(before[half:], "y", 3)]
    return [column, following, before, *far]


def widen(wide, mine, theirs):
    wide[:ROWS, :] = mine[...]
    wide[HALF : HALF + ROWS, :] = theirs[...]


def clear(wide):
    pad = jnp.zeros((HALF - ROWS, wide.shape[1]), wide.dtype)
    wide[ROWS:HALF, :] = pad
    wide[HALF + ROWS :, :] = pad


def hidden_kernel(z_ref, *refs):
    *parts, mine, theirs, out_ref, total, wide, tile = refs
    at = pl.program_id(0)

    @pl.when(at == 0)
    def _():
        total[...] = jnp.zeros_like(total)
        clear(wide)

    widen(wide, mine, theirs)
    row = 0
    for part in parts:
        count = part.shape[0]
        total[row : row + count, :] += dot_t(part[...], wide[...])
        row += count

    @pl.when(at == pl.num_programs(0) - 1)
    def _():
        column, block = row // 4, row // 32
        for dz in range(8):
            for dy in range(4):
                start = dy * column + dz * block
                tile[dy * block : (dy + 1) * block, :] = total[start : start + block, :]
            place = pl.multiple_of(lax.rem(z_ref[0] + dz, 8) * (4 * block), 16)
            out_ref[pl.ds(place, 4 * block), :] = tile[...]


def hidden_of(parts, mine, theirs):
    count = sum(part.shape[0] for part in parts)
    z = jnp.reshape(lax.axis_index("z"), (1,)).astype(jnp.int32)
    weights = pl.BlockSpec((ROWS, BLOCK), lambda at: (2, at))
    return pl.pallas_call(
        hidden_kernel,
        grid=(D // BLOCK,),
        in_specs=[pl.BlockSpec(memory_space=pltpu.SMEM)]
        + [pl.BlockSpec((part.shape[0], BLOCK), lambda at: (0, at)) for part in parts]
        + [weights, weights],
        out_specs=pl.BlockSpec((count, 2 * HALF), lambda at: (0, 0)),
        out_shape=jax.ShapeDtypeStruct((count, 2 * HALF), jnp.float32),
        scratch_shapes=[
            pltpu.VMEM((count, 2 * HALF), jnp.float32),
            pltpu.VMEM((2 * HALF, BLOCK), jnp.bfloat16),
            pltpu.VMEM((count // 8, 2 * HALF), jnp.float32),
        ],
        compiler_params=params_of(40),
        cost_estimate=pl.CostEstimate(
            flops=2 * count * D * 2 * HALF, bytes_accessed=2 * count * D + 2**22, transcendentals=0
        ),
        name="hidden",
    )(z, *parts, mine, theirs)


def other_kernel(
    x_ref, my_params, their_params, my_up, their_up, hidden_ref, own_ref, grad_ref,
    preact, up_proj, other, wide_params, wide_up,
):
    at = pl.program_id(0)
    blocks = D // BLOCK

    @pl.when(at == 0)
    def _():
        preact[...] = jnp.zeros_like(preact)
        up_proj[...] = jnp.zeros_like(up_proj)
        clear(wide_params)
        clear(wide_up)

    @pl.when(at < blocks)
    def _():
        widen(wide_params, my_params, their_params)
        widen(wide_up, my_up, their_up)
        preact[...] += dot_t(x_ref[...], wide_params[...])
        up_proj[...] += dot_t(x_ref[...], wide_up[...])

    @pl.when(at == blocks - 1)
    def _():
        slope = silu_slope(preact[...] * WIDTH_SCALE)
        turned = (hidden_ref[...] * up_proj[...] * slope).T.astype(jnp.bfloat16)
        own_ref[...] = turned[:HALF]
        other[...] = turned[HALF:]

    @pl.when(at >= blocks)
    def _():
        grad = jnp.dot(other[...], x_ref[...], preferred_element_type=jnp.float32)
        grad_ref[...] = grad[:ROWS] * WIDTH_SCALE


def other_half(rows_in, mine, theirs, hidden):
    count = rows_in.shape[0]
    blocks = D // BLOCK

    def weights(which):
        return pl.BlockSpec((ROWS, BLOCK), lambda at: (which, jnp.minimum(at, blocks - 1)))

    return pl.pallas_call(
        other_kernel,
        grid=(2 * blocks,),
        in_specs=[
            pl.BlockSpec((count, BLOCK), lambda at: (0, lax.rem(at, blocks))),
            weights(0),
            weights(0),
            weights(1),
            weights(1),
            pl.BlockSpec((count, 2 * HALF), lambda at: (0, 0)),
        ],
        out_specs=[
            pl.BlockSpec((HALF, count), lambda at: (0, 0)),
            pl.BlockSpec((ROWS, BLOCK), lambda at: (0, jnp.maximum(at - blocks, 0))),
        ],
        out_shape=[
            jax.ShapeDtypeStruct((HALF, count), jnp.bfloat16),
            jax.ShapeDtypeStruct((ROWS, D), jnp.float32),
        ],
        scratch_shapes=[
            pltpu.VMEM((count, 2 * HALF), jnp.float32),
            pltpu.VMEM((count, 2 * HALF), jnp.float32),
            pltpu.VMEM((HALF, count), jnp.bfloat16),
            pltpu.VMEM((2 * HALF, BLOCK), jnp.bfloat16),
            pltpu.VMEM((2 * HALF, BLOCK), jnp.bfloat16),
        ],
        compiler_params=params_of(40),
        cost_estimate=pl.CostEstimate(
            flops=2 * count * D * 640, bytes_accessed=4 * count * D + 2**23, transcendentals=0
        ),
        name="other_half",
    )(rows_in, mine, theirs, mine, theirs, hidden)


def own_kernel(x_ref, own_ref, grad_ref):
    grad = jnp.dot(own_ref[...], x_ref[...], preferred_element_type=jnp.float32)
    grad_ref[...] = grad[:ROWS] * WIDTH_SCALE


def own_half(rows_in, own):
    count = rows_in.shape[0]
    return pl.pallas_call(
        own_kernel,
        grid=(D // BLOCK,),
        in_specs=[
            pl.BlockSpec((count, BLOCK), lambda at: (0, at)),
            pl.BlockSpec((HALF, count), lambda at: (0, 0)),
        ],
        out_specs=pl.BlockSpec((ROWS, BLOCK), lambda at: (0, at)),
        out_shape=jax.ShapeDtypeStruct((ROWS, D), jnp.float32),
        compiler_params=params_of(40),
        cost_estimate=pl.CostEstimate(
            flops=2 * count * D * HALF, bytes_accessed=2 * count * D + 2**21, transcendentals=0
        ),
        name="own_half",
    )(rows_in, own)


def crossed(value):
    pairs = [
        (2 * (1 - x_hi) + core, 2 * core + x_hi) for core in range(2) for x_hi in range(2)
    ]
    return lax.ppermute(value, ("core", "x_hi"), pairs)


def shards(
    tokens, cotangent, gate_num, push_weight, stale_num, stale_weight, up_weight, down_weight, step
):
    rate = plan_rate(step)
    numerator = gate_num[0]

    rows_in, rows_grad = transposed(tokens[0]), transposed(cotangent[0])
    rows_in = held(rows_in, rows_grad)
    near = [rows_in] + [shifted(rows_in, "y", steps) for steps in (1, 3, 2)]
    near = stacked(near)
    column = gathered_z(rows_grad)
    parts = gathered_y(held(column, near))

    params = (numerator / push_weight[0]).astype(jnp.bfloat16)
    weights = jnp.concatenate([params, up_weight, down_weight], axis=0)
    mine = held(transposed(held(weights, rows_grad)), *parts[1:3])
    theirs = shifted(mine, "core", 1)
    stale = jnp.concatenate([stale_num[0], jnp.broadcast_to(stale_weight, (8, D))], axis=0)
    received = deliver(held(stale, rows_in), step, *parts)
    rows_in = lax.all_gather(near, "z", axis=0, tiled=True)
    hidden = hidden_of(parts, mine, theirs)
    rows_in, received = lax.optimization_barrier((rows_in, received))

    own, other_grad = other_half(rows_in, mine, theirs, hidden)
    gate_grad = own_half(rows_in, own) + shifted(other_grad, "core", 1)
    norm_sq = jnp.sum(gate_grad * gate_grad)
    gate_grad = transposed(gate_grad)
    for axes in ("z", "y"):
        norm_sq = lax.psum(norm_sq, axes)
    norm_sq = transposed(norm_sq) + crossed(norm_sq)

    clip_factor = jnp.minimum(1.0, MAX_NORM / jnp.sqrt(norm_sq + eps))
    kept_half = 0.5 * (numerator - rate * clip_factor * gate_grad)
    kept_weight = 0.5 * push_weight
    new_num = kept_half + received[:ROWS]
    new_weight = kept_weight + received[ROWS, :1]
    return (new_num[None], new_weight, kept_half[None], kept_weight)


def solution(mesh):
    named = Mesh(np.asarray(mesh.devices).reshape(tuple(SIZES.values())), tuple(SIZES))
    groups = P(GOSSIP, FSDP, None)
    in_specs = (
        groups,
        groups,
        groups,
        P(GOSSIP),
        groups,
        P(GOSSIP),
        P(FSDP, None),
        P(FSDP, None),
        P(),
    )
    out_specs = (groups, P(GOSSIP), groups, P(GOSSIP))
    return jax.shard_map(shards, mesh=named, in_specs=in_specs, out_specs=out_specs, check_vma=False)
```

```python
import math

import jax
import jax.numpy as jnp
import numpy as np
from jax import lax
from jax.experimental import pallas as pl
from jax.experimental.pallas import tpu as pltpu
from jax.sharding import Mesh, PartitionSpec as P

D = 5120
FFW = 7168

eps = 1e-06

WIDTH_SCALE = D ** (-0.5)
MAX_NORM = 0.05 * math.sqrt(D * FFW)

SIZES = {"x_lo": 2, "core": 2, "z": 8, "x_hi": 2, "y": 4}
GOSSIP = ("x_lo", "core")
FSDP = ("z", "x_hi", "y")

ROWS = 112
HALF = 128
BLOCK = 1024


def shifted(value, axis, steps):
    count = SIZES[axis]
    pairs = [((place + steps) % count, place) for place in range(count)]
    return lax.ppermute(value, axis, pairs)


def transposed(value):
    pairs = [(2 * x_hi + core, 2 * core + x_hi) for core in range(2) for x_hi in range(2)]
    return lax.ppermute(value, ("core", "x_hi"), pairs)


def held(value, *ready):
    return pl.pallas_call(
        lambda *refs: None,
        in_specs=[pl.BlockSpec(memory_space=pl.ANY)] * (1 + len(ready)),
        out_specs=pl.BlockSpec(memory_space=pl.ANY),
        out_shape=jax.ShapeDtypeStruct(value.shape, value.dtype),
        input_output_aliases={0: 0},
        compiler_params=params_of(1),
        name="held",
    )(value, *ready)


def silu_slope(preact):
    sigmoid_val = jax.nn.sigmoid(preact)
    return sigmoid_val * (1.0 + preact * (1.0 - sigmoid_val))


def plan_rate(step):
    phase = (step[0] % 1000).astype(jnp.float32) / 1000.0
    return 0.4 + 1.8 * (1.0 + jnp.cos(math.pi * phase))


def dot_t(rows, weights):
    return lax.dot_general(
        rows, weights, (((1,), (1,)), ((), ())), preferred_element_type=jnp.float32
    )


def params_of(vmem, **more):
    return pltpu.CompilerParams(vmem_limit_bytes=vmem * 2**20, **more)


def stack_kernel(*refs):
    *blocks, out_ref = refs
    for at, block in enumerate(blocks):
        count = block.shape[0]
        out_ref[at * count : (at + 1) * count, :] = block[...]


def stacked(blocks):
    count = blocks[0].shape[0]
    wide = D // 4
    return pl.pallas_call(
        stack_kernel,
        grid=(4,),
        in_specs=[pl.BlockSpec((count, wide), lambda at: (0, at))] * len(blocks),
        out_specs=pl.BlockSpec((count * len(blocks), wide), lambda at: (0, at)),
        out_shape=jax.ShapeDtypeStruct((count * len(blocks), D), blocks[0].dtype),
        compiler_params=params_of(8),
        name="stacked",
    )(*blocks)


def widen(wide, mine, theirs):
    wide[:ROWS, :] = mine[...]
    wide[HALF : HALF + ROWS, :] = theirs[...]


def clear(wide):
    pad = jnp.zeros((HALF - ROWS, wide.shape[1]), wide.dtype)
    wide[ROWS:HALF, :] = pad
    wide[HALF + ROWS :, :] = pad


def hidden_kernel(*refs):
    *parts, mine, theirs, out_ref, total, wide = refs
    at = pl.program_id(0)

    @pl.when(at == 0)
    def _():
        total[...] = jnp.zeros_like(total)
        clear(wide)

    widen(wide, mine, theirs)
    row = 0
    for part in parts:
        count = part.shape[0]
        total[row : row + count, :] += dot_t(part[...], wide[...])
        row += count

    @pl.when(at == pl.num_programs(0) - 1)
    def _():
        column, block = row // 4, row // 32
        for dz in range(8):
            for dy in range(4):
                start, place = dy * column + dz * block, (4 * dz + dy) * block
                out_ref[place : place + block, :] = total[start : start + block, :]


def hidden_of(parts, mine, theirs):
    count = sum(part.shape[0] for part in parts)
    weights = pl.BlockSpec((ROWS, BLOCK), lambda at: (2, at))
    return pl.pallas_call(
        hidden_kernel,
        grid=(D // BLOCK,),
        in_specs=[pl.BlockSpec((part.shape[0], BLOCK), lambda at: (0, at)) for part in parts]
        + [weights, weights],
        out_specs=pl.BlockSpec((count, 2 * HALF), lambda at: (0, 0)),
        out_shape=jax.ShapeDtypeStruct((count, 2 * HALF), jnp.float32),
        scratch_shapes=[
            pltpu.VMEM((count, 2 * HALF), jnp.float32),
            pltpu.VMEM((2 * HALF, BLOCK), jnp.bfloat16),
        ],
        compiler_params=params_of(16),
        cost_estimate=pl.CostEstimate(
            flops=2 * count * D * 2 * HALF, bytes_accessed=2 * count * D + 2**22, transcendentals=0
        ),
        name="hidden",
    )(*parts, mine, theirs)


def grad_kernel(*refs):
    *parts, my_params, their_params, my_up, their_up, hidden_ref, own_ref, other_ref = refs[:-6]
    rows, preact, up_proj, turned, wide_params, wide_up = refs[-6:]
    at = pl.program_id(0)

    @pl.when(at == 0)
    def _():
        preact[...] = jnp.zeros_like(preact)
        up_proj[...] = jnp.zeros_like(up_proj)
        clear(wide_params)
        clear(wide_up)

    columns = pl.ds(pl.multiple_of(at * BLOCK, BLOCK), BLOCK)
    row = 0
    for part in parts:
        count = part.shape[0]
        rows[row : row + count, columns] = part[...]
        row += count
    widen(wide_params, my_params, their_params)
    widen(wide_up, my_up, their_up)
    preact[...] += dot_t(rows[:, columns], wide_params[...])
    up_proj[...] += dot_t(rows[:, columns], wide_up[...])

    @pl.when(at == pl.num_programs(0) - 1)
    def _():
        slope = silu_slope(preact[...] * WIDTH_SCALE)
        turned[...] = (hidden_ref[...] * up_proj[...] * slope).T.astype(jnp.bfloat16)

        @pl.loop(0, D // BLOCK)
        def _(block):
            columns = pl.ds(pl.multiple_of(block * BLOCK, BLOCK), BLOCK)
            grad = jnp.dot(turned[...], rows[:, columns], preferred_element_type=jnp.float32)
            own_ref[:, columns] = grad[:ROWS] * WIDTH_SCALE
            other_ref[:, columns] = grad[HALF : HALF + ROWS] * WIDTH_SCALE


def gate_grads(parts, mine, theirs, hidden):
    count = sum(part.shape[0] for part in parts)

    def weights(which):
        return pl.BlockSpec((ROWS, BLOCK), lambda at: (which, at))

    whole = pl.BlockSpec((ROWS, D), lambda at: (0, 0))
    return pl.pallas_call(
        grad_kernel,
        grid=(D // BLOCK,),
        in_specs=[pl.BlockSpec((part.shape[0], BLOCK), lambda at: (0, at)) for part in parts]
        + [weights(0), weights(0), weights(1), weights(1)]
        + [pl.BlockSpec((count, 2 * HALF), lambda at: (0, 0))],
        out_specs=[whole, whole],
        out_shape=[jax.ShapeDtypeStruct((ROWS, D), jnp.float32)] * 2,
        scratch_shapes=[
            pltpu.VMEM((count, D), jnp.bfloat16),
            pltpu.VMEM((count, 2 * HALF), jnp.float32),
            pltpu.VMEM((count, 2 * HALF), jnp.float32),
            pltpu.VMEM((2 * HALF, count), jnp.bfloat16),
            pltpu.VMEM((2 * HALF, BLOCK), jnp.bfloat16),
            pltpu.VMEM((2 * HALF, BLOCK), jnp.bfloat16),
        ],
        compiler_params=params_of(36),
        cost_estimate=pl.CostEstimate(
            flops=2 * count * D * 768, bytes_accessed=2 * count * D + 2**23, transcendentals=0
        ),
        name="gate_grads",
    )(*parts, mine, theirs, mine, theirs, hidden)


def crossed(value):
    pairs = [
        (2 * (1 - x_hi) + core, 2 * core + x_hi) for core in range(2) for x_hi in range(2)
    ]
    return lax.ppermute(value, ("core", "x_hi"), pairs)


def shards(
    tokens, cotangent, gate_num, push_weight, stale_num, stale_weight, up_weight, down_weight, step
):
    rate = plan_rate(step)
    numerator = gate_num[0]

    params = (numerator / push_weight[0]).astype(jnp.bfloat16)
    weights = jnp.concatenate([params, up_weight, down_weight], axis=0)
    rows_in, rows_grad = transposed(tokens[0]), transposed(cotangent[0])
    rows_in = held(rows_in, rows_grad, weights)
    near = [rows_in] + [shifted(rows_in, "y", steps) for steps in (1, 3, 2)]
    ring = {0: rows_grad, 1: shifted(rows_grad, "z", 1), 7: shifted(rows_grad, "z", 7)}
    mine = transposed(held(weights, rows_grad))
    ring[2], ring[6] = shifted(ring[1], "z", 1), shifted(ring[7], "z", 7)
    near[3] = held(near[3], ring[1], ring[7])
    blocks = {0: stacked(near)}
    for steps in (1, 7):
        blocks[steps] = shifted(blocks[0], "z", steps)
    ring[3], ring[5] = shifted(ring[2], "z", 1), shifted(ring[6], "z", 7)
    ring[4] = shifted(ring[2], "z", 2)
    column = stacked([ring[steps] for steps in range(8)])

    following, before = shifted(column, "y", 1), shifted(column, "y", 3)
    blocks[1], blocks[7] = held(blocks[1], column), held(blocks[7], column)
    blocks[2], blocks[6] = shifted(blocks[1], "z", 1), shifted(blocks[7], "z", 7)
    mine = held(mine, blocks[2], blocks[6])
    theirs = shifted(mine, "core", 1)
    stale = jnp.concatenate([stale_num[0], jnp.broadcast_to(stale_weight, (8, D))], axis=0)
    stale = held(stale, blocks[1])
    two_before = shifted(stale, "x_lo", 1)
    blocks[3], blocks[5] = shifted(blocks[2], "z", 1), shifted(blocks[6], "z", 7)
    following, before = held(following, blocks[2]), held(before, blocks[6])
    half = column.shape[0] // 2
    far = [shifted(following[:half], "y", 1), shifted(before[half:], "y", 3)]
    blocks[3], blocks[5] = held(blocks[3], following), held(blocks[5], before)
    cut = 48
    last = [shifted(blocks[3][:cut], "z", 1), shifted(blocks[5][cut:], "z", 7)]

    hidden = hidden_of([column, following, before, *far], mine, theirs)
    parts = [blocks[steps] for steps in (0, 1, 2, 3)] + last + [blocks[steps] for steps in (5, 6, 7)]
    own_grad, other_grad = gate_grads(parts, mine, theirs, hidden)
    two_before = held(two_before, own_grad)
    first = lax.axis_index("core") == 0
    one_before = jnp.where(first, shifted(two_before, "core", 1), shifted(stale, "core", 1))
    received = jnp.where(step[0] % 2 == 0, one_before, two_before)

    gate_grad = own_grad + shifted(other_grad, "core", 1)
    norm_sq = jnp.sum(gate_grad * gate_grad)
    gate_grad = transposed(gate_grad)
    for axes in ("z", "y"):
        norm_sq = lax.psum(norm_sq, axes)
    norm_sq = transposed(norm_sq) + crossed(norm_sq)

    clip_factor = jnp.minimum(1.0, MAX_NORM / jnp.sqrt(norm_sq + eps))
    kept_half = 0.5 * (numerator - rate * clip_factor * gate_grad)
    kept_weight = 0.5 * push_weight
    new_num = kept_half + received[:ROWS]
    new_weight = kept_weight + received[ROWS, :1]
    return (new_num[None], new_weight, kept_half[None], kept_weight)


def solution(mesh):
    named = Mesh(np.asarray(mesh.devices).reshape(tuple(SIZES.values())), tuple(SIZES))
    groups = P(GOSSIP, FSDP, None)
    in_specs = (
        groups,
        groups,
        groups,
        P(GOSSIP),
        groups,
        P(GOSSIP),
        P(FSDP, None),
        P(FSDP, None),
        P(),
    )
    out_specs = (groups, P(GOSSIP), groups, P(GOSSIP))
    return jax.shard_map(shards, mesh=named, in_specs=in_specs, out_specs=out_specs, check_vma=False)
```

```python
import math

import jax
import jax.numpy as jnp
import numpy as np
from jax import lax
from jax.experimental import pallas as pl
from jax.experimental.pallas import tpu as pltpu
from jax.sharding import Mesh, PartitionSpec as P

D = 5120
FFW = 7168

eps = 1e-06

WIDTH_SCALE = D ** (-0.5)
MAX_NORM = 0.05 * math.sqrt(D * FFW)

SIZES = {"x_lo": 2, "core": 2, "z": 8, "x_hi": 2, "y": 4}
GOSSIP = ("x_lo", "core")
FSDP = ("z", "x_hi", "y")

ROWS = 112
HALF = 128
CUT = 64
BLOCK = 1024


def shifted(value, axis, steps):
    count = SIZES[axis]
    pairs = [((place + steps) % count, place) for place in range(count)]
    return lax.ppermute(value, axis, pairs)


def transposed(value):
    pairs = [(2 * x_hi + core, 2 * core + x_hi) for core in range(2) for x_hi in range(2)]
    return lax.ppermute(value, ("core", "x_hi"), pairs)


def held(value, *ready):
    values = value if isinstance(value, tuple) else (value,)
    anywhere = pl.BlockSpec(memory_space=pl.ANY)
    out = pl.pallas_call(
        lambda *refs: None,
        in_specs=[anywhere] * (len(values) + len(ready)),
        out_specs=[anywhere] * len(values),
        out_shape=[jax.ShapeDtypeStruct(one.shape, one.dtype) for one in values],
        input_output_aliases={at: at for at in range(len(values))},
        compiler_params=params_of(1),
        name="held",
    )(*values, *ready)
    return tuple(out) if isinstance(value, tuple) else out[0]


def silu_slope(preact):
    sigmoid_val = jax.nn.sigmoid(preact)
    return sigmoid_val * (1.0 + preact * (1.0 - sigmoid_val))


def plan_rate(step):
    phase = (step[0] % 1000).astype(jnp.float32) / 1000.0
    return 0.4 + 1.8 * (1.0 + jnp.cos(math.pi * phase))


def dot_t(rows, weights):
    return lax.dot_general(
        rows, weights, (((1,), (1,)), ((), ())), preferred_element_type=jnp.float32
    )


def params_of(vmem, **more):
    return pltpu.CompilerParams(vmem_limit_bytes=vmem * 2**20, **more)


def stack_kernel(*refs):
    *blocks, out_ref = refs
    for at, block in enumerate(blocks):
        count = block.shape[0]
        out_ref[at * count : (at + 1) * count, :] = block[...]


def stacked(blocks):
    count = blocks[0].shape[0]
    wide = D // 4
    return pl.pallas_call(
        stack_kernel,
        grid=(4,),
        in_specs=[pl.BlockSpec((count, wide), lambda at: (0, at))] * len(blocks),
        out_specs=pl.BlockSpec((count * len(blocks), wide), lambda at: (0, at)),
        out_shape=jax.ShapeDtypeStruct((count * len(blocks), D), blocks[0].dtype),
        compiler_params=params_of(8),
        name="stacked",
    )(*blocks)


def widen(wide, mine, theirs):
    wide[:ROWS, :] = mine[...]
    wide[HALF : HALF + ROWS, :] = theirs[...]


def clear(wide):
    pad = jnp.zeros((HALF - ROWS, wide.shape[1]), wide.dtype)
    wide[ROWS:HALF, :] = pad
    wide[HALF + ROWS :, :] = pad


def hidden_kernel(*refs):
    *parts, mine, theirs, out_ref, total, wide = refs
    at = pl.program_id(0)

    @pl.when(at == 0)
    def _():
        total[...] = jnp.zeros_like(total)
        clear(wide)

    widen(wide, mine, theirs)
    row = 0
    for part in parts:
        count = part.shape[0]
        total[row : row + count, :] += dot_t(part[...], wide[...])
        row += count

    @pl.when(at == pl.num_programs(0) - 1)
    def _():
        column, block = row // 4, row // 32
        for dz in range(8):
            for dy in range(4):
                start, place = dy * column + dz * block, (4 * dz + dy) * block
                out_ref[place : place + block, :] = total[start : start + block, :]


def hidden_of(parts, mine, theirs):
    count = sum(part.shape[0] for part in parts)
    weights = pl.BlockSpec((ROWS, BLOCK), lambda at: (2, at))
    return pl.pallas_call(
        hidden_kernel,
        grid=(D // BLOCK,),
        in_specs=[pl.BlockSpec((part.shape[0], BLOCK), lambda at: (0, at)) for part in parts]
        + [weights, weights],
        out_specs=pl.BlockSpec((count, 2 * HALF), lambda at: (0, 0)),
        out_shape=jax.ShapeDtypeStruct((count, 2 * HALF), jnp.float32),
        scratch_shapes=[
            pltpu.VMEM((count, 2 * HALF), jnp.float32),
            pltpu.VMEM((2 * HALF, BLOCK), jnp.bfloat16),
        ],
        compiler_params=params_of(16),
        cost_estimate=pl.CostEstimate(
            flops=2 * count * D * 2 * HALF, bytes_accessed=2 * count * D + 2**22, transcendentals=0
        ),
        name="hidden",
    )(*parts, mine, theirs)


def grad_kernel(*refs):
    *parts, my_params, their_params, my_up, their_up, hidden_ref, own_ref, other_ref = refs[:-6]
    rows, preact, up_proj, turned, wide_params, wide_up = refs[-6:]
    at = pl.program_id(0)

    @pl.when(at == 0)
    def _():
        preact[...] = jnp.zeros_like(preact)
        up_proj[...] = jnp.zeros_like(up_proj)
        clear(wide_params)
        clear(wide_up)

    columns = pl.ds(pl.multiple_of(at * BLOCK, BLOCK), BLOCK)
    row = 0
    for part in parts:
        count = part.shape[0]
        rows[row : row + count, columns] = part[...]
        row += count
    widen(wide_params, my_params, their_params)
    widen(wide_up, my_up, their_up)
    preact[...] += dot_t(rows[:, columns], wide_params[...])
    up_proj[...] += dot_t(rows[:, columns], wide_up[...])

    @pl.when(at == pl.num_programs(0) - 1)
    def _():
        slope = silu_slope(preact[...] * WIDTH_SCALE)
        turned[...] = (hidden_ref[...] * up_proj[...] * slope).T.astype(jnp.bfloat16)

        @pl.loop(0, D // BLOCK)
        def _(block):
            columns = pl.ds(pl.multiple_of(block * BLOCK, BLOCK), BLOCK)
            grad = jnp.dot(turned[...], rows[:, columns], preferred_element_type=jnp.float32)
            own_ref[:, columns] = grad[:ROWS] * WIDTH_SCALE
            other_ref[:, columns] = grad[HALF : HALF + ROWS] * WIDTH_SCALE


def gate_grads(parts, mine, theirs, hidden):
    count = sum(part.shape[0] for part in parts)

    def weights(which):
        return pl.BlockSpec((ROWS, BLOCK), lambda at: (which, at))

    whole = pl.BlockSpec((ROWS, D), lambda at: (0, 0))
    return pl.pallas_call(
        grad_kernel,
        grid=(D // BLOCK,),
        in_specs=[pl.BlockSpec((part.shape[0], BLOCK), lambda at: (0, at)) for part in parts]
        + [weights(0), weights(0), weights(1), weights(1)]
        + [pl.BlockSpec((count, 2 * HALF), lambda at: (0, 0))],
        out_specs=[whole, whole],
        out_shape=[jax.ShapeDtypeStruct((ROWS, D), jnp.float32)] * 2,
        scratch_shapes=[
            pltpu.VMEM((count, D), jnp.bfloat16),
            pltpu.VMEM((count, 2 * HALF), jnp.float32),
            pltpu.VMEM((count, 2 * HALF), jnp.float32),
            pltpu.VMEM((2 * HALF, count), jnp.bfloat16),
            pltpu.VMEM((2 * HALF, BLOCK), jnp.bfloat16),
            pltpu.VMEM((2 * HALF, BLOCK), jnp.bfloat16),
        ],
        compiler_params=params_of(36),
        cost_estimate=pl.CostEstimate(
            flops=2 * count * D * 768, bytes_accessed=2 * count * D + 2**23, transcendentals=0
        ),
        name="gate_grads",
    )(*parts, mine, theirs, mine, theirs, hidden)


def updated_kernel(factor, which, numerator, grad, *refs):
    *parts, kept_ref, new_ref = refs
    kept = 0.5 * (numerator[...] - factor[0] * grad[...])
    kept_ref[...] = kept
    for at in range(3):

        @pl.when(which[0] == at)
        def _():
            new_ref[:CUT, :] = kept[:CUT] + parts[2 * at][...]
            new_ref[CUT:, :] = kept[CUT:] + parts[2 * at + 1][: ROWS - CUT, :]


def updated(numerator, grad, factor, which, received):
    own = pl.BlockSpec((ROWS, BLOCK), lambda at: (0, at))
    scalar = pl.BlockSpec(memory_space=pltpu.SMEM)
    more = [part for parts in received for part in parts]
    return pl.pallas_call(
        updated_kernel,
        grid=(D // BLOCK,),
        in_specs=[scalar, scalar, own, own]
        + [pl.BlockSpec((part.shape[0], BLOCK), lambda at: (0, at)) for part in more],
        out_specs=[own, own],
        out_shape=[jax.ShapeDtypeStruct((ROWS, D), jnp.float32)] * 2,
        compiler_params=params_of(16),
        name="updated",
    )(jnp.reshape(factor, (1,)), jnp.reshape(which, (1,)), numerator, grad, *more)


def crossed(value):
    pairs = [
        (2 * (1 - x_hi) + core, 2 * core + x_hi) for core in range(2) for x_hi in range(2)
    ]
    return lax.ppermute(value, ("core", "x_hi"), pairs)


def shards(
    tokens, cotangent, gate_num, push_weight, stale_num, stale_weight, up_weight, down_weight, step
):
    rate = plan_rate(step)
    numerator = gate_num[0]

    params = (numerator / push_weight[0]).astype(jnp.bfloat16)
    weights = jnp.concatenate([params, up_weight, down_weight], axis=0)
    rows_in, rows_grad = transposed(tokens[0]), transposed(cotangent[0])
    rows_in = held(rows_in, rows_grad, weights)
    near = [rows_in] + [shifted(rows_in, "y", steps) for steps in (1, 3, 2)]
    ring = {0: rows_grad, 1: shifted(rows_grad, "z", 1), 7: shifted(rows_grad, "z", 7)}
    mine = transposed(held(weights, rows_grad))
    ring[2], ring[6] = shifted(ring[1], "z", 1), shifted(ring[7], "z", 7)
    near[3] = held(near[3], ring[2], ring[6])
    blocks = {0: stacked(near)}
    for steps in (1, 7):
        blocks[steps] = shifted(blocks[0], "z", steps)
    ring[3], ring[5] = shifted(ring[2], "z", 1), shifted(ring[6], "z", 7)
    ring[4] = shifted(ring[2], "z", 2)
    column = stacked([ring[steps] for steps in range(8)])

    following, before = shifted(column, "y", 1), shifted(column, "y", 3)
    blocks[1], blocks[7] = held((blocks[1], blocks[7]), column)
    blocks[2], blocks[6] = shifted(blocks[1], "z", 1), shifted(blocks[7], "z", 7)
    blocks[2], blocks[6] = held((blocks[2], blocks[6]))
    blocks[3], blocks[5] = shifted(blocks[2], "z", 1), shifted(blocks[6], "z", 7)
    following, before = held((following, before), blocks[2], blocks[6])
    weight_rows = jnp.broadcast_to(stale_weight, (8, D))
    stale = [stale_num[0, :CUT], jnp.concatenate([stale_num[0, CUT:], weight_rows], axis=0)]
    stale[0] = held(stale[0], mine)
    two_before = [shifted(stale[0], "x_lo", 1)]
    stale[1] = held(stale[1], two_before[0])
    two_before.append(shifted(stale[1], "x_lo", 1))
    mine = held(mine, following, before)
    theirs = shifted(mine, "core", 1)
    half = column.shape[0] // 2
    far = [shifted(following[:half], "y", 1), shifted(before[half:], "y", 3)]
    blocks[3], blocks[5] = held((blocks[3], blocks[5]), following, before)
    cut = 48
    last = [shifted(blocks[3][:cut], "z", 1), shifted(blocks[5][cut:], "z", 7)]

    hidden = hidden_of([column, following, before, *far], mine, theirs)
    parts = [blocks[steps] for steps in (0, 1, 2, 3)] + last + [blocks[steps] for steps in (5, 6, 7)]
    first_hop = shifted(two_before[0], "core", 1)
    stale_hop = [shifted(part, "core", 1) for part in stale]
    hidden = held(hidden, first_hop, *stale_hop)
    own_grad, other_grad = gate_grads(parts, mine, theirs, hidden)
    gate_grad = own_grad + shifted(other_grad, "core", 1)
    norm_sq = jnp.sum(gate_grad * gate_grad)
    gate_grad = transposed(gate_grad)
    norm_sq = lax.psum(norm_sq, "z")
    two_before[1] = held(two_before[1], jnp.reshape(norm_sq, (1,)))
    received = [two_before, [first_hop, shifted(two_before[1], "core", 1)], stale_hop]
    norm_sq = lax.psum(norm_sq, "y")
    norm_sq = transposed(norm_sq) + crossed(norm_sq)

    clip_factor = jnp.minimum(1.0, MAX_NORM / jnp.sqrt(norm_sq + eps))
    which = jnp.where(step[0] % 2 == 1, 0, 1 + lax.axis_index("core"))
    kept_half, new_num = updated(numerator, gate_grad, rate * clip_factor, which, received)
    kept_weight = 0.5 * push_weight
    new_weight = kept_weight + jnp.stack([parts[1][-1, :1] for parts in received])[which]
    return (new_num[None], new_weight, kept_half[None], kept_weight)


def solution(mesh):
    named = Mesh(np.asarray(mesh.devices).reshape(tuple(SIZES.values())), tuple(SIZES))
    groups = P(GOSSIP, FSDP, None)
    in_specs = (
        groups,
        groups,
        groups,
        P(GOSSIP),
        groups,
        P(GOSSIP),
        P(FSDP, None),
        P(FSDP, None),
        P(),
    )
    out_specs = (groups, P(GOSSIP), groups, P(GOSSIP))
    return jax.shard_map(shards, mesh=named, in_specs=in_specs, out_specs=out_specs, check_vma=False)
```

```python
import math

import jax
import jax.numpy as jnp
import numpy as np
from jax import lax
from jax.experimental import pallas as pl
from jax.experimental.pallas import tpu as pltpu
from jax.sharding import Mesh, PartitionSpec as P

D = 5120
FFW = 7168

eps = 1e-06

WIDTH_SCALE = D ** (-0.5)
MAX_NORM = 0.05 * math.sqrt(D * FFW)

SIZES = {"x_lo": 2, "core": 2, "z": 8, "x_hi": 2, "y": 4}
GOSSIP = ("x_lo", "core")
FSDP = ("z", "x_hi", "y")

ROWS = 112
HALF = 128
NO_COST = pl.CostEstimate(flops=1, bytes_accessed=1, transcendentals=0)
BLOCK = 1024


def shifted(value, axis, steps):
    count = SIZES[axis]
    pairs = [((place + steps) % count, place) for place in range(count)]
    return lax.ppermute(value, axis, pairs)


def transposed(value):
    pairs = [(2 * x_hi + core, 2 * core + x_hi) for core in range(2) for x_hi in range(2)]
    return lax.ppermute(value, ("core", "x_hi"), pairs)


def held(value, *ready):
    values = value if isinstance(value, tuple) else (value,)
    anywhere = pl.BlockSpec(memory_space=pl.ANY)
    out = pl.pallas_call(
        lambda *refs: None,
        in_specs=[anywhere] * (len(values) + len(ready)),
        out_specs=[anywhere] * len(values),
        out_shape=[jax.ShapeDtypeStruct(one.shape, one.dtype) for one in values],
        input_output_aliases={at: at for at in range(len(values))},
        compiler_params=params_of(1),
        name="held",
    )(*values, *ready)
    return tuple(out) if isinstance(value, tuple) else out[0]


def silu_slope(preact):
    sigmoid_val = jax.nn.sigmoid(preact)
    return sigmoid_val * (1.0 + preact * (1.0 - sigmoid_val))


def plan_rate(step):
    phase = (step[0] % 1000).astype(jnp.float32) / 1000.0
    return 0.4 + 1.8 * (1.0 + jnp.cos(math.pi * phase))


def dot_t(rows, weights):
    return lax.dot_general(
        rows, weights, (((1,), (1,)), ((), ())), preferred_element_type=jnp.float32
    )


def params_of(vmem, **more):
    return pltpu.CompilerParams(vmem_limit_bytes=vmem * 2**20, **more)


def stack_kernel(*refs):
    *blocks, out_ref = refs
    for at, block in enumerate(blocks):
        count = block.shape[0]
        out_ref[at * count : (at + 1) * count, :] = block[...]


def stacked(blocks):
    count = blocks[0].shape[0]
    wide = D // 4
    return pl.pallas_call(
        stack_kernel,
        grid=(4,),
        in_specs=[pl.BlockSpec((count, wide), lambda at: (0, at))] * len(blocks),
        out_specs=pl.BlockSpec((count * len(blocks), wide), lambda at: (0, at)),
        out_shape=jax.ShapeDtypeStruct((count * len(blocks), D), blocks[0].dtype),
        compiler_params=params_of(8),
        name="stacked",
    )(*blocks)


def widen(wide, mine, theirs):
    wide[:ROWS, :] = mine[...]
    wide[HALF : HALF + ROWS, :] = theirs[...]


def clear(wide):
    pad = jnp.zeros((HALF - ROWS, wide.shape[1]), wide.dtype)
    wide[ROWS:HALF, :] = pad
    wide[HALF + ROWS :, :] = pad


def hidden_kernel(z_ref, *refs):
    *parts, mine, theirs, out_ref, total, wide, tile = refs
    at = pl.program_id(0)

    @pl.when(at == 0)
    def _():
        total[...] = jnp.zeros_like(total)
        clear(wide)

    widen(wide, mine, theirs)
    row = 0
    for part in parts:
        count = part.shape[0]
        total[row : row + count, :] += dot_t(part[...], wide[...])
        row += count

    @pl.when(at == pl.num_programs(0) - 1)
    def _():
        column, block = row // 4, row // 32
        for dz in range(8):
            for dy in range(4):
                start = dy * column + dz * block
                tile[dy * block : (dy + 1) * block, :] = total[start : start + block, :]
            place = pl.multiple_of(lax.rem(z_ref[0] + dz, 8) * (4 * block), 16)
            out_ref[pl.ds(place, 4 * block), :] = tile[...]


def hidden_of(parts, mine, theirs):
    count = sum(part.shape[0] for part in parts)
    z = jnp.reshape(lax.axis_index("z"), (1,)).astype(jnp.int32)
    weights = pl.BlockSpec((ROWS, BLOCK), lambda at: (2, at))
    return pl.pallas_call(
        hidden_kernel,
        grid=(D // BLOCK,),
        in_specs=[pl.BlockSpec(memory_space=pltpu.SMEM)]
        + [pl.BlockSpec((part.shape[0], BLOCK), lambda at: (0, at)) for part in parts]
        + [weights, weights],
        out_specs=pl.BlockSpec((count, 2 * HALF), lambda at: (0, 0)),
        out_shape=jax.ShapeDtypeStruct((count, 2 * HALF), jnp.float32),
        scratch_shapes=[
            pltpu.VMEM((count, 2 * HALF), jnp.float32),
            pltpu.VMEM((2 * HALF, BLOCK), jnp.bfloat16),
            pltpu.VMEM((count // 8, 2 * HALF), jnp.float32),
        ],
        compiler_params=params_of(16),
        cost_estimate=NO_COST,
        name="hidden",
    )(z, *parts, mine, theirs)


def grad_kernel(
    x_ref, my_params, their_params, my_up, their_up, hidden_ref, own_ref, other_ref,
    rows, preact, up_proj, turned, wide_params, wide_up, sems,
):
    at = pl.program_id(0)
    blocks = D // BLOCK

    def copy(block):
        columns = pl.ds(block * BLOCK, BLOCK)
        return pltpu.make_async_copy(x_ref.at[:, columns], rows.at[:, columns], sems.at[block])

    @pl.when(at == 0)
    def _():
        for block in range(blocks):
            copy(block).start()
        preact[...] = jnp.zeros_like(preact)
        up_proj[...] = jnp.zeros_like(up_proj)
        clear(wide_params)
        clear(wide_up)

    widen(wide_params, my_params, their_params)
    widen(wide_up, my_up, their_up)
    for block in range(blocks):

        @pl.when(at == block)
        def _():
            copy(block).wait()
            part = rows[:, block * BLOCK : (block + 1) * BLOCK]
            preact[...] += dot_t(part, wide_params[...])
            up_proj[...] += dot_t(part, wide_up[...])

    @pl.when(at == blocks - 1)
    def _():
        slope = silu_slope(preact[...] * WIDTH_SCALE)
        turned[...] = (hidden_ref[...] * up_proj[...] * slope).T.astype(jnp.bfloat16)

        @pl.loop(0, blocks)
        def _(block):
            columns = pl.ds(pl.multiple_of(block * BLOCK, BLOCK), BLOCK)
            grad = jnp.dot(turned[...], rows[:, columns], preferred_element_type=jnp.float32)
            own_ref[:, columns] = grad[:ROWS] * WIDTH_SCALE
            other_ref[:, columns] = grad[HALF : HALF + ROWS] * WIDTH_SCALE


def gate_grads(rows_in, mine, theirs, hidden):
    count = rows_in.shape[0]
    blocks = D // BLOCK

    def weights(which):
        return pl.BlockSpec((ROWS, BLOCK), lambda at: (which, at))

    whole = pl.BlockSpec((ROWS, D), lambda at: (0, 0))
    return pl.pallas_call(
        grad_kernel,
        grid=(blocks,),
        in_specs=[pl.BlockSpec(memory_space=pl.ANY)]
        + [weights(0), weights(0), weights(1), weights(1)]
        + [pl.BlockSpec((count, 2 * HALF), lambda at: (0, 0))],
        out_specs=[whole, whole],
        out_shape=[jax.ShapeDtypeStruct((ROWS, D), jnp.float32)] * 2,
        scratch_shapes=[
            pltpu.VMEM((count, D), jnp.bfloat16),
            pltpu.VMEM((count, 2 * HALF), jnp.float32),
            pltpu.VMEM((count, 2 * HALF), jnp.float32),
            pltpu.VMEM((2 * HALF, count), jnp.bfloat16),
            pltpu.VMEM((2 * HALF, BLOCK), jnp.bfloat16),
            pltpu.VMEM((2 * HALF, BLOCK), jnp.bfloat16),
            pltpu.SemaphoreType.DMA((blocks,)),
        ],
        compiler_params=params_of(36),
        cost_estimate=NO_COST,
        name="gate_grads",
    )(rows_in, mine, theirs, mine, theirs, hidden)


def updated_kernel(factor, which, kept_weight, numerator, grad, *refs):
    *received, kept_ref, new_ref, weight_ref, part, sems = refs
    at = pl.program_id(0)
    blocks = D // BLOCK

    def copy(source, block):
        columns = pl.ds(block * BLOCK, BLOCK)
        return pltpu.make_async_copy(source.at[:, columns], part.at[:, columns], sems.at[block])

    @pl.when(at == 0)
    def _():
        for place, source in enumerate(received):

            @pl.when(which[0] == place)
            def _():
                for block in range(blocks):
                    copy(source, block).start()

    kept = 0.5 * (numerator[...] - factor[0] * grad[...])
    kept_ref[...] = kept
    for block in range(blocks):

        @pl.when(at == block)
        def _():
            copy(received[0], block).wait()
            new_ref[...] = kept + part[:ROWS, block * BLOCK : (block + 1) * BLOCK]

    @pl.when(at == 0)
    def _():
        weight_ref[0] = kept_weight[0] + jnp.max(part[ROWS:, :128])


def updated(numerator, grad, kept_weight, factor, which, received):
    own = pl.BlockSpec((ROWS, BLOCK), lambda at: (0, at))
    scalar = pl.BlockSpec(memory_space=pltpu.SMEM)
    anywhere = pl.BlockSpec(memory_space=pl.ANY)
    blocks = D // BLOCK
    return pl.pallas_call(
        updated_kernel,
        grid=(blocks,),
        in_specs=[scalar, scalar, scalar, own, own] + [anywhere] * len(received),
        out_specs=[own, own, scalar],
        out_shape=[
            jax.ShapeDtypeStruct((ROWS, D), jnp.float32),
            jax.ShapeDtypeStruct((ROWS, D), jnp.float32),
            jax.ShapeDtypeStruct((1,), jnp.float32),
        ],
        scratch_shapes=[
            pltpu.VMEM(received[0].shape, jnp.float32),
            pltpu.SemaphoreType.DMA((blocks,)),
        ],
        compiler_params=params_of(16),
        name="updated",
    )(
        jnp.reshape(factor, (1,)), jnp.reshape(which, (1,)), kept_weight,
        numerator, grad, *received,
    )


def crossed(value):
    pairs = [
        (2 * (1 - x_hi) + core, 2 * core + x_hi) for core in range(2) for x_hi in range(2)
    ]
    return lax.ppermute(value, ("core", "x_hi"), pairs)


def shards(
    tokens, cotangent, gate_num, push_weight, stale_num, stale_weight, up_weight, down_weight, step
):
    rate = plan_rate(step)
    numerator = gate_num[0]

    params = (numerator / push_weight[0]).astype(jnp.bfloat16)
    weights = jnp.concatenate([params, up_weight, down_weight], axis=0)
    rows_in, rows_grad = transposed(tokens[0]), transposed(cotangent[0])
    rows_in = held(rows_in, rows_grad, weights)
    near = [rows_in] + [shifted(rows_in, "y", steps) for steps in (1, 3, 2)]
    ring = {0: rows_grad, 1: shifted(rows_grad, "z", 1), 7: shifted(rows_grad, "z", 7)}
    near[3] = held(near[3], ring[1], ring[7])
    near = stacked(near)
    rows_in = lax.all_gather(near, "z", axis=0, tiled=True)
    mine = transposed(held(weights, rows_grad))
    ring[2], ring[6] = shifted(ring[1], "z", 1), shifted(ring[7], "z", 7)
    ring[3], ring[5] = shifted(ring[2], "z", 1), shifted(ring[6], "z", 7)
    ring[4] = shifted(ring[2], "z", 2)
    column = stacked([ring[steps] for steps in range(8)])
    column = held(column, near)
    following, before = shifted(column, "y", 1), shifted(column, "y", 3)
    mine = held(mine, column)
    theirs = shifted(mine, "core", 1)
    stale = jnp.concatenate([stale_num[0], jnp.broadcast_to(stale_weight, (8, D))], axis=0)
    stale = held(stale, mine)
    two_before = shifted(stale, "x_lo", 1)
    following, before = held((following, before), theirs)
    half = column.shape[0] // 2
    far = [shifted(following[:half], "y", 1), shifted(before[half:], "y", 3)]
    hidden = hidden_of([column, following, before, *far], mine, theirs)

    two_before = held(two_before, hidden)
    received = (two_before, shifted(two_before, "core", 1), shifted(stale, "core", 1))
    hidden = held(hidden, *received[1:])
    own_grad, other_grad = gate_grads(rows_in, mine, theirs, hidden)
    gate_grad = own_grad + shifted(other_grad, "core", 1)
    norm_sq = jnp.sum(gate_grad * gate_grad)
    gate_grad = transposed(gate_grad)
    for axes in ("z", "y"):
        norm_sq = lax.psum(norm_sq, axes)
    norm_sq = transposed(norm_sq) + crossed(norm_sq)

    clip_factor = jnp.minimum(1.0, MAX_NORM / jnp.sqrt(norm_sq + eps))
    kept_weight = 0.5 * push_weight
    which = jnp.where(step[0] % 2 == 1, 0, 1 + lax.axis_index("core"))
    kept_half, new_num, new_weight = updated(
        numerator, gate_grad, kept_weight, rate * clip_factor, which, received
    )
    return (new_num[None], new_weight, kept_half[None], kept_weight)


def solution(mesh):
    named = Mesh(np.asarray(mesh.devices).reshape(tuple(SIZES.values())), tuple(SIZES))
    groups = P(GOSSIP, FSDP, None)
    in_specs = (
        groups,
        groups,
        groups,
        P(GOSSIP),
        groups,
        P(GOSSIP),
        P(FSDP, None),
        P(FSDP, None),
        P(),
    )
    out_specs = (groups, P(GOSSIP), groups, P(GOSSIP))
    return jax.shard_map(shards, mesh=named, in_specs=in_specs, out_specs=out_specs, check_vma=False)
```

```python
import math

import jax
import jax.numpy as jnp
import numpy as np
from jax import lax
from jax.experimental import pallas as pl
from jax.experimental.pallas import tpu as pltpu
from jax.sharding import Mesh, PartitionSpec as P

D = 5120
FFW = 7168

eps = 1e-06

WIDTH_SCALE = D ** (-0.5)
MAX_NORM = 0.05 * math.sqrt(D * FFW)

SIZES = {"x_lo": 2, "core": 2, "z": 8, "x_hi": 2, "y": 4}
GOSSIP = ("x_lo", "core")
FSDP = ("z", "x_hi", "y")

ROWS = 112
HALF = 128
CUT = 64
NO_COST = pl.CostEstimate(flops=1, bytes_accessed=1, transcendentals=0)
BLOCK = 1024


def shifted(value, axis, steps):
    count = SIZES[axis]
    pairs = [((place + steps) % count, place) for place in range(count)]
    return lax.ppermute(value, axis, pairs)


def transposed(value):
    pairs = [(2 * x_hi + core, 2 * core + x_hi) for core in range(2) for x_hi in range(2)]
    return lax.ppermute(value, ("core", "x_hi"), pairs)


def held(value, *ready):
    values = value if isinstance(value, tuple) else (value,)
    anywhere = pl.BlockSpec(memory_space=pl.ANY)
    out = pl.pallas_call(
        lambda *refs: None,
        in_specs=[anywhere] * (len(values) + len(ready)),
        out_specs=[anywhere] * len(values),
        out_shape=[jax.ShapeDtypeStruct(one.shape, one.dtype) for one in values],
        input_output_aliases={at: at for at in range(len(values))},
        compiler_params=params_of(1),
        name="held",
    )(*values, *ready)
    return tuple(out) if isinstance(value, tuple) else out[0]


def silu_slope(preact):
    sigmoid_val = jax.nn.sigmoid(preact)
    return sigmoid_val * (1.0 + preact * (1.0 - sigmoid_val))


def plan_rate(step):
    phase = (step[0] % 1000).astype(jnp.float32) / 1000.0
    return 0.4 + 1.8 * (1.0 + jnp.cos(math.pi * phase))


def dot_t(rows, weights):
    return lax.dot_general(
        rows, weights, (((1,), (1,)), ((), ())), preferred_element_type=jnp.float32
    )


def params_of(vmem, **more):
    return pltpu.CompilerParams(vmem_limit_bytes=vmem * 2**20, **more)


def stack_kernel(*refs):
    *blocks, out_ref = refs
    for at, block in enumerate(blocks):
        count = block.shape[0]
        out_ref[at * count : (at + 1) * count, :] = block[...]


def stacked(blocks):
    count = blocks[0].shape[0]
    wide = D // 4
    return pl.pallas_call(
        stack_kernel,
        grid=(4,),
        in_specs=[pl.BlockSpec((count, wide), lambda at: (0, at))] * len(blocks),
        out_specs=pl.BlockSpec((count * len(blocks), wide), lambda at: (0, at)),
        out_shape=jax.ShapeDtypeStruct((count * len(blocks), D), blocks[0].dtype),
        compiler_params=params_of(8),
        name="stacked",
    )(*blocks)


def widen(wide, mine, theirs):
    wide[:ROWS, :] = mine[...]
    wide[HALF : HALF + ROWS, :] = theirs[...]


def clear(wide):
    pad = jnp.zeros((HALF - ROWS, wide.shape[1]), wide.dtype)
    wide[ROWS:HALF, :] = pad
    wide[HALF + ROWS :, :] = pad


def hidden_kernel(*refs):
    *parts, mine, theirs, out_ref, total, wide = refs
    at = pl.program_id(0)

    @pl.when(at == 0)
    def _():
        total[...] = jnp.zeros_like(total)
        clear(wide)

    widen(wide, mine, theirs)
    row = 0
    for part in parts:
        count = part.shape[0]
        total[row : row + count, :] += dot_t(part[...], wide[...])
        row += count

    @pl.when(at == pl.num_programs(0) - 1)
    def _():
        column, block = row // 4, row // 32
        for dz in range(8):
            for dy in range(4):
                start, place = dy * column + dz * block, (4 * dz + dy) * block
                out_ref[place : place + block, :] = total[start : start + block, :]


def hidden_of(parts, mine, theirs):
    count = sum(part.shape[0] for part in parts)
    weights = pl.BlockSpec((ROWS, BLOCK), lambda at: (2, at))
    return pl.pallas_call(
        hidden_kernel,
        grid=(D // BLOCK,),
        in_specs=[pl.BlockSpec((part.shape[0], BLOCK), lambda at: (0, at)) for part in parts]
        + [weights, weights],
        out_specs=pl.BlockSpec((count, 2 * HALF), lambda at: (0, 0)),
        out_shape=jax.ShapeDtypeStruct((count, 2 * HALF), jnp.float32),
        scratch_shapes=[
            pltpu.VMEM((count, 2 * HALF), jnp.float32),
            pltpu.VMEM((2 * HALF, BLOCK), jnp.bfloat16),
        ],
        compiler_params=params_of(16),
        cost_estimate=NO_COST,
        name="hidden",
    )(*parts, mine, theirs)


def grad_kernel(*refs):
    *parts, my_params, their_params, my_up, their_up, hidden_ref, own_ref, other_ref = refs[:-6]
    rows, preact, up_proj, turned, wide_params, wide_up = refs[-6:]
    at = pl.program_id(0)

    @pl.when(at == 0)
    def _():
        preact[...] = jnp.zeros_like(preact)
        up_proj[...] = jnp.zeros_like(up_proj)
        clear(wide_params)
        clear(wide_up)

    columns = pl.ds(pl.multiple_of(at * BLOCK, BLOCK), BLOCK)
    row = 0
    for part in parts:
        count = part.shape[0]
        rows[row : row + count, columns] = part[...]
        row += count
    widen(wide_params, my_params, their_params)
    widen(wide_up, my_up, their_up)
    preact[...] += dot_t(rows[:, columns], wide_params[...])
    up_proj[...] += dot_t(rows[:, columns], wide_up[...])

    @pl.when(at == pl.num_programs(0) - 1)
    def _():
        slope = silu_slope(preact[...] * WIDTH_SCALE)
        turned[...] = (hidden_ref[...] * up_proj[...] * slope).T.astype(jnp.bfloat16)

        @pl.loop(0, D // BLOCK)
        def _(block):
            columns = pl.ds(pl.multiple_of(block * BLOCK, BLOCK), BLOCK)
            grad = jnp.dot(turned[...], rows[:, columns], preferred_element_type=jnp.float32)
            own_ref[:, columns] = grad[:ROWS] * WIDTH_SCALE
            other_ref[:, columns] = grad[HALF : HALF + ROWS] * WIDTH_SCALE


def gate_grads(parts, mine, theirs, hidden):
    count = sum(part.shape[0] for part in parts)

    def weights(which):
        return pl.BlockSpec((ROWS, BLOCK), lambda at: (which, at))

    whole = pl.BlockSpec((ROWS, D), lambda at: (0, 0))
    return pl.pallas_call(
        grad_kernel,
        grid=(D // BLOCK,),
        in_specs=[pl.BlockSpec((part.shape[0], BLOCK), lambda at: (0, at)) for part in parts]
        + [weights(0), weights(0), weights(1), weights(1)]
        + [pl.BlockSpec((count, 2 * HALF), lambda at: (0, 0))],
        out_specs=[whole, whole],
        out_shape=[jax.ShapeDtypeStruct((ROWS, D), jnp.float32)] * 2,
        scratch_shapes=[
            pltpu.VMEM((count, D), jnp.bfloat16),
            pltpu.VMEM((count, 2 * HALF), jnp.float32),
            pltpu.VMEM((count, 2 * HALF), jnp.float32),
            pltpu.VMEM((2 * HALF, count), jnp.bfloat16),
            pltpu.VMEM((2 * HALF, BLOCK), jnp.bfloat16),
            pltpu.VMEM((2 * HALF, BLOCK), jnp.bfloat16),
        ],
        compiler_params=params_of(36),
        cost_estimate=NO_COST,
        name="gate_grads",
    )(*parts, mine, theirs, mine, theirs, hidden)


def updated_kernel(factor, which, kept_weight, numerator, grad, *refs):
    two_top, two_rest, one_top, one_rest, other = refs[:5]
    kept_ref, new_ref, weight_ref, part, sems = refs[5:]
    received = (
        (two_top, two_rest),
        (one_top, one_rest),
        (other.at[:CUT, :], other.at[CUT:, :]),
    )
    at = pl.program_id(0)
    blocks = D // BLOCK

    def copies(sources, block):
        columns = pl.ds(block * BLOCK, BLOCK)
        targets = (part.at[:CUT, columns], part.at[CUT:, columns])
        return [
            pltpu.make_async_copy(source.at[:, columns], target, sems.at[half, block])
            for half, (source, target) in enumerate(zip(sources, targets))
        ]

    @pl.when(at == 0)
    def _():
        for place, sources in enumerate(received):

            @pl.when(which[0] == place)
            def _():
                for block in range(blocks):
                    for copy in copies(sources, block):
                        copy.start()

    kept = 0.5 * (numerator[...] - factor[0] * grad[...])
    kept_ref[...] = kept
    for block in range(blocks):

        @pl.when(at == block)
        def _():
            for copy in copies(received[0], block):
                copy.wait()
            new_ref[...] = kept + part[:ROWS, block * BLOCK : (block + 1) * BLOCK]

    @pl.when(at == 0)
    def _():
        weight_ref[0] = kept_weight[0] + jnp.max(part[ROWS:, :128])


def updated(numerator, grad, kept_weight, factor, which, two_before, one_before, other):
    own = pl.BlockSpec((ROWS, BLOCK), lambda at: (0, at))
    scalar = pl.BlockSpec(memory_space=pltpu.SMEM)
    anywhere = pl.BlockSpec(memory_space=pl.ANY)
    blocks = D // BLOCK
    return pl.pallas_call(
        updated_kernel,
        grid=(blocks,),
        in_specs=[scalar, scalar, scalar, own, own] + [anywhere] * 5,
        out_specs=[own, own, scalar],
        out_shape=[
            jax.ShapeDtypeStruct((ROWS, D), jnp.float32),
            jax.ShapeDtypeStruct((ROWS, D), jnp.float32),
            jax.ShapeDtypeStruct((1,), jnp.float32),
        ],
        scratch_shapes=[
            pltpu.VMEM(other.shape, jnp.float32),
            pltpu.SemaphoreType.DMA((2, blocks)),
        ],
        compiler_params=params_of(16),
        name="updated",
    )(
        jnp.reshape(factor, (1,)), jnp.reshape(which, (1,)), kept_weight,
        numerator, grad, *two_before, *one_before, other,
    )


def crossed(value):
    pairs = [
        (2 * (1 - x_hi) + core, 2 * core + x_hi) for core in range(2) for x_hi in range(2)
    ]
    return lax.ppermute(value, ("core", "x_hi"), pairs)


def shards(
    tokens, cotangent, gate_num, push_weight, stale_num, stale_weight, up_weight, down_weight, step
):
    rate = plan_rate(step)
    numerator = gate_num[0]

    params = (numerator / push_weight[0]).astype(jnp.bfloat16)
    weights = jnp.concatenate([params, up_weight, down_weight], axis=0)
    rows_in, rows_grad = transposed(tokens[0]), transposed(cotangent[0])
    rows_in = held(rows_in, rows_grad, weights)
    near = [rows_in] + [shifted(rows_in, "y", steps) for steps in (1, 3, 2)]
    ring = {0: rows_grad, 1: shifted(rows_grad, "z", 1), 7: shifted(rows_grad, "z", 7)}
    mine = transposed(held(weights, rows_grad))
    ring[2], ring[6] = shifted(ring[1], "z", 1), shifted(ring[7], "z", 7)
    ring[2], ring[6] = held((ring[2], ring[6]), *near[1:])
    ring[3], ring[5] = shifted(ring[2], "z", 1), shifted(ring[6], "z", 7)
    ring[4] = shifted(ring[2], "z", 2)
    near[3] = held(near[3], ring[3], ring[4], ring[5])
    blocks = {0: stacked(near)}
    for steps in (1, 7):
        blocks[steps] = shifted(blocks[0], "z", steps)
    column = stacked([ring[steps] for steps in range(8)])

    following, before = shifted(column, "y", 1), shifted(column, "y", 3)
    blocks[1], blocks[7] = held((blocks[1], blocks[7]), column)
    blocks[2], blocks[6] = shifted(blocks[1], "z", 1), shifted(blocks[7], "z", 7)
    mine = held(mine, blocks[1], blocks[7])
    theirs = shifted(mine, "core", 1)
    stale = jnp.concatenate([stale_num[0], jnp.broadcast_to(stale_weight, (8, D))], axis=0)
    blocks[2], blocks[6] = held((blocks[2], blocks[6]), theirs)
    two_before = [shifted(held(stale[:CUT], theirs), "x_lo", 1)]
    two_before.append(shifted(held(stale[CUT:], two_before[0]), "x_lo", 1))
    blocks[3], blocks[5] = shifted(blocks[2], "z", 1), shifted(blocks[6], "z", 7)
    following, before = held((following, before), blocks[2], blocks[6])
    half = column.shape[0] // 2
    far = [shifted(following[:half], "y", 1), shifted(before[half:], "y", 3)]
    blocks[3], blocks[5] = held((blocks[3], blocks[5]), following, before, two_before[0])
    cut = 48
    last = [shifted(blocks[3][:cut], "z", 1), shifted(blocks[5][cut:], "z", 7)]

    hidden = hidden_of([column, following, before, *far], mine, theirs)
    parts = [blocks[steps] for steps in (0, 1, 2, 3)] + last + [blocks[steps] for steps in (5, 6, 7)]
    hidden = held(hidden, two_before[1])
    own_grad, other_grad = gate_grads(parts, mine, theirs, hidden)
    two_before = held(tuple(two_before), own_grad)
    one_before = [shifted(part, "core", 1) for part in two_before]
    stale_hop = shifted(held(stale, own_grad), "core", 1)
    gate_grad = own_grad + shifted(other_grad, "core", 1)
    norm_sq = jnp.sum(gate_grad * gate_grad)
    gate_grad = transposed(gate_grad)
    for axes in ("z", "y"):
        norm_sq = lax.psum(norm_sq, axes)
    norm_sq = held(jnp.reshape(norm_sq, (1,)), *one_before, stale_hop)[0]
    norm_sq = transposed(norm_sq) + crossed(norm_sq)

    clip_factor = jnp.minimum(1.0, MAX_NORM / jnp.sqrt(norm_sq + eps))
    kept_weight = 0.5 * push_weight
    which = jnp.where(step[0] % 2 == 1, 0, 1 + lax.axis_index("core"))
    kept_half, new_num, new_weight = updated(
        numerator, gate_grad, kept_weight, rate * clip_factor, which, two_before, one_before, stale_hop
    )
    return (new_num[None], new_weight, kept_half[None], kept_weight)


def solution(mesh):
    named = Mesh(np.asarray(mesh.devices).reshape(tuple(SIZES.values())), tuple(SIZES))
    groups = P(GOSSIP, FSDP, None)
    in_specs = (
        groups,
        groups,
        groups,
        P(GOSSIP),
        groups,
        P(GOSSIP),
        P(FSDP, None),
        P(FSDP, None),
        P(),
    )
    out_specs = (groups, P(GOSSIP), groups, P(GOSSIP))
    return jax.shard_map(shards, mesh=named, in_specs=in_specs, out_specs=out_specs, check_vma=False)
```

```python
import math

import jax
import jax.numpy as jnp
import numpy as np
from jax import lax
from jax.experimental import pallas as pl
from jax.experimental.pallas import tpu as pltpu
from jax.sharding import Mesh, PartitionSpec as P

D = 5120
FFW = 7168

eps = 1e-06

WIDTH_SCALE = D ** (-0.5)
MAX_NORM = 0.05 * math.sqrt(D * FFW)

SIZES = {"x_lo": 2, "core": 2, "z": 8, "x_hi": 2, "y": 4}
GOSSIP = ("x_lo", "core")
FSDP = ("z", "x_hi", "y")

ROWS = 112
HALF = 128
CUT = 64
NO_COST = pl.CostEstimate(flops=1, bytes_accessed=1, transcendentals=0)
MUCH_COST = pl.CostEstimate(flops=3 * 10**10, bytes_accessed=1, transcendentals=0)
BLOCK = 1024


def shifted(value, axis, steps):
    count = SIZES[axis]
    pairs = [((place + steps) % count, place) for place in range(count)]
    return lax.ppermute(value, axis, pairs)


def transposed(value, stay=True):
    pairs = [
        (2 * x_hi + core, 2 * core + x_hi)
        for core in range(2)
        for x_hi in range(2)
        if stay or core != x_hi
    ]
    return lax.ppermute(value, ("core", "x_hi"), pairs)


def held(value, *ready):
    values = value if isinstance(value, tuple) else (value,)
    anywhere = pl.BlockSpec(memory_space=pl.ANY)
    out = pl.pallas_call(
        lambda *refs: None,
        in_specs=[anywhere] * (len(values) + len(ready)),
        out_specs=[anywhere] * len(values),
        out_shape=[jax.ShapeDtypeStruct(one.shape, one.dtype) for one in values],
        input_output_aliases={at: at for at in range(len(values))},
        compiler_params=params_of(1),
        name="held",
    )(*values, *ready)
    return tuple(out) if isinstance(value, tuple) else out[0]


def silu_slope(preact):
    sigmoid_val = jax.nn.sigmoid(preact)
    return sigmoid_val * (1.0 + preact * (1.0 - sigmoid_val))


def plan_rate(step):
    phase = (step[0] % 1000).astype(jnp.float32) / 1000.0
    return 0.4 + 1.8 * (1.0 + jnp.cos(math.pi * phase))


def dot_t(rows, weights):
    return lax.dot_general(
        rows, weights, (((1,), (1,)), ((), ())), preferred_element_type=jnp.float32
    )


def params_of(vmem, **more):
    return pltpu.CompilerParams(vmem_limit_bytes=vmem * 2**20, **more)


def stack_kernel(*refs):
    *blocks, out_ref = refs
    for at, block in enumerate(blocks):
        count = block.shape[0]
        out_ref[at * count : (at + 1) * count, :] = block[...]


def stacked(blocks):
    count = blocks[0].shape[0]
    wide = D // 4
    return pl.pallas_call(
        stack_kernel,
        grid=(4,),
        in_specs=[pl.BlockSpec((count, wide), lambda at: (0, at))] * len(blocks),
        out_specs=pl.BlockSpec((count * len(blocks), wide), lambda at: (0, at)),
        out_shape=jax.ShapeDtypeStruct((count * len(blocks), D), blocks[0].dtype),
        compiler_params=params_of(8),
        name="stacked",
    )(*blocks)


def widen(wide, mine, theirs):
    wide[:ROWS, :] = mine[...]
    wide[HALF : HALF + ROWS, :] = theirs[...]


def clear(wide):
    pad = jnp.zeros((HALF - ROWS, wide.shape[1]), wide.dtype)
    wide[ROWS:HALF, :] = pad
    wide[HALF + ROWS :, :] = pad


def hidden_kernel(*refs):
    *parts, mine, theirs, out_ref, total, wide = refs
    at = pl.program_id(0)

    @pl.when(at == 0)
    def _():
        total[...] = jnp.zeros_like(total)
        clear(wide)

    widen(wide, mine, theirs)
    row = 0
    for part in parts:
        count = part.shape[0]
        total[row : row + count, :] += dot_t(part[...], wide[...])
        row += count

    @pl.when(at == pl.num_programs(0) - 1)
    def _():
        column, block = row // 4, row // 32
        for dz in range(8):
            for dy in range(4):
                start, place = dy * column + dz * block, (4 * dz + dy) * block
                out_ref[place : place + block, :] = total[start : start + block, :]


def hidden_of(parts, mine, theirs):
    count = sum(part.shape[0] for part in parts)
    weights = pl.BlockSpec((ROWS, BLOCK), lambda at: (2, at))
    return pl.pallas_call(
        hidden_kernel,
        grid=(D // BLOCK,),
        in_specs=[pl.BlockSpec((part.shape[0], BLOCK), lambda at: (0, at)) for part in parts]
        + [weights, weights],
        out_specs=pl.BlockSpec((count, 2 * HALF), lambda at: (0, 0)),
        out_shape=jax.ShapeDtypeStruct((count, 2 * HALF), jnp.float32),
        scratch_shapes=[
            pltpu.VMEM((count, 2 * HALF), jnp.float32),
            pltpu.VMEM((2 * HALF, BLOCK), jnp.bfloat16),
        ],
        compiler_params=params_of(16),
        cost_estimate=MUCH_COST,
        name="hidden",
    )(*parts, mine, theirs)


def grad_kernel(*refs):
    *parts, my_params, their_params, my_up, their_up, hidden_ref, own_ref, other_ref = refs[:-6]
    rows, preact, up_proj, turned, wide_params, wide_up = refs[-6:]
    at = pl.program_id(0)

    @pl.when(at == 0)
    def _():
        preact[...] = jnp.zeros_like(preact)
        up_proj[...] = jnp.zeros_like(up_proj)
        clear(wide_params)
        clear(wide_up)

    columns = pl.ds(pl.multiple_of(at * BLOCK, BLOCK), BLOCK)
    row = 0
    for part in parts:
        count = part.shape[0]
        rows[row : row + count, columns] = part[...]
        row += count
    widen(wide_params, my_params, their_params)
    widen(wide_up, my_up, their_up)
    preact[...] += dot_t(rows[:, columns], wide_params[...])
    up_proj[...] += dot_t(rows[:, columns], wide_up[...])

    @pl.when(at == pl.num_programs(0) - 1)
    def _():
        slope = silu_slope(preact[...] * WIDTH_SCALE)
        turned[...] = (hidden_ref[...] * up_proj[...] * slope).T.astype(jnp.bfloat16)

        @pl.loop(0, D // BLOCK)
        def _(block):
            columns = pl.ds(pl.multiple_of(block * BLOCK, BLOCK), BLOCK)
            grad = jnp.dot(turned[...], rows[:, columns], preferred_element_type=jnp.float32)
            own_ref[:, columns] = grad[:ROWS] * WIDTH_SCALE
            other_ref[:, columns] = grad[HALF : HALF + ROWS] * WIDTH_SCALE


def gate_grads(parts, mine, theirs, hidden):
    count = sum(part.shape[0] for part in parts)

    def weights(which):
        return pl.BlockSpec((ROWS, BLOCK), lambda at: (which, at))

    whole = pl.BlockSpec((ROWS, D), lambda at: (0, 0))
    return pl.pallas_call(
        grad_kernel,
        grid=(D // BLOCK,),
        in_specs=[pl.BlockSpec((part.shape[0], BLOCK), lambda at: (0, at)) for part in parts]
        + [weights(0), weights(0), weights(1), weights(1)]
        + [pl.BlockSpec((count, 2 * HALF), lambda at: (0, 0))],
        out_specs=[whole, whole],
        out_shape=[jax.ShapeDtypeStruct((ROWS, D), jnp.float32)] * 2,
        scratch_shapes=[
            pltpu.VMEM((count, D), jnp.bfloat16),
            pltpu.VMEM((count, 2 * HALF), jnp.float32),
            pltpu.VMEM((count, 2 * HALF), jnp.float32),
            pltpu.VMEM((2 * HALF, count), jnp.bfloat16),
            pltpu.VMEM((2 * HALF, BLOCK), jnp.bfloat16),
            pltpu.VMEM((2 * HALF, BLOCK), jnp.bfloat16),
        ],
        compiler_params=params_of(36),
        cost_estimate=NO_COST,
        name="gate_grads",
    )(*parts, mine, theirs, mine, theirs, hidden)


def updated_kernel(factor, kept_weight, which, numerator, *refs):
    two_top, two_rest, one_top, one_rest, hop, stayed, returned = refs[:7]
    kept_ref, new_ref, weight_ref, part, grad, sems, grad_sems = refs[7:]
    received = (
        (two_top, two_rest),
        (one_top, one_rest),
        (hop.at[:CUT, :], hop.at[CUT:, :]),
    )
    at = pl.program_id(0)
    blocks = D // BLOCK

    def copies(sources, source, block):
        columns = pl.ds(block * BLOCK, BLOCK)
        targets = (part.at[:CUT, columns], part.at[CUT:, columns])
        parts = [
            pltpu.make_async_copy(one.at[:, columns], target, sems.at[half, block])
            for half, (one, target) in enumerate(zip(sources, targets))
        ]
        whole = pltpu.make_async_copy(
            source.at[:, columns], grad.at[:, columns], grad_sems.at[block]
        )
        return parts, whole

    @pl.when(at == 0)
    def _():
        for block in range(blocks):
            for place, sources in enumerate(received):

                @pl.when(which[0] == place)
                def _():
                    for copy in copies(sources, stayed, block)[0]:
                        copy.start()

            for place, source in enumerate((stayed, returned)):

                @pl.when(which[1] == place)
                def _():
                    copies(received[0], source, block)[1].start()

    for block in range(blocks):

        @pl.when(at == block)
        def _():
            parts, whole = copies(received[0], stayed, block)
            for copy in (*parts, whole):
                copy.wait()
            columns = slice(block * BLOCK, (block + 1) * BLOCK)
            kept = 0.5 * (numerator[...] - factor[0] * grad[:, columns])
            kept_ref[...] = kept
            new_ref[...] = kept + part[:ROWS, columns]

    @pl.when(at == 0)
    def _():
        weight_ref[0] = kept_weight[0] + jnp.max(part[ROWS:, :128])


def updated(numerator, factor, kept_weight, which, received, grads):
    own = pl.BlockSpec((ROWS, BLOCK), lambda at: (0, at))
    scalar = pl.BlockSpec(memory_space=pltpu.SMEM)
    anywhere = pl.BlockSpec(memory_space=pl.ANY)
    more = [part for parts in received for part in parts] + grads
    blocks = D // BLOCK
    return pl.pallas_call(
        updated_kernel,
        grid=(blocks,),
        in_specs=[scalar, scalar, scalar, own] + [anywhere] * len(more),
        out_specs=[own, own, scalar],
        out_shape=[
            jax.ShapeDtypeStruct((ROWS, D), jnp.float32),
            jax.ShapeDtypeStruct((ROWS, D), jnp.float32),
            jax.ShapeDtypeStruct((1,), jnp.float32),
        ],
        scratch_shapes=[
            pltpu.VMEM((ROWS + 8, D), jnp.float32),
            pltpu.VMEM((ROWS, D), jnp.float32),
            pltpu.SemaphoreType.DMA((2, blocks)),
            pltpu.SemaphoreType.DMA((blocks,)),
        ],
        compiler_params=params_of(16),
        name="updated",
    )(factor, kept_weight, which, numerator, *more)


def shards(
    tokens, cotangent, gate_num, push_weight, stale_num, stale_weight, up_weight, down_weight, step
):
    rate = plan_rate(step)
    numerator = gate_num[0]

    params = (numerator / push_weight[0]).astype(jnp.bfloat16)
    weights = jnp.concatenate([params, up_weight, down_weight], axis=0)
    rows_in, rows_grad = transposed(tokens[0]), transposed(cotangent[0])
    rows_in = held(rows_in, rows_grad, weights)
    near = [rows_in] + [shifted(rows_in, "y", steps) for steps in (1, 3, 2)]
    ring = {0: rows_grad, 1: shifted(rows_grad, "z", 1), 7: shifted(rows_grad, "z", 7)}
    mine = transposed(held(weights, rows_grad))
    ring[2], ring[6] = shifted(ring[1], "z", 1), shifted(ring[7], "z", 7)
    ring[2], ring[6] = held((ring[2], ring[6]), *near[1:])
    ring[3], ring[5] = shifted(ring[2], "z", 1), shifted(ring[6], "z", 7)
    ring[4] = shifted(ring[2], "z", 2)
    near[3] = held(near[3], ring[3], ring[4], ring[5])
    blocks = {0: stacked(near)}
    columns = [stacked([ring[steps] for steps in some]) for some in (range(4), range(4, 8))]

    blocks[1], blocks[7] = shifted(blocks[0], "z", 1), shifted(blocks[0], "z", 7)
    following, before = [shifted(columns[0], "y", 1)], [shifted(columns[0], "y", 3)]
    blocks[1], blocks[7] = held((blocks[1], blocks[7]), columns[1], following[0], before[0])

    blocks[2], blocks[6] = shifted(blocks[1], "z", 1), shifted(blocks[7], "z", 7)
    columns[1] = held(columns[1], blocks[1], blocks[7])
    following.append(shifted(columns[1], "y", 1))
    before.append(shifted(columns[1], "y", 3))
    mine = held(mine, blocks[1], blocks[7])
    theirs = shifted(mine, "core", 1)
    blocks[2], blocks[6] = held((blocks[2], blocks[6]), theirs, following[1], before[1])

    blocks[3], blocks[5] = shifted(blocks[2], "z", 1), shifted(blocks[6], "z", 7)
    following[0] = held(following[0], blocks[2])
    far = [shifted(following[0], "y", 1), shifted(before[1], "y", 3)]
    stale = jnp.concatenate([stale_num[0], jnp.broadcast_to(stale_weight, (8, D))], axis=0)
    two_before = [shifted(held(stale[:CUT], theirs), "x_lo", 1)]
    blocks[3], blocks[5] = held((blocks[3], blocks[5]), two_before[0], *far)

    cut = 48
    last = [shifted(blocks[3][:cut], "z", 1), shifted(blocks[5][cut:], "z", 7)]
    two_before.append(shifted(held(stale[CUT:], two_before[0]), "x_lo", 1))
    hidden = hidden_of([*columns, *following, *before, *far], mine, theirs)
    hidden = held(hidden, two_before[1])
    parts = [blocks[steps] for steps in (0, 1, 2, 3)] + last + [blocks[steps] for steps in (5, 6, 7)]

    own_grad, other_grad = gate_grads(parts, mine, theirs, hidden)
    two_before = held(tuple(two_before), own_grad)
    one_before = [shifted(part, "core", 1) for part in two_before]
    stale_hop = shifted(held(stale, own_grad), "core", 1)
    gate_grad = own_grad + shifted(other_grad, "core", 1)
    norm_sq = jnp.sum(gate_grad * gate_grad)
    returned = transposed(gate_grad, stay=False)
    for axes in ("z", "y"):
        norm_sq = lax.psum(norm_sq, axes)
    x_hi, core = lax.axis_index("x_hi"), lax.axis_index("core")
    norms = lax.psum(jnp.where(jnp.arange(2) == x_hi, norm_sq, 0.0), ("core", "x_hi"))
    norm_sq = jnp.where(core == 0, norms[0], norms[1])

    clip_factor = jnp.minimum(1.0, MAX_NORM / jnp.sqrt(norm_sq + eps))
    kept_weight = 0.5 * push_weight
    which = jnp.where(step[0] % 2 == 1, 0, 1 + core)
    kept_half, new_num, new_weight = updated(
        numerator,
        jnp.reshape(rate * clip_factor, (1,)),
        kept_weight,
        jnp.stack([which, jnp.where(core == x_hi, 0, 1)]),
        [two_before, one_before, [stale_hop]],
        [gate_grad, returned],
    )
    return (new_num[None], new_weight, kept_half[None], kept_weight)


def solution(mesh):
    named = Mesh(np.asarray(mesh.devices).reshape(tuple(SIZES.values())), tuple(SIZES))
    groups = P(GOSSIP, FSDP, None)
    in_specs = (
        groups,
        groups,
        groups,
        P(GOSSIP),
        groups,
        P(GOSSIP),
        P(FSDP, None),
        P(FSDP, None),
        P(),
    )
    out_specs = (groups, P(GOSSIP), groups, P(GOSSIP))
    return jax.shard_map(shards, mesh=named, in_specs=in_specs, out_specs=out_specs, check_vma=False)
```

```python
import math

import jax
import jax.numpy as jnp
import numpy as np
from jax import lax
from jax.experimental import pallas as pl
from jax.experimental.pallas import tpu as pltpu
from jax.sharding import Mesh, PartitionSpec as P

D = 5120
FFW = 7168

eps = 1e-06

WIDTH_SCALE = D ** (-0.5)
MAX_NORM = 0.05 * math.sqrt(D * FFW)

SIZES = {"x_lo": 2, "core": 2, "z": 8, "x_hi": 2, "y": 4}
GOSSIP = ("x_lo", "core")
FSDP = ("z", "x_hi", "y")

ROWS = 112
HALF = 128
CUT = 64
NO_COST = pl.CostEstimate(flops=1, bytes_accessed=1, transcendentals=0)
BLOCK = 1024


def shifted(value, axis, steps):
    count = SIZES[axis]
    pairs = [((place + steps) % count, place) for place in range(count)]
    return lax.ppermute(value, axis, pairs)


def transposed(value, stay=True):
    pairs = [
        (2 * x_hi + core, 2 * core + x_hi)
        for core in range(2)
        for x_hi in range(2)
        if stay or core != x_hi
    ]
    return lax.ppermute(value, ("core", "x_hi"), pairs)


def held(value, *ready):
    values = value if isinstance(value, tuple) else (value,)
    anywhere = pl.BlockSpec(memory_space=pl.ANY)
    out = pl.pallas_call(
        lambda *refs: None,
        in_specs=[anywhere] * (len(values) + len(ready)),
        out_specs=[anywhere] * len(values),
        out_shape=[jax.ShapeDtypeStruct(one.shape, one.dtype) for one in values],
        input_output_aliases={at: at for at in range(len(values))},
        compiler_params=params_of(1),
        name="held",
    )(*values, *ready)
    return tuple(out) if isinstance(value, tuple) else out[0]


def silu_slope(preact):
    sigmoid_val = jax.nn.sigmoid(preact)
    return sigmoid_val * (1.0 + preact * (1.0 - sigmoid_val))


def plan_rate(step):
    phase = (step[0] % 1000).astype(jnp.float32) / 1000.0
    return 0.4 + 1.8 * (1.0 + jnp.cos(math.pi * phase))


def dot_t(rows, weights):
    return lax.dot_general(
        rows, weights, (((1,), (1,)), ((), ())), preferred_element_type=jnp.float32
    )


def params_of(vmem, **more):
    return pltpu.CompilerParams(vmem_limit_bytes=vmem * 2**20, **more)


def stack_kernel(*refs):
    *blocks, out_ref = refs
    for at, block in enumerate(blocks):
        count = block.shape[0]
        out_ref[at * count : (at + 1) * count, :] = block[...]


def stacked(blocks):
    count = blocks[0].shape[0]
    wide = D // 4
    return pl.pallas_call(
        stack_kernel,
        grid=(4,),
        in_specs=[pl.BlockSpec((count, wide), lambda at: (0, at))] * len(blocks),
        out_specs=pl.BlockSpec((count * len(blocks), wide), lambda at: (0, at)),
        out_shape=jax.ShapeDtypeStruct((count * len(blocks), D), blocks[0].dtype),
        compiler_params=params_of(8),
        name="stacked",
    )(*blocks)


def widen(wide, mine, theirs):
    wide[:ROWS, :] = mine[...]
    wide[HALF : HALF + ROWS, :] = theirs[...]


def clear(wide):
    pad = jnp.zeros((HALF - ROWS, wide.shape[1]), wide.dtype)
    wide[ROWS:HALF, :] = pad
    wide[HALF + ROWS :, :] = pad


def hidden_kernel(*refs):
    *parts, mine, theirs, out_ref, total, wide = refs
    at = pl.program_id(0)

    @pl.when(at == 0)
    def _():
        total[...] = jnp.zeros_like(total)
        clear(wide)

    widen(wide, mine, theirs)
    row = 0
    for part in parts:
        count = part.shape[0]
        total[row : row + count, :] += dot_t(part[...], wide[...])
        row += count

    @pl.when(at == pl.num_programs(0) - 1)
    def _():
        out_ref[...] = total[...]


def hidden_of(parts, mine, theirs):
    count = sum(part.shape[0] for part in parts)
    weights = pl.BlockSpec((ROWS, BLOCK), lambda at: (2, at))
    return pl.pallas_call(
        hidden_kernel,
        grid=(D // BLOCK,),
        in_specs=[pl.BlockSpec((part.shape[0], BLOCK), lambda at: (0, at)) for part in parts]
        + [weights, weights],
        out_specs=pl.BlockSpec((count, 2 * HALF), lambda at: (0, 0)),
        out_shape=jax.ShapeDtypeStruct((count, 2 * HALF), jnp.float32),
        scratch_shapes=[
            pltpu.VMEM((count, 2 * HALF), jnp.float32),
            pltpu.VMEM((2 * HALF, BLOCK), jnp.bfloat16),
        ],
        compiler_params=params_of(16),
        cost_estimate=NO_COST,
        name="hidden",
    )(*parts, mine, theirs)


def grad_kernel(*refs):
    *parts, my_params, their_params, my_up, their_up, most_ref, far_ref = refs[:-9]
    own_ref, other_ref, rows, preact, up_proj, hidden, turned, wide_params, wide_up = refs[-9:]
    at = pl.program_id(0)

    @pl.when(at == 0)
    def _():
        preact[...] = jnp.zeros_like(preact)
        up_proj[...] = jnp.zeros_like(up_proj)
        clear(wide_params)
        clear(wide_up)
        column, block = hidden.shape[0] // 4, hidden.shape[0] // 32
        for dz in range(8):
            for dy in range(4):
                place, start = (4 * dz + dy) * block, dz * block
                if dy < 3:
                    start += dy * column
                source = most_ref if dy < 3 else far_ref
                hidden[place : place + block, :] = source[start : start + block, :]

    columns = pl.ds(pl.multiple_of(at * BLOCK, BLOCK), BLOCK)
    row = 0
    for part in parts:
        count = part.shape[0]
        rows[row : row + count, columns] = part[...]
        row += count
    widen(wide_params, my_params, their_params)
    widen(wide_up, my_up, their_up)
    preact[...] += dot_t(rows[:, columns], wide_params[...])
    up_proj[...] += dot_t(rows[:, columns], wide_up[...])

    @pl.when(at == pl.num_programs(0) - 1)
    def _():
        slope = silu_slope(preact[...] * WIDTH_SCALE)
        turned[...] = (hidden[...] * up_proj[...] * slope).T.astype(jnp.bfloat16)

        @pl.loop(0, D // BLOCK)
        def _(block):
            columns = pl.ds(pl.multiple_of(block * BLOCK, BLOCK), BLOCK)
            grad = jnp.dot(turned[...], rows[:, columns], preferred_element_type=jnp.float32)
            own_ref[:, columns] = grad[:ROWS] * WIDTH_SCALE
            other_ref[:, columns] = grad[HALF : HALF + ROWS] * WIDTH_SCALE


def gate_grads(parts, mine, theirs, hidden_most, hidden_far):
    count = sum(part.shape[0] for part in parts)

    def weights(which):
        return pl.BlockSpec((ROWS, BLOCK), lambda at: (which, at))

    whole = pl.BlockSpec((ROWS, D), lambda at: (0, 0))
    return pl.pallas_call(
        grad_kernel,
        grid=(D // BLOCK,),
        in_specs=[pl.BlockSpec((part.shape[0], BLOCK), lambda at: (0, at)) for part in parts]
        + [weights(0), weights(0), weights(1), weights(1)]
        + [pl.BlockSpec(one.shape, lambda at: (0, 0)) for one in (hidden_most, hidden_far)],
        out_specs=[whole, whole],
        out_shape=[jax.ShapeDtypeStruct((ROWS, D), jnp.float32)] * 2,
        scratch_shapes=[
            pltpu.VMEM((count, D), jnp.bfloat16),
            pltpu.VMEM((count, 2 * HALF), jnp.float32),
            pltpu.VMEM((count, 2 * HALF), jnp.float32),
            pltpu.VMEM((count, 2 * HALF), jnp.float32),
            pltpu.VMEM((2 * HALF, count), jnp.bfloat16),
            pltpu.VMEM((2 * HALF, BLOCK), jnp.bfloat16),
            pltpu.VMEM((2 * HALF, BLOCK), jnp.bfloat16),
        ],
        compiler_params=params_of(36),
        cost_estimate=NO_COST,
        name="gate_grads",
    )(*parts, mine, theirs, mine, theirs, hidden_most, hidden_far)


def updated_kernel(factor, kept_weight, which, numerator, *refs):
    two_top, two_rest, one_top, one_rest, hop, stayed, returned = refs[:7]
    kept_ref, new_ref, weight_ref, part, grad, sems, grad_sems = refs[7:]
    received = (
        (two_top, two_rest),
        (one_top, one_rest),
        (hop.at[:CUT, :], hop.at[CUT:, :]),
    )
    at = pl.program_id(0)
    blocks = D // BLOCK

    def copies(sources, source, block):
        columns = pl.ds(block * BLOCK, BLOCK)
        targets = (part.at[:CUT, columns], part.at[CUT:, columns])
        parts = [
            pltpu.make_async_copy(one.at[:, columns], target, sems.at[half, block])
            for half, (one, target) in enumerate(zip(sources, targets))
        ]
        whole = pltpu.make_async_copy(
            source.at[:, columns], grad.at[:, columns], grad_sems.at[block]
        )
        return parts, whole

    @pl.when(at == 0)
    def _():
        for block in range(blocks):
            for place, sources in enumerate(received):

                @pl.when(which[0] == place)
                def _():
                    for copy in copies(sources, stayed, block)[0]:
                        copy.start()

            for place, source in enumerate((stayed, returned)):

                @pl.when(which[1] == place)
                def _():
                    copies(received[0], source, block)[1].start()

    for block in range(blocks):

        @pl.when(at == block)
        def _():
            parts, whole = copies(received[0], stayed, block)
            for copy in (*parts, whole):
                copy.wait()
            columns = slice(block * BLOCK, (block + 1) * BLOCK)
            kept = 0.5 * (numerator[...] - factor[0] * grad[:, columns])
            kept_ref[...] = kept
            new_ref[...] = kept + part[:ROWS, columns]

    @pl.when(at == 0)
    def _():
        weight_ref[0] = kept_weight[0] + jnp.max(part[ROWS:, :128])


def updated(numerator, factor, kept_weight, which, received, grads):
    own = pl.BlockSpec((ROWS, BLOCK), lambda at: (0, at))
    scalar = pl.BlockSpec(memory_space=pltpu.SMEM)
    anywhere = pl.BlockSpec(memory_space=pl.ANY)
    more = [part for parts in received for part in parts] + grads
    blocks = D // BLOCK
    return pl.pallas_call(
        updated_kernel,
        grid=(blocks,),
        in_specs=[scalar, scalar, scalar, own] + [anywhere] * len(more),
        out_specs=[own, own, scalar],
        out_shape=[
            jax.ShapeDtypeStruct((ROWS, D), jnp.float32),
            jax.ShapeDtypeStruct((ROWS, D), jnp.float32),
            jax.ShapeDtypeStruct((1,), jnp.float32),
        ],
        scratch_shapes=[
            pltpu.VMEM((ROWS + 8, D), jnp.float32),
            pltpu.VMEM((ROWS, D), jnp.float32),
            pltpu.SemaphoreType.DMA((2, blocks)),
            pltpu.SemaphoreType.DMA((blocks,)),
        ],
        compiler_params=params_of(56),
        name="updated",
    )(factor, kept_weight, which, numerator, *more)


def shards(
    tokens, cotangent, gate_num, push_weight, stale_num, stale_weight, up_weight, down_weight, step
):
    rate = plan_rate(step)
    numerator = gate_num[0]

    params = (numerator / push_weight[0]).astype(jnp.bfloat16)
    weights = jnp.concatenate([params, up_weight, down_weight], axis=0)
    rows_in, rows_grad = transposed(tokens[0]), transposed(cotangent[0])
    rows_in = held(rows_in, rows_grad, weights)
    near = [rows_in] + [shifted(rows_in, "y", steps) for steps in (1, 3, 2)]
    ring = {0: rows_grad, 1: shifted(rows_grad, "z", 1), 7: shifted(rows_grad, "z", 7)}
    mine = transposed(held(weights, ring[1], ring[7]))
    ring[2], ring[6] = shifted(ring[1], "z", 1), shifted(ring[7], "z", 7)
    ring[2], ring[6] = held((ring[2], ring[6]), *near[1:])
    ring[3], ring[5] = shifted(ring[2], "z", 1), shifted(ring[6], "z", 7)
    ring[4] = shifted(ring[2], "z", 2)
    near[3] = held(near[3], ring[3], ring[4], ring[5])
    blocks = {0: stacked(near)}
    columns = [stacked([ring[steps] for steps in some]) for some in (range(4), range(4, 8))]

    blocks[1], blocks[7] = shifted(blocks[0], "z", 1), shifted(blocks[0], "z", 7)
    following, before = [shifted(columns[0], "y", 1)], [shifted(columns[0], "y", 3)]
    ready = (columns[1], following[0], before[0], mine)
    blocks[1], blocks[7] = held((blocks[1], blocks[7]), *ready)

    blocks[2], blocks[6] = shifted(blocks[1], "z", 1), shifted(blocks[7], "z", 7)
    columns[1] = held(columns[1], blocks[1], blocks[7])
    following.append(shifted(columns[1], "y", 1))
    before.append(shifted(columns[1], "y", 3))
    stale = jnp.concatenate([stale_num[0], jnp.broadcast_to(stale_weight, (8, D))], axis=0)
    two_before = [shifted(held(stale[:CUT], mine), "x_lo", 1)]
    ready = (two_before[0], following[1], before[1])
    blocks[2], blocks[6] = held((blocks[2], blocks[6]), *ready)

    blocks[3], blocks[5] = shifted(blocks[2], "z", 1), shifted(blocks[6], "z", 7)
    following[0] = held(following[0], blocks[2])
    far = [shifted(following[0], "y", 1), shifted(before[1], "y", 3)]
    mine = held(mine, blocks[2], blocks[6])
    theirs = shifted(mine, "core", 1)
    two_before.append(shifted(held(stale[CUT:], two_before[0]), "x_lo", 1))
    hidden_most = hidden_of([*columns, *following, *before], mine, theirs)
    blocks[3], blocks[5] = held((blocks[3], blocks[5]), hidden_most, *far)

    cut = 48
    last = [shifted(blocks[3][:cut], "z", 1), shifted(blocks[5][cut:], "z", 7)]
    hidden_far = held(hidden_of(far, mine, theirs), two_before[1])
    parts = [blocks[steps] for steps in (0, 1, 2, 3)] + last + [blocks[steps] for steps in (5, 6, 7)]

    own_grad, other_grad = gate_grads(parts, mine, theirs, hidden_most, hidden_far)
    two_before = held(tuple(two_before), own_grad)
    one_before = [shifted(part, "core", 1) for part in two_before]
    stale_hop = shifted(held(stale, own_grad), "core", 1)
    gate_grad = own_grad + shifted(other_grad, "core", 1)
    norm_sq = jnp.sum(gate_grad * gate_grad)
    returned = transposed(gate_grad, stay=False)
    for axes in ("z", "y"):
        norm_sq = lax.psum(norm_sq, axes)
    x_hi, core = lax.axis_index("x_hi"), lax.axis_index("core")
    norms = lax.psum(jnp.where(jnp.arange(2) == x_hi, norm_sq, 0.0), ("core", "x_hi"))
    norm_sq = jnp.where(core == 0, norms[0], norms[1])

    clip_factor = jnp.minimum(1.0, MAX_NORM / jnp.sqrt(norm_sq + eps))
    kept_weight = 0.5 * push_weight
    which = jnp.where(step[0] % 2 == 1, 0, 1 + core)
    kept_half, new_num, new_weight = updated(
        numerator,
        jnp.reshape(rate * clip_factor, (1,)),
        kept_weight,
        jnp.stack([which, jnp.where(core == x_hi, 0, 1)]),
        [two_before, one_before, [stale_hop]],
        [gate_grad, returned],
    )
    return (new_num[None], new_weight, kept_half[None], kept_weight)


def solution(mesh):
    named = Mesh(np.asarray(mesh.devices).reshape(tuple(SIZES.values())), tuple(SIZES))
    groups = P(GOSSIP, FSDP, None)
    in_specs = (
        groups,
        groups,
        groups,
        P(GOSSIP),
        groups,
        P(GOSSIP),
        P(FSDP, None),
        P(FSDP, None),
        P(),
    )
    out_specs = (groups, P(GOSSIP), groups, P(GOSSIP))
    return jax.shard_map(shards, mesh=named, in_specs=in_specs, out_specs=out_specs, check_vma=False)
```

```python
import math

import jax
import jax.numpy as jnp
import numpy as np
from jax import lax
from jax.experimental import pallas as pl
from jax.experimental.pallas import tpu as pltpu
from jax.sharding import Mesh, PartitionSpec as P

D = 5120
FFW = 7168

eps = 1e-06

WIDTH_SCALE = D ** (-0.5)
MAX_NORM = 0.05 * math.sqrt(D * FFW)

SIZES = {"x_lo": 2, "core": 2, "z": 8, "x_hi": 2, "y": 4}
GOSSIP = ("x_lo", "core")
FSDP = ("z", "x_hi", "y")

ROWS = 112
HALF = 128
CUT = 64
NO_COST = pl.CostEstimate(flops=1, bytes_accessed=1, transcendentals=0)
BLOCK = 1024


def shifted(value, axis, steps):
    count = SIZES[axis]
    pairs = [((place + steps) % count, place) for place in range(count)]
    return lax.ppermute(value, axis, pairs)


def transposed(value, stay=True):
    pairs = [
        (2 * x_hi + core, 2 * core + x_hi)
        for core in range(2)
        for x_hi in range(2)
        if stay or core != x_hi
    ]
    return lax.ppermute(value, ("core", "x_hi"), pairs)


def summed(value):
    crossing = [(2 * (1 - x_hi) + core, 2 * core + x_hi) for core in range(2) for x_hi in range(2)]
    value = transposed(value) + lax.ppermute(value, ("core", "x_hi"), crossing)
    for axis in ("y", "z"):
        reach = 1
        while reach < SIZES[axis]:
            pairs = [(place ^ reach, place) for place in range(SIZES[axis])]
            value = value + lax.ppermute(value, axis, pairs)
            reach *= 2
    return value


def held(value, *ready):
    values = value if isinstance(value, tuple) else (value,)
    anywhere = pl.BlockSpec(memory_space=pl.ANY)
    out = pl.pallas_call(
        lambda *refs: None,
        in_specs=[anywhere] * (len(values) + len(ready)),
        out_specs=[anywhere] * len(values),
        out_shape=[jax.ShapeDtypeStruct(one.shape, one.dtype) for one in values],
        input_output_aliases={at: at for at in range(len(values))},
        compiler_params=params_of(1),
        name="held",
    )(*values, *ready)
    return tuple(out) if isinstance(value, tuple) else out[0]


def silu_slope(preact):
    sigmoid_val = jax.nn.sigmoid(preact)
    return sigmoid_val * (1.0 + preact * (1.0 - sigmoid_val))


def plan_rate(step):
    phase = (step[0] % 1000).astype(jnp.float32) / 1000.0
    return 0.4 + 1.8 * (1.0 + jnp.cos(math.pi * phase))


def dot_t(rows, weights):
    return lax.dot_general(
        rows, weights, (((1,), (1,)), ((), ())), preferred_element_type=jnp.float32
    )


def params_of(vmem, **more):
    return pltpu.CompilerParams(vmem_limit_bytes=vmem * 2**20, **more)


def stack_kernel(*refs):
    *blocks, out_ref = refs
    for at, block in enumerate(blocks):
        count = block.shape[0]
        out_ref[at * count : (at + 1) * count, :] = block[...]


def stacked(blocks):
    count = blocks[0].shape[0]
    wide = D // 4
    return pl.pallas_call(
        stack_kernel,
        grid=(4,),
        in_specs=[pl.BlockSpec((count, wide), lambda at: (0, at))] * len(blocks),
        out_specs=pl.BlockSpec((count * len(blocks), wide), lambda at: (0, at)),
        out_shape=jax.ShapeDtypeStruct((count * len(blocks), D), blocks[0].dtype),
        compiler_params=params_of(8),
        name="stacked",
    )(*blocks)


def widen(wide, mine, theirs):
    wide[:ROWS, :] = mine[...]
    wide[HALF : HALF + ROWS, :] = theirs[...]


def clear(wide):
    pad = jnp.zeros((HALF - ROWS, wide.shape[1]), wide.dtype)
    wide[ROWS:HALF, :] = pad
    wide[HALF + ROWS :, :] = pad


def hidden_kernel(*refs):
    *parts, mine, theirs, out_ref, total, wide = refs
    at = pl.program_id(0)

    @pl.when(at == 0)
    def _():
        total[...] = jnp.zeros_like(total)
        clear(wide)

    widen(wide, mine, theirs)
    row = 0
    for part in parts:
        count = part.shape[0]
        total[row : row + count, :] += dot_t(part[...], wide[...])
        row += count

    @pl.when(at == pl.num_programs(0) - 1)
    def _():
        out_ref[...] = total[...]


def hidden_of(parts, mine, theirs):
    count = sum(part.shape[0] for part in parts)
    weights = pl.BlockSpec((ROWS, BLOCK), lambda at: (2, at))
    return pl.pallas_call(
        hidden_kernel,
        grid=(D // BLOCK,),
        in_specs=[pl.BlockSpec((part.shape[0], BLOCK), lambda at: (0, at)) for part in parts]
        + [weights, weights],
        out_specs=pl.BlockSpec((count, 2 * HALF), lambda at: (0, 0)),
        out_shape=jax.ShapeDtypeStruct((count, 2 * HALF), jnp.float32),
        scratch_shapes=[
            pltpu.VMEM((count, 2 * HALF), jnp.float32),
            pltpu.VMEM((2 * HALF, BLOCK), jnp.bfloat16),
        ],
        compiler_params=params_of(16),
        cost_estimate=NO_COST,
        name="hidden",
    )(*parts, mine, theirs)


def grad_kernel(*refs):
    *parts, my_params, their_params, my_up, their_up, most_ref, far_ref = refs[:-9]
    own_ref, other_ref, rows, preact, up_proj, hidden, turned, wide_params, wide_up = refs[-9:]
    at = pl.program_id(0)

    @pl.when(at == 0)
    def _():
        preact[...] = jnp.zeros_like(preact)
        up_proj[...] = jnp.zeros_like(up_proj)
        clear(wide_params)
        clear(wide_up)
        column, block = hidden.shape[0] // 4, hidden.shape[0] // 32
        for dz in range(8):
            for dy in range(4):
                place, start = (4 * dz + dy) * block, dz * block
                if dy < 3:
                    start += dy * column
                source = most_ref if dy < 3 else far_ref
                hidden[place : place + block, :] = source[start : start + block, :]

    columns = pl.ds(pl.multiple_of(at * BLOCK, BLOCK), BLOCK)
    row = 0
    for part in parts:
        count = part.shape[0]
        rows[row : row + count, columns] = part[...]
        row += count
    widen(wide_params, my_params, their_params)
    widen(wide_up, my_up, their_up)
    preact[...] += dot_t(rows[:, columns], wide_params[...])
    up_proj[...] += dot_t(rows[:, columns], wide_up[...])

    @pl.when(at == pl.num_programs(0) - 1)
    def _():
        slope = silu_slope(preact[...] * WIDTH_SCALE)
        turned[...] = (hidden[...] * up_proj[...] * slope).T.astype(jnp.bfloat16)

        @pl.loop(0, D // BLOCK)
        def _(block):
            columns = pl.ds(pl.multiple_of(block * BLOCK, BLOCK), BLOCK)
            grad = jnp.dot(turned[...], rows[:, columns], preferred_element_type=jnp.float32)
            own_ref[:, columns] = grad[:ROWS] * WIDTH_SCALE
            other_ref[:, columns] = grad[HALF : HALF + ROWS] * WIDTH_SCALE


def gate_grads(parts, mine, theirs, hidden_most, hidden_far):
    count = sum(part.shape[0] for part in parts)

    def weights(which):
        return pl.BlockSpec((ROWS, BLOCK), lambda at: (which, at))

    whole = pl.BlockSpec((ROWS, D), lambda at: (0, 0))
    return pl.pallas_call(
        grad_kernel,
        grid=(D // BLOCK,),
        in_specs=[pl.BlockSpec((part.shape[0], BLOCK), lambda at: (0, at)) for part in parts]
        + [weights(0), weights(0), weights(1), weights(1)]
        + [pl.BlockSpec(one.shape, lambda at: (0, 0)) for one in (hidden_most, hidden_far)],
        out_specs=[whole, whole],
        out_shape=[jax.ShapeDtypeStruct((ROWS, D), jnp.float32)] * 2,
        scratch_shapes=[
            pltpu.VMEM((count, D), jnp.bfloat16),
            pltpu.VMEM((count, 2 * HALF), jnp.float32),
            pltpu.VMEM((count, 2 * HALF), jnp.float32),
            pltpu.VMEM((count, 2 * HALF), jnp.float32),
            pltpu.VMEM((2 * HALF, count), jnp.bfloat16),
            pltpu.VMEM((2 * HALF, BLOCK), jnp.bfloat16),
            pltpu.VMEM((2 * HALF, BLOCK), jnp.bfloat16),
        ],
        compiler_params=params_of(36),
        cost_estimate=NO_COST,
        name="gate_grads",
    )(*parts, mine, theirs, mine, theirs, hidden_most, hidden_far)


def updated_kernel(factor, kept_weight, which, numerator, *refs):
    two_top, two_rest, one_top, one_rest, hop, stayed, returned = refs[:7]
    kept_ref, new_ref, weight_ref, part, grad, sems, grad_sems = refs[7:]
    received = (
        (two_top, two_rest),
        (one_top, one_rest),
        (hop.at[:CUT, :], hop.at[CUT:, :]),
    )
    at = pl.program_id(0)
    blocks = D // BLOCK

    def copies(sources, source, block):
        columns = pl.ds(block * BLOCK, BLOCK)
        targets = (part.at[:CUT, columns], part.at[CUT:, columns])
        parts = [
            pltpu.make_async_copy(one.at[:, columns], target, sems.at[half, block])
            for half, (one, target) in enumerate(zip(sources, targets))
        ]
        whole = pltpu.make_async_copy(
            source.at[:, columns], grad.at[:, columns], grad_sems.at[block]
        )
        return parts, whole

    @pl.when(at == 0)
    def _():
        for block in range(blocks):
            for place, sources in enumerate(received):

                @pl.when(which[0] == place)
                def _():
                    for copy in copies(sources, stayed, block)[0]:
                        copy.start()

            for place, source in enumerate((stayed, returned)):

                @pl.when(which[1] == place)
                def _():
                    copies(received[0], source, block)[1].start()

    for block in range(blocks):

        @pl.when(at == block)
        def _():
            parts, whole = copies(received[0], stayed, block)
            for copy in (*parts, whole):
                copy.wait()
            columns = slice(block * BLOCK, (block + 1) * BLOCK)
            kept = 0.5 * (numerator[...] - factor[0] * grad[:, columns])
            kept_ref[...] = kept
            new_ref[...] = kept + part[:ROWS, columns]

    @pl.when(at == 0)
    def _():
        weight_ref[0] = kept_weight[0] + jnp.max(part[ROWS:, :128])


def updated(numerator, factor, kept_weight, which, received, grads):
    own = pl.BlockSpec((ROWS, BLOCK), lambda at: (0, at))
    scalar = pl.BlockSpec(memory_space=pltpu.SMEM)
    anywhere = pl.BlockSpec(memory_space=pl.ANY)
    more = [part for parts in received for part in parts] + grads
    blocks = D // BLOCK
    return pl.pallas_call(
        updated_kernel,
        grid=(blocks,),
        in_specs=[scalar, scalar, scalar, own] + [anywhere] * len(more),
        out_specs=[own, own, scalar],
        out_shape=[
            jax.ShapeDtypeStruct((ROWS, D), jnp.float32),
            jax.ShapeDtypeStruct((ROWS, D), jnp.float32),
            jax.ShapeDtypeStruct((1,), jnp.float32),
        ],
        scratch_shapes=[
            pltpu.VMEM((ROWS + 8, D), jnp.float32),
            pltpu.VMEM((ROWS, D), jnp.float32),
            pltpu.SemaphoreType.DMA((2, blocks)),
            pltpu.SemaphoreType.DMA((blocks,)),
        ],
        compiler_params=params_of(16),
        name="updated",
    )(factor, kept_weight, which, numerator, *more)


def shards(
    tokens, cotangent, gate_num, push_weight, stale_num, stale_weight, up_weight, down_weight, step
):
    rate = plan_rate(step)
    numerator = gate_num[0]

    params = (numerator / push_weight[0]).astype(jnp.bfloat16)
    weights = jnp.concatenate([params, up_weight, down_weight], axis=0)
    rows_in, rows_grad = transposed(tokens[0]), transposed(cotangent[0])
    rows_in = held(rows_in, rows_grad, weights)
    near = [rows_in] + [shifted(rows_in, "y", steps) for steps in (1, 3, 2)]
    ring = {0: rows_grad, 1: shifted(rows_grad, "z", 1), 7: shifted(rows_grad, "z", 7)}
    mine = transposed(held(weights, rows_grad))
    ring[2], ring[6] = shifted(ring[1], "z", 1), shifted(ring[7], "z", 7)
    ring[2], ring[6] = held((ring[2], ring[6]), *near[1:])
    ring[3], ring[5] = shifted(ring[2], "z", 1), shifted(ring[6], "z", 7)
    ring[4] = shifted(ring[2], "z", 2)
    stale = jnp.concatenate([stale_num[0], jnp.broadcast_to(stale_weight, (8, D))], axis=0)
    stale_hop = shifted(held(stale, ring[2], ring[6]), "core", 1)
    near[3] = held(near[3], ring[3], ring[4], ring[5], stale_hop)
    blocks = {0: stacked(near)}
    columns = [stacked([ring[steps] for steps in some]) for some in (range(4), range(4, 8))]

    blocks[1], blocks[7] = shifted(blocks[0], "z", 1), shifted(blocks[0], "z", 7)
    following, before = [shifted(columns[0], "y", 1)], [shifted(columns[0], "y", 3)]
    mine = held(mine, columns[0], blocks[0])
    theirs = shifted(mine, "core", 1)
    ready = (columns[1], following[0], before[0], theirs)
    blocks[1], blocks[7] = held((blocks[1], blocks[7]), *ready)

    blocks[2], blocks[6] = shifted(blocks[1], "z", 1), shifted(blocks[7], "z", 7)
    columns[1] = held(columns[1], blocks[1], blocks[7])
    following.append(shifted(columns[1], "y", 1))
    before.append(shifted(columns[1], "y", 3))
    two_before = [shifted(held(stale[:CUT], theirs), "x_lo", 1)]
    ready = (two_before[0], following[1], before[1])
    blocks[2], blocks[6] = held((blocks[2], blocks[6]), *ready)

    blocks[3], blocks[5] = shifted(blocks[2], "z", 1), shifted(blocks[6], "z", 7)
    following[0] = held(following[0], blocks[2])
    far = [shifted(following[0], "y", 1), shifted(before[1], "y", 3)]
    two_before.append(shifted(held(stale[CUT:], two_before[0]), "x_lo", 1))
    hidden_most = hidden_of([*columns, *following, *before], mine, theirs)
    blocks[3], blocks[5] = held((blocks[3], blocks[5]), hidden_most, *far)

    cut = 48
    last = [shifted(blocks[3][:cut], "z", 1), shifted(blocks[5][cut:], "z", 7)]
    two_before[0] = held(two_before[0], blocks[3])
    one_before = [shifted(two_before[0], "core", 1)]
    hidden_far = held(hidden_of(far, mine, theirs), two_before[1], one_before[0])
    parts = [blocks[steps] for steps in (0, 1, 2, 3)] + last + [blocks[steps] for steps in (5, 6, 7)]

    own_grad, other_grad = gate_grads(parts, mine, theirs, hidden_most, hidden_far)
    two_before[1] = held(two_before[1], own_grad)
    one_before.append(shifted(two_before[1], "core", 1))
    gate_grad = own_grad + shifted(other_grad, "core", 1)
    norm_sq = jnp.sum(gate_grad * gate_grad)
    returned = transposed(gate_grad, stay=False)
    norm_sq = summed(jnp.reshape(norm_sq, (1,)))[0]

    clip_factor = jnp.minimum(1.0, MAX_NORM / jnp.sqrt(norm_sq + eps))
    kept_weight = 0.5 * push_weight
    core, x_hi = lax.axis_index("core"), lax.axis_index("x_hi")
    which = jnp.where(step[0] % 2 == 1, 0, 1 + core)
    kept_half, new_num, new_weight = updated(
        numerator,
        jnp.reshape(rate * clip_factor, (1,)),
        kept_weight,
        jnp.stack([which, jnp.where(core == x_hi, 0, 1)]),
        [two_before, one_before, [stale_hop]],
        [gate_grad, returned],
    )
    return (new_num[None], new_weight, kept_half[None], kept_weight)


def solution(mesh):
    named = Mesh(np.asarray(mesh.devices).reshape(tuple(SIZES.values())), tuple(SIZES))
    groups = P(GOSSIP, FSDP, None)
    in_specs = (
        groups,
        groups,
        groups,
        P(GOSSIP),
        groups,
        P(GOSSIP),
        P(FSDP, None),
        P(FSDP, None),
        P(),
    )
    out_specs = (groups, P(GOSSIP), groups, P(GOSSIP))
    return jax.shard_map(shards, mesh=named, in_specs=in_specs, out_specs=out_specs, check_vma=False)
```

```python
import math

import jax
import jax.numpy as jnp
import numpy as np
from jax import lax
from jax.experimental import pallas as pl
from jax.experimental.pallas import tpu as pltpu
from jax.sharding import Mesh, PartitionSpec as P

D = 5120
FFW = 7168

eps = 1e-06

WIDTH_SCALE = D ** (-0.5)
MAX_NORM = 0.05 * math.sqrt(D * FFW)

SIZES = {"x_lo": 2, "core": 2, "z": 8, "x_hi": 2, "y": 4}
GOSSIP = ("x_lo", "core")
FSDP = ("z", "x_hi", "y")

ROWS = 112
HALF = 128
CUT = 88
NO_COST = pl.CostEstimate(flops=1, bytes_accessed=1, transcendentals=0)
BLOCK = 1024


def shifted(value, axis, steps):
    count = SIZES[axis]
    pairs = [((place + steps) % count, place) for place in range(count)]
    return lax.ppermute(value, axis, pairs)


def transposed(value, stay=True):
    pairs = [
        (2 * x_hi + core, 2 * core + x_hi)
        for core in range(2)
        for x_hi in range(2)
        if stay or core != x_hi
    ]
    return lax.ppermute(value, ("core", "x_hi"), pairs)


def crossed(value):
    pairs = [(2 * (1 - x_hi) + core, 2 * core + x_hi) for core in range(2) for x_hi in range(2)]
    return lax.ppermute(value, ("core", "x_hi"), pairs)


def held(value, *ready):
    values = value if isinstance(value, tuple) else (value,)
    anywhere = pl.BlockSpec(memory_space=pl.ANY)
    out = pl.pallas_call(
        lambda *refs: None,
        in_specs=[anywhere] * (len(values) + len(ready)),
        out_specs=[anywhere] * len(values),
        out_shape=[jax.ShapeDtypeStruct(one.shape, one.dtype) for one in values],
        input_output_aliases={at: at for at in range(len(values))},
        compiler_params=params_of(1),
        name="held",
    )(*values, *ready)
    return tuple(out) if isinstance(value, tuple) else out[0]


def silu_slope(preact):
    sigmoid_val = jax.nn.sigmoid(preact)
    return sigmoid_val * (1.0 + preact * (1.0 - sigmoid_val))


def plan_rate(step):
    phase = (step[0] % 1000).astype(jnp.float32) / 1000.0
    return 0.4 + 1.8 * (1.0 + jnp.cos(math.pi * phase))


def dot_t(rows, weights):
    return lax.dot_general(
        rows, weights, (((1,), (1,)), ((), ())), preferred_element_type=jnp.float32
    )


def params_of(vmem, **more):
    return pltpu.CompilerParams(vmem_limit_bytes=vmem * 2**20, **more)


def stack_kernel(*refs):
    *blocks, out_ref = refs
    for at, block in enumerate(blocks):
        count = block.shape[0]
        out_ref[at * count : (at + 1) * count, :] = block[...]


def stacked(blocks):
    count = blocks[0].shape[0]
    wide = D // 4
    return pl.pallas_call(
        stack_kernel,
        grid=(4,),
        in_specs=[pl.BlockSpec((count, wide), lambda at: (0, at))] * len(blocks),
        out_specs=pl.BlockSpec((count * len(blocks), wide), lambda at: (0, at)),
        out_shape=jax.ShapeDtypeStruct((count * len(blocks), D), blocks[0].dtype),
        compiler_params=params_of(8),
        name="stacked",
    )(*blocks)


def widen(wide, mine, theirs):
    wide[:ROWS, :] = mine[...]
    wide[HALF : HALF + ROWS, :] = theirs[...]


def clear(wide):
    pad = jnp.zeros((HALF - ROWS, wide.shape[1]), wide.dtype)
    wide[ROWS:HALF, :] = pad
    wide[HALF + ROWS :, :] = pad


def hidden_kernel(*refs):
    *parts, mine, theirs, out_ref, total, wide = refs
    at = pl.program_id(0)

    @pl.when(at == 0)
    def _():
        total[...] = jnp.zeros_like(total)
        clear(wide)

    widen(wide, mine, theirs)
    row = 0
    for part in parts:
        count = part.shape[0]
        total[row : row + count, :] += dot_t(part[...], wide[...])
        row += count

    @pl.when(at == pl.num_programs(0) - 1)
    def _():
        out_ref[...] = total[...]


def hidden_of(parts, mine, theirs):
    count = sum(part.shape[0] for part in parts)
    weights = pl.BlockSpec((ROWS, BLOCK), lambda at: (2, at))
    return pl.pallas_call(
        hidden_kernel,
        grid=(D // BLOCK,),
        in_specs=[pl.BlockSpec((part.shape[0], BLOCK), lambda at: (0, at)) for part in parts]
        + [weights, weights],
        out_specs=pl.BlockSpec((count, 2 * HALF), lambda at: (0, 0)),
        out_shape=jax.ShapeDtypeStruct((count, 2 * HALF), jnp.float32),
        scratch_shapes=[
            pltpu.VMEM((count, 2 * HALF), jnp.float32),
            pltpu.VMEM((2 * HALF, BLOCK), jnp.bfloat16),
        ],
        compiler_params=params_of(16),
        cost_estimate=NO_COST,
        name="hidden",
    )(*parts, mine, theirs)


def grad_kernel(*refs):
    *parts, my_params, their_params, my_up, their_up, most_ref, far_ref = refs[:-9]
    own_ref, other_ref, rows, preact, up_proj, hidden, turned, wide_params, wide_up = refs[-9:]
    at = pl.program_id(0)

    @pl.when(at == 0)
    def _():
        preact[...] = jnp.zeros_like(preact)
        up_proj[...] = jnp.zeros_like(up_proj)
        clear(wide_params)
        clear(wide_up)
        column, block = hidden.shape[0] // 4, hidden.shape[0] // 32
        for dz in range(8):
            for dy in range(4):
                place, start = (4 * dz + dy) * block, dz * block
                if dy < 3:
                    start += dy * column
                source = most_ref if dy < 3 else far_ref
                hidden[place : place + block, :] = source[start : start + block, :]

    columns = pl.ds(pl.multiple_of(at * BLOCK, BLOCK), BLOCK)
    row = 0
    for part in parts:
        count = part.shape[0]
        rows[row : row + count, columns] = part[...]
        row += count
    widen(wide_params, my_params, their_params)
    widen(wide_up, my_up, their_up)
    preact[...] += dot_t(rows[:, columns], wide_params[...])
    up_proj[...] += dot_t(rows[:, columns], wide_up[...])

    @pl.when(at == pl.num_programs(0) - 1)
    def _():
        slope = silu_slope(preact[...] * WIDTH_SCALE)
        turned[...] = (hidden[...] * up_proj[...] * slope).T.astype(jnp.bfloat16)

        @pl.loop(0, D // BLOCK)
        def _(block):
            columns = pl.ds(pl.multiple_of(block * BLOCK, BLOCK), BLOCK)
            grad = jnp.dot(turned[...], rows[:, columns], preferred_element_type=jnp.float32)
            own_ref[:, columns] = grad[:ROWS] * WIDTH_SCALE
            other_ref[:, columns] = grad[HALF : HALF + ROWS] * WIDTH_SCALE


def gate_grads(parts, mine, theirs, hidden_most, hidden_far):
    count = sum(part.shape[0] for part in parts)

    def weights(which):
        return pl.BlockSpec((ROWS, BLOCK), lambda at: (which, at))

    whole = pl.BlockSpec((ROWS, D), lambda at: (0, 0))
    return pl.pallas_call(
        grad_kernel,
        grid=(D // BLOCK,),
        in_specs=[pl.BlockSpec((part.shape[0], BLOCK), lambda at: (0, at)) for part in parts]
        + [weights(0), weights(0), weights(1), weights(1)]
        + [pl.BlockSpec(one.shape, lambda at: (0, 0)) for one in (hidden_most, hidden_far)],
        out_specs=[whole, whole],
        out_shape=[jax.ShapeDtypeStruct((ROWS, D), jnp.float32)] * 2,
        scratch_shapes=[
            pltpu.VMEM((count, D), jnp.bfloat16),
            pltpu.VMEM((count, 2 * HALF), jnp.float32),
            pltpu.VMEM((count, 2 * HALF), jnp.float32),
            pltpu.VMEM((count, 2 * HALF), jnp.float32),
            pltpu.VMEM((2 * HALF, count), jnp.bfloat16),
            pltpu.VMEM((2 * HALF, BLOCK), jnp.bfloat16),
            pltpu.VMEM((2 * HALF, BLOCK), jnp.bfloat16),
        ],
        compiler_params=params_of(36),
        cost_estimate=NO_COST,
        name="gate_grads",
    )(*parts, mine, theirs, mine, theirs, hidden_most, hidden_far)


def updated_kernel(factor, kept_weight, which, numerator, *refs):
    two_top, two_rest, one_top, one_rest, hop, stayed, returned = refs[:7]
    kept_ref, new_ref, weight_ref, part, grad, sems, grad_sems = refs[7:]
    received = (
        (two_top, two_rest),
        (one_top, one_rest),
        (hop.at[:CUT, :], hop.at[CUT:, :]),
    )
    at = pl.program_id(0)
    blocks = D // BLOCK

    def copies(sources, source, block):
        columns = pl.ds(block * BLOCK, BLOCK)
        targets = (part.at[:CUT, columns], part.at[CUT:, columns])
        parts = [
            pltpu.make_async_copy(one.at[:, columns], target, sems.at[half, block])
            for half, (one, target) in enumerate(zip(sources, targets))
        ]
        whole = pltpu.make_async_copy(
            source.at[:, columns], grad.at[:, columns], grad_sems.at[block]
        )
        return parts, whole

    @pl.when(at == 0)
    def _():
        for block in range(blocks):
            for place, sources in enumerate(received):

                @pl.when(which[0] == place)
                def _():
                    for copy in copies(sources, stayed, block)[0]:
                        copy.start()

            for place, source in enumerate((stayed, returned)):

                @pl.when(which[1] == place)
                def _():
                    copies(received[0], source, block)[1].start()

    for block in range(blocks):

        @pl.when(at == block)
        def _():
            parts, whole = copies(received[0], stayed, block)
            for copy in (*parts, whole):
                copy.wait()
            columns = slice(block * BLOCK, (block + 1) * BLOCK)
            kept = 0.5 * (numerator[...] - factor[0] * grad[:, columns])
            kept_ref[...] = kept
            new_ref[...] = kept + part[:ROWS, columns]

    @pl.when(at == 0)
    def _():
        weight_ref[0] = kept_weight[0] + jnp.max(part[ROWS:, :128])


def updated(numerator, factor, kept_weight, which, received, grads):
    own = pl.BlockSpec((ROWS, BLOCK), lambda at: (0, at))
    scalar = pl.BlockSpec(memory_space=pltpu.SMEM)
    anywhere = pl.BlockSpec(memory_space=pl.ANY)
    more = [part for parts in received for part in parts] + grads
    blocks = D // BLOCK
    return pl.pallas_call(
        updated_kernel,
        grid=(blocks,),
        in_specs=[scalar, scalar, scalar, own] + [anywhere] * len(more),
        out_specs=[own, own, scalar],
        out_shape=[
            jax.ShapeDtypeStruct((ROWS, D), jnp.float32),
            jax.ShapeDtypeStruct((ROWS, D), jnp.float32),
            jax.ShapeDtypeStruct((1,), jnp.float32),
        ],
        scratch_shapes=[
            pltpu.VMEM((ROWS + 8, D), jnp.float32),
            pltpu.VMEM((ROWS, D), jnp.float32),
            pltpu.SemaphoreType.DMA((2, blocks)),
            pltpu.SemaphoreType.DMA((blocks,)),
        ],
        compiler_params=params_of(16),
        name="updated",
    )(factor, kept_weight, which, numerator, *more)


def shards(
    tokens, cotangent, gate_num, push_weight, stale_num, stale_weight, up_weight, down_weight, step
):
    rate = plan_rate(step)
    numerator = gate_num[0]

    params = (numerator / push_weight[0]).astype(jnp.bfloat16)
    weights = jnp.concatenate([params, up_weight, down_weight], axis=0)
    rows_in, rows_grad = transposed(tokens[0]), transposed(cotangent[0])
    rows_in = held(rows_in, rows_grad, weights)
    near = [rows_in] + [shifted(rows_in, "y", steps) for steps in (1, 3, 2)]
    ring = {0: rows_grad, 1: shifted(rows_grad, "z", 1), 7: shifted(rows_grad, "z", 7)}
    mine = transposed(held(weights, rows_grad))
    ring[2], ring[6] = shifted(ring[1], "z", 1), shifted(ring[7], "z", 7)
    ring[2], ring[6] = held((ring[2], ring[6]), *near[1:])
    ring[3], ring[5] = shifted(ring[2], "z", 1), shifted(ring[6], "z", 7)
    ring[4] = shifted(ring[2], "z", 2)
    near[3] = held(near[3], ring[3], ring[4], ring[5])
    blocks = {0: stacked(near)}
    columns = [stacked([ring[steps] for steps in some]) for some in (range(4), range(4, 8))]

    blocks[1], blocks[7] = shifted(blocks[0], "z", 1), shifted(blocks[0], "z", 7)
    following, before = [shifted(columns[0], "y", 1)], [shifted(columns[0], "y", 3)]
    blocks[1], blocks[7] = held((blocks[1], blocks[7]), columns[1], following[0], before[0])

    blocks[2], blocks[6] = shifted(blocks[1], "z", 1), shifted(blocks[7], "z", 7)
    columns[1] = held(columns[1], blocks[1], blocks[7])
    following.append(shifted(columns[1], "y", 1))
    before.append(shifted(columns[1], "y", 3))
    mine = held(mine, blocks[1], blocks[7])
    theirs = shifted(mine, "core", 1)
    blocks[2], blocks[6] = held((blocks[2], blocks[6]), theirs, following[1], before[1])

    blocks[3], blocks[5] = shifted(blocks[2], "z", 1), shifted(blocks[6], "z", 7)
    following[0] = held(following[0], blocks[2])
    far = [shifted(following[0], "y", 1), shifted(before[1], "y", 3)]
    stale = jnp.concatenate([stale_num[0], jnp.broadcast_to(stale_weight, (8, D))], axis=0)
    two_before = [shifted(held(stale[:CUT], theirs), "x_lo", 1)]
    hidden_most = hidden_of([*columns, *following, *before], mine, theirs)
    ready = (two_before[0], hidden_most, *far)
    blocks[3], blocks[5] = held((blocks[3], blocks[5]), *ready)

    cut = 48
    last = [shifted(blocks[3][:cut], "z", 1), shifted(blocks[5][cut:], "z", 7)]
    two_before.append(shifted(held(stale[CUT:], two_before[0]), "x_lo", 1))
    two_before[0] = held(two_before[0], blocks[3])
    one_before = [shifted(two_before[0], "core", 1)]
    hidden_far = held(hidden_of(far, mine, theirs), one_before[0])
    parts = [blocks[steps] for steps in (0, 1, 2, 3)] + last + [blocks[steps] for steps in (5, 6, 7)]

    own_grad, other_grad = gate_grads(parts, mine, theirs, hidden_most, hidden_far)
    stale_hop = shifted(held(stale, own_grad), "core", 1)
    gate_grad = own_grad + shifted(other_grad, "core", 1)
    norm_sq = jnp.sum(gate_grad * gate_grad)
    returned = transposed(gate_grad, stay=False)
    norm_sq = lax.psum(norm_sq, "z")
    two_before[1] = held(two_before[1], jnp.reshape(norm_sq, (1,)))
    one_before.append(shifted(two_before[1], "core", 1))
    norm_sq = lax.psum(norm_sq, "y")
    norm_sq = transposed(norm_sq) + crossed(norm_sq)

    clip_factor = jnp.minimum(1.0, MAX_NORM / jnp.sqrt(norm_sq + eps))
    kept_weight = 0.5 * push_weight
    core, x_hi = lax.axis_index("core"), lax.axis_index("x_hi")
    which = jnp.where(step[0] % 2 == 1, 0, 1 + core)
    kept_half, new_num, new_weight = updated(
        numerator,
        jnp.reshape(rate * clip_factor, (1,)),
        kept_weight,
        jnp.stack([which, jnp.where(core == x_hi, 0, 1)]),
        [two_before, one_before, [stale_hop]],
        [gate_grad, returned],
    )
    return (new_num[None], new_weight, kept_half[None], kept_weight)


def solution(mesh):
    named = Mesh(np.asarray(mesh.devices).reshape(tuple(SIZES.values())), tuple(SIZES))
    groups = P(GOSSIP, FSDP, None)
    in_specs = (
        groups,
        groups,
        groups,
        P(GOSSIP),
        groups,
        P(GOSSIP),
        P(FSDP, None),
        P(FSDP, None),
        P(),
    )
    out_specs = (groups, P(GOSSIP), groups, P(GOSSIP))
    return jax.shard_map(shards, mesh=named, in_specs=in_specs, out_specs=out_specs, check_vma=False)
```

```python
import math

import jax
import jax.numpy as jnp
import numpy as np
from jax import lax
from jax.experimental import pallas as pl
from jax.experimental.pallas import tpu as pltpu
from jax.sharding import Mesh, PartitionSpec as P

D = 5120
FFW = 7168

eps = 1e-06

WIDTH_SCALE = D ** (-0.5)
MAX_NORM = 0.05 * math.sqrt(D * FFW)

SIZES = {"x_lo": 2, "core": 2, "z": 8, "x_hi": 2, "y": 4}
GOSSIP = ("x_lo", "core")
FSDP = ("z", "x_hi", "y")

ROWS = 112
HALF = 128
CUT = 64
NO_COST = pl.CostEstimate(flops=1, bytes_accessed=1, transcendentals=0)
BLOCK = 1024


def shifted(value, axis, steps):
    count = SIZES[axis]
    pairs = [((place + steps) % count, place) for place in range(count)]
    return lax.ppermute(value, axis, pairs)


def transposed(value, axis=None, steps=0, stay=True):
    names = [name for name in SIZES if name in ("core", "x_hi", axis)]
    sizes = [SIZES[name] for name in names]
    pairs = []
    for place in np.ndindex(*sizes):
        here = dict(zip(names, place))
        there = dict(here, core=here["x_hi"], x_hi=here["core"])
        if axis is not None:
            there[axis] = (there[axis] + steps) % SIZES[axis]
        source, target = (
            int(np.ravel_multi_index([one[name] for name in names], sizes)) for one in (there, here)
        )
        if stay or here["core"] != here["x_hi"]:
            pairs.append((source, target))
    return lax.ppermute(value, tuple(names), pairs)


def crossed(value):
    pairs = [(2 * (1 - x_hi) + core, 2 * core + x_hi) for core in range(2) for x_hi in range(2)]
    return lax.ppermute(value, ("core", "x_hi"), pairs)


def held(value, *ready):
    values = value if isinstance(value, tuple) else (value,)
    anywhere = pl.BlockSpec(memory_space=pl.ANY)
    out = pl.pallas_call(
        lambda *refs: None,
        in_specs=[anywhere] * (len(values) + len(ready)),
        out_specs=[anywhere] * len(values),
        out_shape=[jax.ShapeDtypeStruct(one.shape, one.dtype) for one in values],
        input_output_aliases={at: at for at in range(len(values))},
        compiler_params=params_of(1),
        name="held",
    )(*values, *ready)
    return tuple(out) if isinstance(value, tuple) else out[0]


def silu_slope(preact):
    sigmoid_val = jax.nn.sigmoid(preact)
    return sigmoid_val * (1.0 + preact * (1.0 - sigmoid_val))


def plan_rate(step):
    phase = (step[0] % 1000).astype(jnp.float32) / 1000.0
    return 0.4 + 1.8 * (1.0 + jnp.cos(math.pi * phase))


def dot_t(rows, weights):
    return lax.dot_general(
        rows, weights, (((1,), (1,)), ((), ())), preferred_element_type=jnp.float32
    )


def params_of(vmem, **more):
    return pltpu.CompilerParams(vmem_limit_bytes=vmem * 2**20, **more)


def stack_kernel(*refs):
    *blocks, out_ref = refs
    for at, block in enumerate(blocks):
        count = block.shape[0]
        out_ref[at * count : (at + 1) * count, :] = block[...]


def stacked(blocks):
    count = blocks[0].shape[0]
    wide = D // 4
    return pl.pallas_call(
        stack_kernel,
        grid=(4,),
        in_specs=[pl.BlockSpec((count, wide), lambda at: (0, at))] * len(blocks),
        out_specs=pl.BlockSpec((count * len(blocks), wide), lambda at: (0, at)),
        out_shape=jax.ShapeDtypeStruct((count * len(blocks), D), blocks[0].dtype),
        compiler_params=params_of(8),
        name="stacked",
    )(*blocks)


def widen(wide, mine, theirs):
    wide[:ROWS, :] = mine[...]
    wide[HALF : HALF + ROWS, :] = theirs[...]


def clear(wide):
    pad = jnp.zeros((HALF - ROWS, wide.shape[1]), wide.dtype)
    wide[ROWS:HALF, :] = pad
    wide[HALF + ROWS :, :] = pad


def hidden_kernel(*refs):
    *parts, mine, theirs, out_ref, total, wide = refs
    at = pl.program_id(0)

    @pl.when(at == 0)
    def _():
        total[...] = jnp.zeros_like(total)
        clear(wide)

    widen(wide, mine, theirs)
    row = 0
    for part in parts:
        count = part.shape[0]
        total[row : row + count, :] += dot_t(part[...], wide[...])
        row += count

    @pl.when(at == pl.num_programs(0) - 1)
    def _():
        out_ref[...] = total[...]


def hidden_of(parts, mine, theirs):
    count = sum(part.shape[0] for part in parts)
    weights = pl.BlockSpec((ROWS, BLOCK), lambda at: (2, at))
    return pl.pallas_call(
        hidden_kernel,
        grid=(D // BLOCK,),
        in_specs=[pl.BlockSpec((part.shape[0], BLOCK), lambda at: (0, at)) for part in parts]
        + [weights, weights],
        out_specs=pl.BlockSpec((count, 2 * HALF), lambda at: (0, 0)),
        out_shape=jax.ShapeDtypeStruct((count, 2 * HALF), jnp.float32),
        scratch_shapes=[
            pltpu.VMEM((count, 2 * HALF), jnp.float32),
            pltpu.VMEM((2 * HALF, BLOCK), jnp.bfloat16),
        ],
        compiler_params=params_of(16),
        cost_estimate=NO_COST,
        name="hidden",
    )(*parts, mine, theirs)


def grad_kernel(*refs):
    *parts, my_params, their_params, my_up, their_up, most_ref, far_ref = refs[:-9]
    own_ref, other_ref, rows, preact, up_proj, hidden, turned, wide_params, wide_up = refs[-9:]
    at = pl.program_id(0)

    @pl.when(at == 0)
    def _():
        preact[...] = jnp.zeros_like(preact)
        up_proj[...] = jnp.zeros_like(up_proj)
        clear(wide_params)
        clear(wide_up)
        column, block = hidden.shape[0] // 4, hidden.shape[0] // 32
        for dz in range(8):
            for dy in range(4):
                place, start = (4 * dz + dy) * block, dz * block
                if dy < 3:
                    start += dy * column
                source = most_ref if dy < 3 else far_ref
                hidden[place : place + block, :] = source[start : start + block, :]

    columns = pl.ds(pl.multiple_of(at * BLOCK, BLOCK), BLOCK)
    row = 0
    for part in parts:
        count = part.shape[0]
        rows[row : row + count, columns] = part[...]
        row += count
    widen(wide_params, my_params, their_params)
    widen(wide_up, my_up, their_up)
    preact[...] += dot_t(rows[:, columns], wide_params[...])
    up_proj[...] += dot_t(rows[:, columns], wide_up[...])

    @pl.when(at == pl.num_programs(0) - 1)
    def _():
        slope = silu_slope(preact[...] * WIDTH_SCALE)
        turned[...] = (hidden[...] * up_proj[...] * slope).T.astype(jnp.bfloat16)

        @pl.loop(0, D // BLOCK)
        def _(block):
            columns = pl.ds(pl.multiple_of(block * BLOCK, BLOCK), BLOCK)
            grad = jnp.dot(turned[...], rows[:, columns], preferred_element_type=jnp.float32)
            own_ref[:, columns] = grad[:ROWS] * WIDTH_SCALE
            other_ref[:, columns] = grad[HALF : HALF + ROWS] * WIDTH_SCALE


def gate_grads(parts, mine, theirs, hidden_most, hidden_far):
    count = sum(part.shape[0] for part in parts)

    def weights(which):
        return pl.BlockSpec((ROWS, BLOCK), lambda at: (which, at))

    whole = pl.BlockSpec((ROWS, D), lambda at: (0, 0))
    return pl.pallas_call(
        grad_kernel,
        grid=(D // BLOCK,),
        in_specs=[pl.BlockSpec((part.shape[0], BLOCK), lambda at: (0, at)) for part in parts]
        + [weights(0), weights(0), weights(1), weights(1)]
        + [pl.BlockSpec(one.shape, lambda at: (0, 0)) for one in (hidden_most, hidden_far)],
        out_specs=[whole, whole],
        out_shape=[jax.ShapeDtypeStruct((ROWS, D), jnp.float32)] * 2,
        scratch_shapes=[
            pltpu.VMEM((count, D), jnp.bfloat16),
            pltpu.VMEM((count, 2 * HALF), jnp.float32),
            pltpu.VMEM((count, 2 * HALF), jnp.float32),
            pltpu.VMEM((count, 2 * HALF), jnp.float32),
            pltpu.VMEM((2 * HALF, count), jnp.bfloat16),
            pltpu.VMEM((2 * HALF, BLOCK), jnp.bfloat16),
            pltpu.VMEM((2 * HALF, BLOCK), jnp.bfloat16),
        ],
        compiler_params=params_of(36),
        cost_estimate=NO_COST,
        name="gate_grads",
    )(*parts, mine, theirs, mine, theirs, hidden_most, hidden_far)


def updated_kernel(factor, kept_weight, which, numerator, *refs):
    two_top, two_rest, one_top, one_rest, hop, stayed, returned = refs[:7]
    kept_ref, new_ref, weight_ref, part, grad, sems, grad_sems = refs[7:]
    received = (
        (two_top, two_rest),
        (one_top, one_rest),
        (hop.at[:CUT, :], hop.at[CUT:, :]),
    )
    at = pl.program_id(0)
    blocks = D // BLOCK

    def copies(sources, source, block):
        columns = pl.ds(block * BLOCK, BLOCK)
        targets = (part.at[:CUT, columns], part.at[CUT:, columns])
        parts = [
            pltpu.make_async_copy(one.at[:, columns], target, sems.at[half, block])
            for half, (one, target) in enumerate(zip(sources, targets))
        ]
        whole = pltpu.make_async_copy(
            source.at[:, columns], grad.at[:, columns], grad_sems.at[block]
        )
        return parts, whole

    @pl.when(at == 0)
    def _():
        for block in range(blocks):
            for place, sources in enumerate(received):

                @pl.when(which[0] == place)
                def _():
                    for copy in copies(sources, stayed, block)[0]:
                        copy.start()

            for place, source in enumerate((stayed, returned)):

                @pl.when(which[1] == place)
                def _():
                    copies(received[0], source, block)[1].start()

    for block in range(blocks):

        @pl.when(at == block)
        def _():
            parts, whole = copies(received[0], stayed, block)
            for copy in (*parts, whole):
                copy.wait()
            columns = slice(block * BLOCK, (block + 1) * BLOCK)
            kept = 0.5 * (numerator[...] - factor[0] * grad[:, columns])
            kept_ref[...] = kept
            new_ref[...] = kept + part[:ROWS, columns]

    @pl.when(at == 0)
    def _():
        weight_ref[0] = kept_weight[0] + jnp.max(part[ROWS:, :128])


def updated(numerator, factor, kept_weight, which, received, grads):
    own = pl.BlockSpec((ROWS, BLOCK), lambda at: (0, at))
    scalar = pl.BlockSpec(memory_space=pltpu.SMEM)
    anywhere = pl.BlockSpec(memory_space=pl.ANY)
    more = [part for parts in received for part in parts] + grads
    blocks = D // BLOCK
    return pl.pallas_call(
        updated_kernel,
        grid=(blocks,),
        in_specs=[scalar, scalar, scalar, own] + [anywhere] * len(more),
        out_specs=[own, own, scalar],
        out_shape=[
            jax.ShapeDtypeStruct((ROWS, D), jnp.float32),
            jax.ShapeDtypeStruct((ROWS, D), jnp.float32),
            jax.ShapeDtypeStruct((1,), jnp.float32),
        ],
        scratch_shapes=[
            pltpu.VMEM((ROWS + 8, D), jnp.float32),
            pltpu.VMEM((ROWS, D), jnp.float32),
            pltpu.SemaphoreType.DMA((2, blocks)),
            pltpu.SemaphoreType.DMA((blocks,)),
        ],
        compiler_params=params_of(16),
        name="updated",
    )(factor, kept_weight, which, numerator, *more)


def shards(
    tokens, cotangent, gate_num, push_weight, stale_num, stale_weight, up_weight, down_weight, step
):
    rate = plan_rate(step)
    numerator = gate_num[0]

    params = (numerator / push_weight[0]).astype(jnp.bfloat16)
    weights = jnp.concatenate([params, up_weight, down_weight], axis=0)
    ring = {steps: transposed(cotangent[0], "z", steps) for steps in (0, 1, 7)}
    rows_in = held(tokens[0], *ring.values(), weights)
    near = [transposed(rows_in, "y", steps) for steps in (0, 1, 3, 2)]
    mine = transposed(held(weights, *near))
    ring[2], ring[6] = shifted(ring[1], "z", 1), shifted(ring[7], "z", 7)
    ring[2], ring[6] = held((ring[2], ring[6]), *near)
    ring[3], ring[5] = shifted(ring[2], "z", 1), shifted(ring[6], "z", 7)
    ring[4] = shifted(ring[2], "z", 2)
    near[3] = held(near[3], ring[3], ring[4], ring[5])
    blocks = {0: stacked(near)}
    columns = [stacked([ring[steps] for steps in some]) for some in (range(4), range(4, 8))]

    blocks[1], blocks[7] = shifted(blocks[0], "z", 1), shifted(blocks[0], "z", 7)
    following, before = [shifted(columns[0], "y", 1)], [shifted(columns[0], "y", 3)]
    blocks[1], blocks[7] = held((blocks[1], blocks[7]), columns[1], following[0], before[0])

    blocks[2], blocks[6] = shifted(blocks[1], "z", 1), shifted(blocks[7], "z", 7)
    columns[1] = held(columns[1], blocks[1], blocks[7])
    following.append(shifted(columns[1], "y", 1))
    before.append(shifted(columns[1], "y", 3))
    mine = held(mine, blocks[1], blocks[7])
    theirs = shifted(mine, "core", 1)
    blocks[2], blocks[6] = held((blocks[2], blocks[6]), theirs, following[1], before[1])

    blocks[3], blocks[5] = shifted(blocks[2], "z", 1), shifted(blocks[6], "z", 7)
    following[0] = held(following[0], blocks[2])
    far = [shifted(following[0], "y", 1), shifted(before[1], "y", 3)]
    stale = jnp.concatenate([stale_num[0], jnp.broadcast_to(stale_weight, (8, D))], axis=0)
    two_before = [shifted(held(stale[:CUT], theirs), "x_lo", 1)]
    hidden_most = hidden_of([*columns, *following, *before], mine, theirs)
    ready = (two_before[0], hidden_most, *far)
    blocks[3], blocks[5] = held((blocks[3], blocks[5]), *ready)

    cut = 48
    last = [shifted(blocks[3][:cut], "z", 1), shifted(blocks[5][cut:], "z", 7)]
    two_before.append(shifted(held(stale[CUT:], two_before[0]), "x_lo", 1))
    hidden_far = held(hidden_of(far, mine, theirs), two_before[1])
    parts = [blocks[steps] for steps in (0, 1, 2, 3)] + last + [blocks[steps] for steps in (5, 6, 7)]

    own_grad, other_grad = gate_grads(parts, mine, theirs, hidden_most, hidden_far)
    two_before = held(tuple(two_before), own_grad)
    one_before = [shifted(part, "core", 1) for part in two_before]
    stale_hop = shifted(held(stale, own_grad), "core", 1)
    gate_grad = own_grad + shifted(other_grad, "core", 1)
    norm_sq = jnp.sum(gate_grad * gate_grad)
    returned = transposed(gate_grad, stay=False)
    for axes in ("z", "y"):
        norm_sq = lax.psum(norm_sq, axes)
    norm_sq = transposed(norm_sq) + crossed(norm_sq)

    clip_factor = jnp.minimum(1.0, MAX_NORM / jnp.sqrt(norm_sq + eps))
    kept_weight = 0.5 * push_weight
    core, x_hi = lax.axis_index("core"), lax.axis_index("x_hi")
    which = jnp.where(step[0] % 2 == 1, 0, 1 + core)
    kept_half, new_num, new_weight = updated(
        numerator,
        jnp.reshape(rate * clip_factor, (1,)),
        kept_weight,
        jnp.stack([which, jnp.where(core == x_hi, 0, 1)]),
        [two_before, one_before, [stale_hop]],
        [gate_grad, returned],
    )
    return (new_num[None], new_weight, kept_half[None], kept_weight)


def solution(mesh):
    named = Mesh(np.asarray(mesh.devices).reshape(tuple(SIZES.values())), tuple(SIZES))
    groups = P(GOSSIP, FSDP, None)
    in_specs = (
        groups,
        groups,
        groups,
        P(GOSSIP),
        groups,
        P(GOSSIP),
        P(FSDP, None),
        P(FSDP, None),
        P(),
    )
    out_specs = (groups, P(GOSSIP), groups, P(GOSSIP))
    return jax.shard_map(shards, mesh=named, in_specs=in_specs, out_specs=out_specs, check_vma=False)
```

```python
import math

import jax
import jax.numpy as jnp
import numpy as np
from jax import lax
from jax.experimental import pallas as pl
from jax.experimental.pallas import tpu as pltpu
from jax.sharding import Mesh, PartitionSpec as P

D = 5120
FFW = 7168

eps = 1e-06

WIDTH_SCALE = D ** (-0.5)
MAX_NORM = 0.05 * math.sqrt(D * FFW)

SIZES = {"x_lo": 2, "core": 2, "z": 8, "x_hi": 2, "y": 4}
GOSSIP = ("x_lo", "core")
FSDP = ("z", "x_hi", "y")

ROWS = 112
HALF = 128
CUT = 64
NO_COST = pl.CostEstimate(flops=1, bytes_accessed=1, transcendentals=0)
BLOCK = 1024


def shifted(value, axis, steps):
    count = SIZES[axis]
    pairs = [((place + steps) % count, place) for place in range(count)]
    return lax.ppermute(value, axis, pairs)


def transposed(value, stay=True):
    pairs = [
        (2 * x_hi + core, 2 * core + x_hi)
        for core in range(2)
        for x_hi in range(2)
        if stay or core != x_hi
    ]
    return lax.ppermute(value, ("core", "x_hi"), pairs)


def crossed(value):
    pairs = [(2 * (1 - x_hi) + core, 2 * core + x_hi) for core in range(2) for x_hi in range(2)]
    return lax.ppermute(value, ("core", "x_hi"), pairs)


def held(value, *ready):
    values = value if isinstance(value, tuple) else (value,)
    anywhere = pl.BlockSpec(memory_space=pl.ANY)
    out = pl.pallas_call(
        lambda *refs: None,
        in_specs=[anywhere] * (len(values) + len(ready)),
        out_specs=[anywhere] * len(values),
        out_shape=[jax.ShapeDtypeStruct(one.shape, one.dtype) for one in values],
        input_output_aliases={at: at for at in range(len(values))},
        compiler_params=params_of(1),
        name="held",
    )(*values, *ready)
    return tuple(out) if isinstance(value, tuple) else out[0]


def silu_slope(preact):
    sigmoid_val = jax.nn.sigmoid(preact)
    return sigmoid_val * (1.0 + preact * (1.0 - sigmoid_val))


def plan_rate(step):
    phase = (step[0] % 1000).astype(jnp.float32) / 1000.0
    return 0.4 + 1.8 * (1.0 + jnp.cos(math.pi * phase))


def dot_t(rows, weights):
    return lax.dot_general(
        rows, weights, (((1,), (1,)), ((), ())), preferred_element_type=jnp.float32
    )


def params_of(vmem, **more):
    return pltpu.CompilerParams(vmem_limit_bytes=vmem * 2**20, **more)


def stack_kernel(*refs):
    *blocks, out_ref = refs
    for at, block in enumerate(blocks):
        count = block.shape[0]
        out_ref[at * count : (at + 1) * count, :] = block[...]


def stacked(blocks):
    count = blocks[0].shape[0]
    wide = D // 4
    return pl.pallas_call(
        stack_kernel,
        grid=(4,),
        in_specs=[pl.BlockSpec((count, wide), lambda at: (0, at))] * len(blocks),
        out_specs=pl.BlockSpec((count * len(blocks), wide), lambda at: (0, at)),
        out_shape=jax.ShapeDtypeStruct((count * len(blocks), D), blocks[0].dtype),
        compiler_params=params_of(8),
        name="stacked",
    )(*blocks)


def widen(wide, mine, theirs):
    wide[:ROWS, :] = mine[...]
    wide[HALF : HALF + ROWS, :] = theirs[...]


def clear(wide):
    pad = jnp.zeros((HALF - ROWS, wide.shape[1]), wide.dtype)
    wide[ROWS:HALF, :] = pad
    wide[HALF + ROWS :, :] = pad


def hidden_kernel(*refs):
    *parts, mine, theirs, out_ref, total, wide = refs
    at = pl.program_id(0)

    @pl.when(at == 0)
    def _():
        total[...] = jnp.zeros_like(total)
        clear(wide)

    widen(wide, mine, theirs)
    row = 0
    for part in parts:
        count = part.shape[0]
        total[row : row + count, :] += dot_t(part[...], wide[...])
        row += count

    @pl.when(at == pl.num_programs(0) - 1)
    def _():
        out_ref[...] = total[...]


def hidden_of(parts, mine, theirs):
    count = sum(part.shape[0] for part in parts)
    weights = pl.BlockSpec((ROWS, BLOCK), lambda at: (2, at))
    return pl.pallas_call(
        hidden_kernel,
        grid=(D // BLOCK,),
        in_specs=[pl.BlockSpec((part.shape[0], BLOCK), lambda at: (0, at)) for part in parts]
        + [weights, weights],
        out_specs=pl.BlockSpec((count, 2 * HALF), lambda at: (0, 0)),
        out_shape=jax.ShapeDtypeStruct((count, 2 * HALF), jnp.float32),
        scratch_shapes=[
            pltpu.VMEM((count, 2 * HALF), jnp.float32),
            pltpu.VMEM((2 * HALF, BLOCK), jnp.bfloat16),
        ],
        compiler_params=params_of(16),
        cost_estimate=NO_COST,
        name="hidden",
    )(*parts, mine, theirs)


def grad_kernel(*refs):
    *parts, my_params, their_params, my_up, their_up, most_ref, far_ref = refs[:-9]
    own_ref, other_ref, rows, preact, up_proj, hidden, turned, wide_params, wide_up = refs[-9:]
    at = pl.program_id(0)

    @pl.when(at == 0)
    def _():
        preact[...] = jnp.zeros_like(preact)
        up_proj[...] = jnp.zeros_like(up_proj)
        clear(wide_params)
        clear(wide_up)
        column, block = hidden.shape[0] // 4, hidden.shape[0] // 32
        for dz in range(8):
            for dy in range(4):
                place, start = (4 * dz + dy) * block, dz * block
                if dy < 3:
                    start += dy * column
                source = most_ref if dy < 3 else far_ref
                hidden[place : place + block, :] = source[start : start + block, :]

    columns = pl.ds(pl.multiple_of(at * BLOCK, BLOCK), BLOCK)
    row = 0
    for part in parts:
        count = part.shape[0]
        rows[row : row + count, columns] = part[...]
        row += count
    widen(wide_params, my_params, their_params)
    widen(wide_up, my_up, their_up)
    preact[...] += dot_t(rows[:, columns], wide_params[...])
    up_proj[...] += dot_t(rows[:, columns], wide_up[...])

    @pl.when(at == pl.num_programs(0) - 1)
    def _():
        slope = silu_slope(preact[...] * WIDTH_SCALE)
        turned[...] = (hidden[...] * up_proj[...] * slope).T.astype(jnp.bfloat16)

        @pl.loop(0, D // BLOCK)
        def _(block):
            columns = pl.ds(pl.multiple_of(block * BLOCK, BLOCK), BLOCK)
            grad = jnp.dot(turned[...], rows[:, columns], preferred_element_type=jnp.float32)
            own_ref[:, columns] = grad[:ROWS] * WIDTH_SCALE
            other_ref[:, columns] = grad[HALF : HALF + ROWS] * WIDTH_SCALE


def gate_grads(parts, mine, theirs, hidden_most, hidden_far):
    count = sum(part.shape[0] for part in parts)

    def weights(which):
        return pl.BlockSpec((ROWS, BLOCK), lambda at: (which, at))

    whole = pl.BlockSpec((ROWS, D), lambda at: (0, 0))
    return pl.pallas_call(
        grad_kernel,
        grid=(D // BLOCK,),
        in_specs=[pl.BlockSpec((part.shape[0], BLOCK), lambda at: (0, at)) for part in parts]
        + [weights(0), weights(0), weights(1), weights(1)]
        + [pl.BlockSpec(one.shape, lambda at: (0, 0)) for one in (hidden_most, hidden_far)],
        out_specs=[whole, whole],
        out_shape=[jax.ShapeDtypeStruct((ROWS, D), jnp.float32)] * 2,
        scratch_shapes=[
            pltpu.VMEM((count, D), jnp.bfloat16),
            pltpu.VMEM((count, 2 * HALF), jnp.float32),
            pltpu.VMEM((count, 2 * HALF), jnp.float32),
            pltpu.VMEM((count, 2 * HALF), jnp.float32),
            pltpu.VMEM((2 * HALF, count), jnp.bfloat16),
            pltpu.VMEM((2 * HALF, BLOCK), jnp.bfloat16),
            pltpu.VMEM((2 * HALF, BLOCK), jnp.bfloat16),
        ],
        compiler_params=params_of(36),
        cost_estimate=NO_COST,
        name="gate_grads",
    )(*parts, mine, theirs, mine, theirs, hidden_most, hidden_far)


def updated_kernel(factor, kept_weight, which, numerator, *refs):
    two_top, two_rest, one_top, one_rest, hop, stayed, returned = refs[:7]
    kept_ref, new_ref, weight_ref, part, grad, sems, grad_sems = refs[7:]
    received = (
        (two_top, two_rest),
        (one_top, one_rest),
        (hop.at[:CUT, :], hop.at[CUT:, :]),
    )
    at = pl.program_id(0)
    blocks = D // BLOCK

    def copies(sources, source, block):
        columns = pl.ds(block * BLOCK, BLOCK)
        targets = (part.at[:CUT, columns], part.at[CUT:, columns])
        parts = [
            pltpu.make_async_copy(one.at[:, columns], target, sems.at[half, block])
            for half, (one, target) in enumerate(zip(sources, targets))
        ]
        whole = pltpu.make_async_copy(
            source.at[:, columns], grad.at[:, columns], grad_sems.at[block]
        )
        return parts, whole

    @pl.when(at == 0)
    def _():
        for block in range(blocks):
            for place, sources in enumerate(received):

                @pl.when(which[0] == place)
                def _():
                    for copy in copies(sources, stayed, block)[0]:
                        copy.start()

            for place, source in enumerate((stayed, returned)):

                @pl.when(which[1] == place)
                def _():
                    copies(received[0], source, block)[1].start()

    for block in range(blocks):

        @pl.when(at == block)
        def _():
            parts, whole = copies(received[0], stayed, block)
            for copy in (*parts, whole):
                copy.wait()
            columns = slice(block * BLOCK, (block + 1) * BLOCK)
            kept = 0.5 * (numerator[...] - factor[0] * grad[:, columns])
            kept_ref[...] = kept
            new_ref[...] = kept + part[:ROWS, columns]

    @pl.when(at == 0)
    def _():
        weight_ref[0] = kept_weight[0] + jnp.max(part[ROWS:, :128])


def updated(numerator, factor, kept_weight, which, received, grads):
    own = pl.BlockSpec((ROWS, BLOCK), lambda at: (0, at))
    scalar = pl.BlockSpec(memory_space=pltpu.SMEM)
    anywhere = pl.BlockSpec(memory_space=pl.ANY)
    more = [part for parts in received for part in parts] + grads
    blocks = D // BLOCK
    return pl.pallas_call(
        updated_kernel,
        grid=(blocks,),
        in_specs=[scalar, scalar, scalar, own] + [anywhere] * len(more),
        out_specs=[own, own, scalar],
        out_shape=[
            jax.ShapeDtypeStruct((ROWS, D), jnp.float32),
            jax.ShapeDtypeStruct((ROWS, D), jnp.float32),
            jax.ShapeDtypeStruct((1,), jnp.float32),
        ],
        scratch_shapes=[
            pltpu.VMEM((ROWS + 8, D), jnp.float32),
            pltpu.VMEM((ROWS, D), jnp.float32),
            pltpu.SemaphoreType.DMA((2, blocks)),
            pltpu.SemaphoreType.DMA((blocks,)),
        ],
        compiler_params=params_of(16),
        name="updated",
    )(factor, kept_weight, which, numerator, *more)


def shards(
    tokens, cotangent, gate_num, push_weight, stale_num, stale_weight, up_weight, down_weight, step
):
    rate = plan_rate(step)
    numerator = gate_num[0]

    params = (numerator / push_weight[0]).astype(jnp.bfloat16)
    weights = jnp.concatenate([params, up_weight, down_weight], axis=0)
    rows_in, rows_grad = transposed(tokens[0]), transposed(cotangent[0])
    rows_in = held(rows_in, rows_grad, weights)
    near = [rows_in] + [shifted(rows_in, "y", steps) for steps in (1, 3, 2)]
    ring = {0: rows_grad, 1: shifted(rows_grad, "z", 1), 7: shifted(rows_grad, "z", 7)}
    mine = transposed(held(weights, rows_grad))
    ring[2], ring[6] = shifted(ring[1], "z", 1), shifted(ring[7], "z", 7)
    ring[2], ring[6] = held((ring[2], ring[6]), *near[1:])
    ring[3], ring[5] = shifted(ring[2], "z", 1), shifted(ring[6], "z", 7)
    ring[4] = shifted(ring[2], "z", 2)
    near[3] = held(near[3], ring[3], ring[4], ring[5])
    blocks = {0: stacked(near)}
    columns = [stacked([ring[steps] for steps in some]) for some in (range(4), range(4, 8))]

    blocks[1], blocks[7] = shifted(blocks[0], "z", 1), shifted(blocks[0], "z", 7)
    following, before = [shifted(columns[0], "y", 1)], [shifted(columns[0], "y", 3)]
    ready = (columns[1], following[0], before[0], mine)
    blocks[1], blocks[7] = held((blocks[1], blocks[7]), *ready)

    blocks[2], blocks[6] = shifted(blocks[1], "z", 1), shifted(blocks[7], "z", 7)
    columns[1] = held(columns[1], blocks[1], blocks[7])
    following.append(shifted(columns[1], "y", 1))
    before.append(shifted(columns[1], "y", 3))
    stale = jnp.concatenate([stale_num[0], jnp.broadcast_to(stale_weight, (8, D))], axis=0)
    two_before = [shifted(held(stale[:CUT], mine), "x_lo", 1)]
    ready = (two_before[0], following[1], before[1])
    blocks[2], blocks[6] = held((blocks[2], blocks[6]), *ready)

    blocks[3], blocks[5] = shifted(blocks[2], "z", 1), shifted(blocks[6], "z", 7)
    following[0] = held(following[0], blocks[2])
    far = [shifted(following[0], "y", 1), shifted(before[1], "y", 3)]
    mine = held(mine, blocks[2], blocks[6])
    theirs = shifted(mine, "core", 1)
    two_before.append(shifted(held(stale[CUT:], two_before[0]), "x_lo", 1))
    hidden_most = hidden_of([*columns, *following, *before], mine, theirs)
    blocks[3], blocks[5] = held((blocks[3], blocks[5]), hidden_most, *far)

    cut = 48
    last = [shifted(blocks[3][:cut], "z", 1), shifted(blocks[5][cut:], "z", 7)]
    hidden_far = held(hidden_of(far, mine, theirs), two_before[1])
    parts = [blocks[steps] for steps in (0, 1, 2, 3)] + last + [blocks[steps] for steps in (5, 6, 7)]

    own_grad, other_grad = gate_grads(parts, mine, theirs, hidden_most, hidden_far)
    two_before = held(tuple(two_before), own_grad)
    one_before = [shifted(part, "core", 1) for part in two_before]
    stale_hop = shifted(held(stale, own_grad), "core", 1)
    gate_grad = own_grad + shifted(other_grad, "core", 1)
    norm_sq = jnp.sum(gate_grad * gate_grad)
    returned = transposed(gate_grad, stay=False)
    for axes in ("z", "y"):
        norm_sq = lax.psum(norm_sq, axes)
    norm_sq = transposed(norm_sq) + crossed(norm_sq)

    clip_factor = jnp.minimum(1.0, MAX_NORM / jnp.sqrt(norm_sq + eps))
    kept_weight = 0.5 * push_weight
    core, x_hi = lax.axis_index("core"), lax.axis_index("x_hi")
    which = jnp.where(step[0] % 2 == 1, 0, 1 + core)
    kept_half, new_num, new_weight = updated(
        numerator,
        jnp.reshape(rate * clip_factor, (1,)),
        kept_weight,
        jnp.stack([which, jnp.where(core == x_hi, 0, 1)]),
        [two_before, one_before, [stale_hop]],
        [gate_grad, returned],
    )
    return (new_num[None], new_weight, kept_half[None], kept_weight)


def solution(mesh):
    named = Mesh(np.asarray(mesh.devices).reshape(tuple(SIZES.values())), tuple(SIZES))
    groups = P(GOSSIP, FSDP, None)
    in_specs = (
        groups,
        groups,
        groups,
        P(GOSSIP),
        groups,
        P(GOSSIP),
        P(FSDP, None),
        P(FSDP, None),
        P(),
    )
    out_specs = (groups, P(GOSSIP), groups, P(GOSSIP))
    return jax.shard_map(shards, mesh=named, in_specs=in_specs, out_specs=out_specs, check_vma=False)
```

```python
import math

import jax
import jax.numpy as jnp
import numpy as np
from jax import lax
from jax.experimental import pallas as pl
from jax.experimental.pallas import tpu as pltpu
from jax.sharding import Mesh, PartitionSpec as P

D = 5120
FFW = 7168

eps = 1e-06

WIDTH_SCALE = D ** (-0.5)
MAX_NORM = 0.05 * math.sqrt(D * FFW)

SIZES = {"x_lo": 2, "core": 2, "z": 8, "x_hi": 2, "y": 4}
GOSSIP = ("x_lo", "core")
FSDP = ("z", "x_hi", "y")

ROWS = 112
HALF = 128
CUT = 64
NO_COST = pl.CostEstimate(flops=1, bytes_accessed=1, transcendentals=0)
BLOCK = 1280


def shifted(value, axis, steps):
    count = SIZES[axis]
    pairs = [((place + steps) % count, place) for place in range(count)]
    return lax.ppermute(value, axis, pairs)


def transposed(value, stay=True):
    pairs = [
        (2 * x_hi + core, 2 * core + x_hi)
        for core in range(2)
        for x_hi in range(2)
        if stay or core != x_hi
    ]
    return lax.ppermute(value, ("core", "x_hi"), pairs)


def crossed(value):
    pairs = [(2 * (1 - x_hi) + core, 2 * core + x_hi) for core in range(2) for x_hi in range(2)]
    return lax.ppermute(value, ("core", "x_hi"), pairs)


def held(value, *ready):
    values = value if isinstance(value, tuple) else (value,)
    anywhere = pl.BlockSpec(memory_space=pl.ANY)
    out = pl.pallas_call(
        lambda *refs: None,
        in_specs=[anywhere] * (len(values) + len(ready)),
        out_specs=[anywhere] * len(values),
        out_shape=[jax.ShapeDtypeStruct(one.shape, one.dtype) for one in values],
        input_output_aliases={at: at for at in range(len(values))},
        compiler_params=params_of(1),
        name="held",
    )(*values, *ready)
    return tuple(out) if isinstance(value, tuple) else out[0]


def silu_slope(preact):
    sigmoid_val = jax.nn.sigmoid(preact)
    return sigmoid_val * (1.0 + preact * (1.0 - sigmoid_val))


def plan_rate(step):
    phase = (step[0] % 1000).astype(jnp.float32) / 1000.0
    return 0.4 + 1.8 * (1.0 + jnp.cos(math.pi * phase))


def dot_t(rows, weights):
    return lax.dot_general(
        rows, weights, (((1,), (1,)), ((), ())), preferred_element_type=jnp.float32
    )


def params_of(vmem, **more):
    return pltpu.CompilerParams(vmem_limit_bytes=vmem * 2**20, **more)


def stack_kernel(*refs):
    *blocks, out_ref = refs
    for at, block in enumerate(blocks):
        count = block.shape[0]
        out_ref[at * count : (at + 1) * count, :] = block[...]


def stacked(blocks):
    count = blocks[0].shape[0]
    wide = D // 4
    return pl.pallas_call(
        stack_kernel,
        grid=(4,),
        in_specs=[pl.BlockSpec((count, wide), lambda at: (0, at))] * len(blocks),
        out_specs=pl.BlockSpec((count * len(blocks), wide), lambda at: (0, at)),
        out_shape=jax.ShapeDtypeStruct((count * len(blocks), D), blocks[0].dtype),
        compiler_params=params_of(8),
        name="stacked",
    )(*blocks)


def widen(wide, mine, theirs):
    wide[:ROWS, :] = mine[...]
    wide[HALF : HALF + ROWS, :] = theirs[...]


def clear(wide):
    pad = jnp.zeros((HALF - ROWS, wide.shape[1]), wide.dtype)
    wide[ROWS:HALF, :] = pad
    wide[HALF + ROWS :, :] = pad


def hidden_kernel(*refs):
    *parts, mine, theirs, out_ref, total, wide = refs
    at = pl.program_id(0)

    @pl.when(at == 0)
    def _():
        total[...] = jnp.zeros_like(total)
        clear(wide)

    widen(wide, mine, theirs)
    row = 0
    for part in parts:
        count = part.shape[0]
        total[row : row + count, :] += dot_t(part[...], wide[...])
        row += count

    @pl.when(at == pl.num_programs(0) - 1)
    def _():
        out_ref[...] = total[...]


def hidden_of(parts, mine, theirs):
    count = sum(part.shape[0] for part in parts)
    weights = pl.BlockSpec((ROWS, BLOCK), lambda at: (2, at))
    return pl.pallas_call(
        hidden_kernel,
        grid=(D // BLOCK,),
        in_specs=[pl.BlockSpec((part.shape[0], BLOCK), lambda at: (0, at)) for part in parts]
        + [weights, weights],
        out_specs=pl.BlockSpec((count, 2 * HALF), lambda at: (0, 0)),
        out_shape=jax.ShapeDtypeStruct((count, 2 * HALF), jnp.float32),
        scratch_shapes=[
            pltpu.VMEM((count, 2 * HALF), jnp.float32),
            pltpu.VMEM((2 * HALF, BLOCK), jnp.bfloat16),
        ],
        compiler_params=params_of(16),
        cost_estimate=NO_COST,
        name="hidden",
    )(*parts, mine, theirs)


def grad_kernel(*refs):
    *parts, my_params, their_params, my_up, their_up, most_ref, far_ref = refs[:-9]
    own_ref, other_ref, rows, preact, up_proj, hidden, turned, wide_params, wide_up = refs[-9:]
    at = pl.program_id(0)

    @pl.when(at == 0)
    def _():
        preact[...] = jnp.zeros_like(preact)
        up_proj[...] = jnp.zeros_like(up_proj)
        clear(wide_params)
        clear(wide_up)
        column, block = hidden.shape[0] // 4, hidden.shape[0] // 32
        for dz in range(8):
            for dy in range(4):
                place, start = (4 * dz + dy) * block, dz * block
                if dy < 3:
                    start += dy * column
                source = most_ref if dy < 3 else far_ref
                hidden[place : place + block, :] = source[start : start + block, :]

    columns = pl.ds(pl.multiple_of(at * BLOCK, BLOCK), BLOCK)
    row = 0
    for part in parts:
        count = part.shape[0]
        rows[row : row + count, columns] = part[...]
        row += count
    widen(wide_params, my_params, their_params)
    widen(wide_up, my_up, their_up)
    preact[...] += dot_t(rows[:, columns], wide_params[...])
    up_proj[...] += dot_t(rows[:, columns], wide_up[...])

    @pl.when(at == pl.num_programs(0) - 1)
    def _():
        slope = silu_slope(preact[...] * WIDTH_SCALE)
        turned[...] = (hidden[...] * up_proj[...] * slope).T.astype(jnp.bfloat16)

        @pl.loop(0, D // BLOCK)
        def _(block):
            columns = pl.ds(pl.multiple_of(block * BLOCK, BLOCK), BLOCK)
            grad = jnp.dot(turned[...], rows[:, columns], preferred_element_type=jnp.float32)
            own_ref[:, columns] = grad[:ROWS] * WIDTH_SCALE
            other_ref[:, columns] = grad[HALF : HALF + ROWS] * WIDTH_SCALE


def gate_grads(parts, mine, theirs, hidden_most, hidden_far):
    count = sum(part.shape[0] for part in parts)

    def weights(which):
        return pl.BlockSpec((ROWS, BLOCK), lambda at: (which, at))

    whole = pl.BlockSpec((ROWS, D), lambda at: (0, 0))
    return pl.pallas_call(
        grad_kernel,
        grid=(D // BLOCK,),
        in_specs=[pl.BlockSpec((part.shape[0], BLOCK), lambda at: (0, at)) for part in parts]
        + [weights(0), weights(0), weights(1), weights(1)]
        + [pl.BlockSpec(one.shape, lambda at: (0, 0)) for one in (hidden_most, hidden_far)],
        out_specs=[whole, whole],
        out_shape=[jax.ShapeDtypeStruct((ROWS, D), jnp.float32)] * 2,
        scratch_shapes=[
            pltpu.VMEM((count, D), jnp.bfloat16),
            pltpu.VMEM((count, 2 * HALF), jnp.float32),
            pltpu.VMEM((count, 2 * HALF), jnp.float32),
            pltpu.VMEM((count, 2 * HALF), jnp.float32),
            pltpu.VMEM((2 * HALF, count), jnp.bfloat16),
            pltpu.VMEM((2 * HALF, BLOCK), jnp.bfloat16),
            pltpu.VMEM((2 * HALF, BLOCK), jnp.bfloat16),
        ],
        compiler_params=params_of(30),
        cost_estimate=NO_COST,
        name="gate_grads",
    )(*parts, mine, theirs, mine, theirs, hidden_most, hidden_far)


def updated_kernel(factor, kept_weight, which, numerator, *refs):
    two_top, two_rest, one_top, one_rest, hop, stayed, returned = refs[:7]
    kept_ref, new_ref, weight_ref, part, grad, sems, grad_sems = refs[7:]
    received = (
        (two_top, two_rest),
        (one_top, one_rest),
        (hop.at[:CUT, :], hop.at[CUT:, :]),
    )
    at = pl.program_id(0)
    blocks = D // BLOCK

    def copies(sources, source, block):
        columns = pl.ds(block * BLOCK, BLOCK)
        targets = (part.at[:CUT, columns], part.at[CUT:, columns])
        parts = [
            pltpu.make_async_copy(one.at[:, columns], target, sems.at[half, block])
            for half, (one, target) in enumerate(zip(sources, targets))
        ]
        whole = pltpu.make_async_copy(
            source.at[:, columns], grad.at[:, columns], grad_sems.at[block]
        )
        return parts, whole

    @pl.when(at == 0)
    def _():
        for block in range(blocks):
            for place, sources in enumerate(received):

                @pl.when(which[0] == place)
                def _():
                    for copy in copies(sources, stayed, block)[0]:
                        copy.start()

            for place, source in enumerate((stayed, returned)):

                @pl.when(which[1] == place)
                def _():
                    copies(received[0], source, block)[1].start()

    for block in range(blocks):

        @pl.when(at == block)
        def _():
            parts, whole = copies(received[0], stayed, block)
            for copy in (*parts, whole):
                copy.wait()
            columns = slice(block * BLOCK, (block + 1) * BLOCK)
            kept = 0.5 * (numerator[...] - factor[0] * grad[:, columns])
            kept_ref[...] = kept
            new_ref[...] = kept + part[:ROWS, columns]

    @pl.when(at == 0)
    def _():
        weight_ref[0] = kept_weight[0] + jnp.max(part[ROWS:, :128])


def updated(numerator, factor, kept_weight, which, received, grads):
    own = pl.BlockSpec((ROWS, BLOCK), lambda at: (0, at))
    scalar = pl.BlockSpec(memory_space=pltpu.SMEM)
    anywhere = pl.BlockSpec(memory_space=pl.ANY)
    more = [part for parts in received for part in parts] + grads
    blocks = D // BLOCK
    return pl.pallas_call(
        updated_kernel,
        grid=(blocks,),
        in_specs=[scalar, scalar, scalar, own] + [anywhere] * len(more),
        out_specs=[own, own, scalar],
        out_shape=[
            jax.ShapeDtypeStruct((ROWS, D), jnp.float32),
            jax.ShapeDtypeStruct((ROWS, D), jnp.float32),
            jax.ShapeDtypeStruct((1,), jnp.float32),
        ],
        scratch_shapes=[
            pltpu.VMEM((ROWS + 8, D), jnp.float32),
            pltpu.VMEM((ROWS, D), jnp.float32),
            pltpu.SemaphoreType.DMA((2, blocks)),
            pltpu.SemaphoreType.DMA((blocks,)),
        ],
        compiler_params=params_of(16),
        name="updated",
    )(factor, kept_weight, which, numerator, *more)


def shards(
    tokens, cotangent, gate_num, push_weight, stale_num, stale_weight, up_weight, down_weight, step
):
    rate = plan_rate(step)
    numerator = gate_num[0]

    params = (numerator / push_weight[0]).astype(jnp.bfloat16)
    weights = jnp.concatenate([params, up_weight, down_weight], axis=0)
    rows_in, rows_grad = transposed(tokens[0]), transposed(cotangent[0])
    rows_in = held(rows_in, rows_grad, weights)
    near = [rows_in] + [shifted(rows_in, "y", steps) for steps in (1, 3, 2)]
    ring = {0: rows_grad, 1: shifted(rows_grad, "z", 1), 7: shifted(rows_grad, "z", 7)}
    mine = transposed(held(weights, rows_grad))
    ring[2], ring[6] = shifted(ring[1], "z", 1), shifted(ring[7], "z", 7)
    ring[2], ring[6] = held((ring[2], ring[6]), *near[1:])
    ring[3], ring[5] = shifted(ring[2], "z", 1), shifted(ring[6], "z", 7)
    ring[4] = shifted(ring[2], "z", 2)
    near[3] = held(near[3], ring[3], ring[4], ring[5])
    blocks = {0: stacked(near)}
    columns = [stacked([ring[steps] for steps in some]) for some in (range(4), range(4, 8))]

    blocks[1], blocks[7] = shifted(blocks[0], "z", 1), shifted(blocks[0], "z", 7)
    following, before = [shifted(columns[0], "y", 1)], [shifted(columns[0], "y", 3)]
    ready = (columns[1], following[0], before[0], mine)
    blocks[1], blocks[7] = held((blocks[1], blocks[7]), *ready)

    blocks[2], blocks[6] = shifted(blocks[1], "z", 1), shifted(blocks[7], "z", 7)
    columns[1] = held(columns[1], blocks[1], blocks[7])
    following.append(shifted(columns[1], "y", 1))
    before.append(shifted(columns[1], "y", 3))
    stale = jnp.concatenate([stale_num[0], jnp.broadcast_to(stale_weight, (8, D))], axis=0)
    two_before = [shifted(held(stale[:CUT], mine), "x_lo", 1)]
    ready = (two_before[0], following[1], before[1])
    blocks[2], blocks[6] = held((blocks[2], blocks[6]), *ready)

    blocks[3], blocks[5] = shifted(blocks[2], "z", 1), shifted(blocks[6], "z", 7)
    following[0] = held(following[0], blocks[2])
    far = [shifted(following[0], "y", 1), shifted(before[1], "y", 3)]
    mine = held(mine, blocks[2], blocks[6])
    theirs = shifted(mine, "core", 1)
    two_before.append(shifted(held(stale[CUT:], two_before[0]), "x_lo", 1))
    hidden_most = hidden_of([*columns, *following, *before], mine, theirs)
    blocks[3], blocks[5] = held((blocks[3], blocks[5]), hidden_most, *far)

    cut = 48
    last = [shifted(blocks[3][:cut], "z", 1), shifted(blocks[5][cut:], "z", 7)]
    hidden_far = held(hidden_of(far, mine, theirs), two_before[1])
    parts = [blocks[steps] for steps in (0, 1, 2, 3)] + last + [blocks[steps] for steps in (5, 6, 7)]

    own_grad, other_grad = gate_grads(parts, mine, theirs, hidden_most, hidden_far)
    two_before = held(tuple(two_before), own_grad)
    one_before = [shifted(part, "core", 1) for part in two_before]
    stale_hop = shifted(held(stale, own_grad), "core", 1)
    gate_grad = own_grad + shifted(other_grad, "core", 1)
    norm_sq = jnp.sum(gate_grad * gate_grad)
    returned = transposed(gate_grad, stay=False)
    for axes in ("z", "y"):
        norm_sq = lax.psum(norm_sq, axes)
    norm_sq = transposed(norm_sq) + crossed(norm_sq)

    clip_factor = jnp.minimum(1.0, MAX_NORM / jnp.sqrt(norm_sq + eps))
    kept_weight = 0.5 * push_weight
    core, x_hi = lax.axis_index("core"), lax.axis_index("x_hi")
    which = jnp.where(step[0] % 2 == 1, 0, 1 + core)
    kept_half, new_num, new_weight = updated(
        numerator,
        jnp.reshape(rate * clip_factor, (1,)),
        kept_weight,
        jnp.stack([which, jnp.where(core == x_hi, 0, 1)]),
        [two_before, one_before, [stale_hop]],
        [gate_grad, returned],
    )
    return (new_num[None], new_weight, kept_half[None], kept_weight)


def solution(mesh):
    named = Mesh(np.asarray(mesh.devices).reshape(tuple(SIZES.values())), tuple(SIZES))
    groups = P(GOSSIP, FSDP, None)
    in_specs = (
        groups,
        groups,
        groups,
        P(GOSSIP),
        groups,
        P(GOSSIP),
        P(FSDP, None),
        P(FSDP, None),
        P(),
    )
    out_specs = (groups, P(GOSSIP), groups, P(GOSSIP))
    return jax.shard_map(shards, mesh=named, in_specs=in_specs, out_specs=out_specs, check_vma=False)
```
